128 devices in a mesh: ctx: 32 (over y, x, core), head: 4 (over z).
Axes of the slice: x: 4, y: 4, z: 4, core: 2. Of those that a mesh axis runs over, the one named last changes fastest.
Arguments:
- queries: bfloat16 [8192, 8192], P('ctx', 'head'), may hold values from -6 to 6
- keys: bfloat16 [8192, 1024], P('ctx', 'head'), may hold values from -6 to 6
- values: bfloat16 [8192, 1024], P('ctx', 'head'), may hold values from -6 to 6
- d_out: bfloat16 [8192, 8192], P('ctx', 'head'), may hold values from -6 to 6
- w_key: bfloat16 [8192, 1024], P(None, 'head'), may hold values from -0.1875 to 0.1875
- w_value: bfloat16 [8192, 1024], P(None, 'head'), may hold values from -0.1875 to 0.1875
- pair_list: int32 [512, 2], P('ctx'), may hold values from 0 to 63, as said below
- span_slot: int32 [64], replicated, may hold values from 0 to 63, each once
Outputs:
- grad_q: bfloat16 [8192, 8192], P('ctx', 'head')
- grad_k: bfloat16 [8192, 1024], P('ctx', 'head')
- grad_v: bfloat16 [8192, 1024], P('ctx', 'head')
- grad_x: bfloat16 [8192, 8192], P(('ctx', 'head'))
The draws below stay inside these ranges and needn't reach their ends.
Inputs may be any that keep to these rules, and one draw needn't show every extreme that they name: `pair_list`: each row is (query span, key span) with the key span no later than the query span; every span's diagonal pair (c, c) is a row; no pair appears twice; the spans 63 and 62 are paired with every key span up to themselves. The rows are stored in drawn order, not by the spans' slots. `span_slot`: slot s lies on index s // 2 of ctx.
All inputs are finite; a program needn't handle non-finite values.
Results may differ from the reference program's by a relative error of at most 0.0074.
Values may be sent and summed in bfloat16 or wider, within the bound.
A program may use at most 192 MiB of HBM per device.

```python
import jax
import jax.numpy as jnp
import numpy as np
from jax import lax

D = 8192
QH = 64
KVH = 8
HD = 128
CH = 128
SPANS = 64
SEQ = 8192
PAIRS = 512


def draw_queries(key, part):
    key = jax.random.fold_in(key, 11)
    first_key = jax.random.fold_in(key, 0)
    base = jnp.clip(jax.random.normal(first_key, (SEQ, QH * HD), jnp.float32), -6.0, 6.0)
    return base.astype(jnp.bfloat16)


def draw_keys(key, part):
    key = jax.random.fold_in(key, 13)
    first_key = jax.random.fold_in(key, 0)
    base = jnp.clip(jax.random.normal(first_key, (SEQ, KVH * HD), jnp.float32), -6.0, 6.0)
    return base.astype(jnp.bfloat16)


def draw_pair_list(key, part):
    key = jax.random.fold_in(key, 23)
    first_key, second_key = jax.random.split(key)
    lower_rows, lower_cols = np.tril_indices(SPANS - 2, -1)
    picked = jax.random.permutation(first_key, (SPANS - 2) * (SPANS - 3) // 2)[:PAIRS - 3 * SPANS + 3]
    diagonal = jnp.arange(SPANS - 2, dtype=jnp.int32)
    last_keys = jnp.arange(SPANS, dtype=jnp.int32)
    before_keys = jnp.arange(SPANS - 1, dtype=jnp.int32)
    last_rows = jnp.full((SPANS,), SPANS - 1, dtype=jnp.int32)
    before_rows = jnp.full((SPANS - 1,), SPANS - 2, dtype=jnp.int32)
    query_ids = jnp.concatenate([diagonal, last_rows, before_rows, jnp.asarray(lower_rows, dtype=jnp.int32)[picked]])
    key_ids = jnp.concatenate([diagonal, last_keys, before_keys, jnp.asarray(lower_cols, dtype=jnp.int32)[picked]])
    order = jax.random.permutation(second_key, PAIRS)
    return jnp.stack([query_ids, key_ids], axis=1)[order].astype(jnp.int32)


def level_of(stream_key, extent, cuts, low, top_value):
    factor_of, own = 1.0, jax.random.fold_in(stream_key, 6)
    for dim, blocks in cuts:
        steps = jnp.exp(jax.random.uniform(jax.random.fold_in(own, dim), (blocks,), jnp.float32, low / len(cuts), top_value / len(cuts)))
        factor_of = factor_of * jnp.repeat(steps, extent[dim] // blocks).reshape([-1 if axis == dim else 1 for axis in range(len(extent))])
    return factor_of


def centred(key, shape, deviation, limit, cuts=(), kind=jnp.bfloat16):
    array = jax.random.normal(key, shape, jnp.float32) * deviation
    if len(cuts) > 0:
        array = level_of(key, shape, cuts, -0.22, 0.18) * array
    return jnp.clip(array, min=-limit, max=limit).astype(kind)


def setup_inputs(seed: int = 0) -> dict:
    arg_keys = jax.random.split(jax.random.key(seed), 9)
    queries = draw_queries(jax.random.fold_in(arg_keys[8], 71), 0)
    keys = draw_keys(jax.random.fold_in(arg_keys[8], 71), 0)
    values = centred(arg_keys[2], (SEQ, KVH * HD), 1.0, 6.0, ((0, 32), (1, 4)))
    d_out = centred(arg_keys[3], (SEQ, QH * HD), 1.0, 6.0, ((0, 32), (1, 4)))
    w_key = centred(arg_keys[4], (D, KVH * HD), (KVH * HD) ** -0.5, 0.1875, ((1, 4),))
    w_value = centred(arg_keys[5], (D, KVH * HD), (KVH * HD) ** -0.5, 0.1875, ((1, 4),))
    pair_list = draw_pair_list(jax.random.fold_in(arg_keys[8], 71), 0)
    span_slot = jax.random.permutation(arg_keys[7], SPANS).astype(jnp.int32)
    return dict(queries=queries, keys=keys, values=values, d_out=d_out, w_key=w_key, w_value=w_value, pair_list=pair_list, span_slot=span_slot)


neg_fill = -1.0e30


def reference(queries, keys, values, d_out, w_key, w_value, pair_list, span_slot):
    group = QH // KVH
    scale_value = HD ** -0.5
    query_spans = queries.reshape(SPANS, CH, KVH, group, HD)[span_slot].astype(jnp.float32)
    grad_spans = d_out.reshape(SPANS, CH, KVH, group, HD)[span_slot].astype(jnp.float32)
    key_spans = keys.reshape(SPANS, CH, KVH, HD)[span_slot].astype(jnp.float32)
    value_spans = values.reshape(SPANS, CH, KVH, HD)[span_slot].astype(jnp.float32)
    row_ids = jnp.arange(CH, dtype=jnp.int32)[:, None]
    col_ids = jnp.arange(CH, dtype=jnp.int32)[None, :]

    def scores_of(first, second):
        scores = jnp.einsum("qkgd,ckd->kgqc", query_spans[first], key_spans[second]) * scale_value
        keep = jnp.logical_or(row_ids >= col_ids, first != second)
        return scores, jnp.broadcast_to(keep, scores.shape)

    def first_pass(carry, pair):
        run_max, run_sum, run_mix = carry
        first, second = pair[0], pair[1]
        scores, keep = scores_of(first, second)
        scores = jnp.where(keep, scores, neg_fill)
        mixed = jnp.einsum("qkgd,ckd->kgqc", grad_spans[first], value_spans[second])
        old_max = run_max[first]
        new_max = jnp.maximum(old_max, jnp.max(scores, axis=3))
        factor = jnp.exp(old_max - new_max)
        weights = jnp.exp(scores - new_max[..., None])
        new_sum = run_sum[first] * factor + jnp.sum(weights, axis=3)
        new_mix = run_mix[first] * factor + jnp.sum(weights * mixed, axis=3)
        return (run_max.at[first].set(new_max), run_sum.at[first].set(new_sum), run_mix.at[first].set(new_mix)), None

    stat_shape = (SPANS, KVH, group, CH)
    start_state = (jnp.full(stat_shape, neg_fill, jnp.float32), jnp.zeros(stat_shape, jnp.float32), jnp.zeros(stat_shape, jnp.float32))
    (run_max, run_sum, run_mix), _ = lax.scan(first_pass, start_state, pair_list)
    log_total = run_max + jnp.log(run_sum)
    mean_mix = run_mix / run_sum

    def second_pass(carry, pair):
        q_acc, k_acc, v_acc = carry
        first, second = pair[0], pair[1]
        scores, keep = scores_of(first, second)
        weights = jnp.exp(jnp.where(keep, scores - log_total[first][..., None], neg_fill))
        weights_half = weights.astype(jnp.bfloat16).astype(jnp.float32)
        dprob = jnp.einsum("qkgd,ckd->kgqc", grad_spans[first], value_spans[second])
        dscore = (weights * (dprob - mean_mix[first][..., None])).astype(jnp.bfloat16).astype(jnp.float32)
        q_acc = q_acc.at[first].add(jnp.einsum("kgqc,ckd->qkgd", dscore, key_spans[second]))
        k_acc = k_acc.at[second].add(jnp.einsum("kgqc,qkgd->ckd", dscore, query_spans[first]))
        v_acc = v_acc.at[second].add(jnp.einsum("kgqc,qkgd->ckd", weights_half, grad_spans[first]))
        return (q_acc, k_acc, v_acc), None

    zero_state = (jnp.zeros((SPANS, CH, KVH, group, HD), jnp.float32), jnp.zeros((SPANS, CH, KVH, HD), jnp.float32), jnp.zeros((SPANS, CH, KVH, HD), jnp.float32))
    (q_acc, k_acc, v_acc), _ = lax.scan(second_pass, zero_state, pair_list)
    grad_q = jnp.zeros_like(q_acc).at[span_slot].set(q_acc * scale_value).reshape(SEQ, QH * HD).astype(jnp.bfloat16)
    grad_k = jnp.zeros_like(k_acc).at[span_slot].set(k_acc * scale_value).reshape(SEQ, KVH * HD).astype(jnp.bfloat16)
    grad_v = jnp.zeros_like(v_acc).at[span_slot].set(v_acc).reshape(SEQ, KVH * HD).astype(jnp.bfloat16)
    dims = (((1,), (1,)), ((), ()))
    grad_x = lax.dot_general(grad_k, w_key, dims, preferred_element_type=jnp.float32) + lax.dot_general(grad_v, w_value, dims, preferred_element_type=jnp.float32)
    return grad_q, grad_k, grad_v, grad_x.astype(jnp.bfloat16)
```

```python
import functools

import jax
import jax.numpy as jnp
from jax import lax
from jax.experimental import pallas as pl
from jax.experimental.pallas import tpu as pltpu
from jax.sharding import PartitionSpec as P

MESH = pl.DeviceIdType.MESH
HD = 128
CH = 128
SPANS = 64
NX = 4
NY = 4
NZ = 4
NCTX = NX * NY * 2
NPAD = 16
SCALE = HD ** -0.5
EXP_SCALE = SCALE * 1.4426950408889634
neg_fill = -1e30
QB = 512
MIB = 1024 * 1024


def ctx_coords():
    me = lax.axis_index("ctx")
    return me // (2 * NX), lax.rem(me // 2, NX), lax.rem(me, 2)


def ctx_id(y, x, core):
    return (y * NX + x) * 2 + core


def turn(pos, step, size):
    return lax.rem(pos + step + size, size)


class Plane:
    def __init__(self, first):
        self.y, self.x, self.core = ctx_coords()
        self.first = first

    def at(self, da, db, flip=False):
        dy, dx = (da, db) if self.first == "y" else (db, da)
        core = 1 - self.core if flip else self.core
        return ctx_id(turn(self.y, dy, NY), turn(self.x, dx, NX), core)


def barrier_with(targets):
    barrier = pltpu.get_barrier_semaphore()
    for device in targets:
        pl.semaphore_signal(barrier, inc=1, device_id=device, device_id_type=MESH)
    pl.semaphore_wait(barrier, len(targets))


def ctx_targets():
    plane = Plane("x")
    steps = [(1, 0), (2, 0), (3, 0), (0, 1), (0, 2), (0, 3)]
    return [{"ctx": plane.at(da, db)} for da, db in steps] + [{"ctx": plane.at(0, 0, True)}]


class Copies:
    def __init__(self, send, recv):
        self.send, self.recv, self.started = send, recv, []

    def start(self, src, dst, index, device):
        copy = pltpu.make_async_remote_copy(
            src_ref=src, dst_ref=dst, send_sem=self.send.at[index], recv_sem=self.recv.at[index],
            device_id=device, device_id_type=MESH,
        )
        copy.start()
        self.started.append(copy)

    def landed(self, dst, index, device):
        pltpu.make_async_remote_copy(
            src_ref=dst, dst_ref=dst, send_sem=self.send.at[index], recv_sem=self.recv.at[index],
            device_id=device, device_id_type=MESH,
        ).wait_recv()

    def finish(self):
        for copy in self.started:
            copy.wait_send()


DA_OF = (0, -1, 1, 2)


class Gather:
    def __init__(self, first, own, out, send, recv, half):
        self.plane = Plane(first)
        self.own, self.out, self.half = own, out, half
        self.copies = Copies(send, recv)
        self.rows = out.shape[1]

    def dev(self, da, db, flip=False):
        return {"ctx": self.plane.at(da, db, flip)}

    def region(self, da, db, flip=False):
        return self.out.at[self.plane.at(da, db, flip)]

    def part(self, ref, which):
        return ref.at[pl.ds(0, self.half)] if which == 0 else ref.at[pl.ds(self.half, self.rows - self.half)]

    def spread(self, m, src):
        dst = self.region(DA_OF[m], 0)
        self.copies.start(src, dst, 4 + 4 * m, self.dev(0, 1))
        self.copies.start(src, dst, 5 + 4 * m, self.dev(0, -1))
        self.cross(m, 0, src)

    def cross(self, m, db, src):
        dst = self.region(DA_OF[m], db)
        self.copies.start(src, dst, 20 + 4 * m + (db % 4), self.dev(0, 0, True))

    def begin(self):
        dst = self.region(0, 0)
        self.copies.start(self.own, dst, 0, self.dev(1, 0))
        self.copies.start(self.own, dst, 1, self.dev(-1, 0))
        self.spread(0, self.own)

    def got_a(self, step):
        index = 0 if step < 0 else 1
        region = self.region(step, 0)
        self.copies.landed(region, index, self.dev(step, 0))
        piece = self.part(region, index)
        self.copies.start(piece, piece, 2 + index, self.dev(-step, 0))
        self.spread(1 + index, region)

    def got_a_far(self):
        region = self.region(2, 0)
        self.copies.landed(self.part(region, 0), 2, self.dev(-1, 0))
        self.copies.landed(self.part(region, 1), 3, self.dev(1, 0))
        self.spread(3, region)

    def got_b(self, m, step):
        index = 0 if step < 0 else 1
        region = self.region(DA_OF[m], step)
        self.copies.landed(region, 4 + 4 * m + index, self.dev(0, step))
        piece = self.part(region, index)
        self.copies.start(piece, piece, 6 + 4 * m + index, self.dev(0, -step))
        self.cross(m, step, region)

    def got_b_far(self, m):
        region = self.region(DA_OF[m], 2)
        self.copies.landed(self.part(region, 0), 6 + 4 * m, self.dev(0, -1))
        self.copies.landed(self.part(region, 1), 7 + 4 * m, self.dev(0, 1))
        self.cross(m, 2, region)

    def got_cross(self):
        for m in range(4):
            for db in (0, -1, 1, 2):
                self.copies.landed(self.region(DA_OF[m], db, True), 20 + 4 * m + (db % 4), self.dev(0, 0, True))


def gather_kernel(
    keys_ref, values_ref, q_ref, do_ref, sel_ref, kg_ref, vg_ref, unit_ref,
    give, held, from_core, first_in, mid, last_in,
    k_send, k_recv, v_send, v_recv, u_send, u_recv, own_sem,
):
    barrier_with(ctx_targets())
    y, x, core = ctx_coords()
    plane = Plane("x")
    gathers = [
        Gather("x", keys_ref, kg_ref, k_send, k_recv, 144),
        Gather("y", values_ref, vg_ref, v_send, v_recv, 128),
    ]
    for gather in gathers:
        gather.begin()
    me = plane.at(0, 0)
    own_copies = [
        pltpu.make_async_copy(keys_ref, kg_ref.at[me], own_sem.at[0]),
        pltpu.make_async_copy(values_ref, vg_ref.at[me], own_sem.at[1]),
    ]
    for copy in own_copies:
        copy.start()

    def pick(dst, which):
        first = sel_ref[which, 0:1, :]
        second = sel_ref[which, 1:2, :]

        def head(j, carry):
            cols = pl.ds(pl.multiple_of(j * HD, HD), HD)
            for n, ref in enumerate((q_ref, do_ref)):
                dst[n, j // NX, lax.rem(j, NX)] = ref[0:CH, cols] * first + ref[CH:2 * CH, cols] * second
            return carry

        lax.fori_loop(0, NX * NY, head, 0)

    units = Copies(u_send, u_recv)
    pick(give, 1 - core)
    sibling = {"ctx": plane.at(0, 0, True)}
    units.start(give, from_core, 0, sibling)
    pick(held, core)

    for gather in gathers:
        gather.got_a(-1)
        gather.got_a(1)

    units.landed(from_core, 0, sibling)

    def add_core(j, carry):
        for n in range(2):
            held[n, j // NX, lax.rem(j, NX)] += from_core[n, j // NX, lax.rem(j, NX)]
        return carry

    lax.fori_loop(0, NX * NY, add_core, 0)
    for d in (1, 2, 3):
        far_x, far_y = turn(x, d, NX), turn(y, d, NY)
        units.start(held.at[0, :, far_x], first_in.at[0, d - 1], d, {"ctx": plane.at(d, 0)})
        units.start(held.at[1, far_y], first_in.at[1, d - 1], 3 + d, {"ctx": plane.at(0, d)})

    for gather in gathers:
        gather.got_b(0, -1)
        gather.got_b(0, 1)
    for gather in gathers:
        gather.got_a_far()

    for d in (1, 2, 3):
        units.landed(first_in.at[0, d - 1], d, {"ctx": plane.at(-d, 0)})
        units.landed(first_in.at[1, d - 1], 3 + d, {"ctx": plane.at(0, -d)})
    for n in range(4):
        mid[0, n] = held[0, n, x] + first_in[0, 0, n] + first_in[0, 1, n] + first_in[0, 2, n]
        mid[1, n] = held[1, y, n] + first_in[1, 0, n] + first_in[1, 1, n] + first_in[1, 2, n]
    for d in (1, 2, 3):
        units.start(mid.at[0, turn(y, d, NY)], last_in.at[0, d - 1], 6 + d, {"ctx": plane.at(0, d)})
        units.start(mid.at[1, turn(x, d, NX)], last_in.at[1, d - 1], 9 + d, {"ctx": plane.at(d, 0)})

    for m in (1, 2, 3):
        for gather in gathers:
            gather.got_b(m, -1)
            gather.got_b(m, 1)

    for d in (1, 2, 3):
        units.landed(last_in.at[0, d - 1], 6 + d, {"ctx": plane.at(0, -d)})
        units.landed(last_in.at[1, d - 1], 9 + d, {"ctx": plane.at(-d, 0)})
    unit_ref[0] = mid[0, y] + last_in[0, 0] + last_in[0, 1] + last_in[0, 2]
    unit_ref[1] = mid[1, x] + last_in[1, 0] + last_in[1, 1] + last_in[1, 2]

    for m in range(4):
        for gather in gathers:
            gather.got_b_far(m)
    for gather in gathers:
        gather.got_cross()
    for gather in gathers:
        gather.copies.finish()
    units.finish()
    for copy in own_copies:
        copy.wait()


def gather_all(keys_pad, values, queries, d_out, select):
    vmem = pl.BlockSpec(memory_space=pltpu.VMEM)
    anyspace = pl.BlockSpec(memory_space=pl.ANY)
    blk = jnp.bfloat16
    return pl.pallas_call(
        gather_kernel,
        out_shape=(
            jax.ShapeDtypeStruct((NCTX,) + keys_pad.shape, blk),
            jax.ShapeDtypeStruct((NCTX,) + values.shape, blk),
            jax.ShapeDtypeStruct((2, CH, HD), blk),
        ),
        in_specs=[anyspace, anyspace, vmem, vmem, vmem],
        out_specs=(anyspace, anyspace, vmem),
        scratch_shapes=[
            pltpu.VMEM((2, NY, NX, CH, HD), blk),
            pltpu.VMEM((2, NY, NX, CH, HD), blk),
            pltpu.VMEM((2, NY, NX, CH, HD), blk),
            pltpu.VMEM((2, 3, 4, CH, HD), blk),
            pltpu.VMEM((2, 4, CH, HD), blk),
            pltpu.VMEM((2, 3, CH, HD), blk),
            pltpu.SemaphoreType.DMA((36,)),
            pltpu.SemaphoreType.DMA((36,)),
            pltpu.SemaphoreType.DMA((36,)),
            pltpu.SemaphoreType.DMA((36,)),
            pltpu.SemaphoreType.DMA((13,)),
            pltpu.SemaphoreType.DMA((13,)),
            pltpu.SemaphoreType.DMA((2,)),
        ],
        compiler_params=pltpu.CompilerParams(
            collective_id=0, has_side_effects=True, vmem_limit_bytes=32 * MIB
        ),
        name="gather_kv",
    )(keys_pad, values, queries, d_out, select)


def dot_nt(a, b):
    return lax.dot_general(a, b, (((1,), (1,)), ((), ())), preferred_element_type=jnp.float32)


def dot_nn(a, b):
    return lax.dot_general(a, b, (((1,), (0,)), ((), ())), preferred_element_type=jnp.float32)


def dot_tn(a, b):
    return lax.dot_general(a, b, (((0,), (0,)), ((), ())), preferred_element_type=jnp.float32)


def attend_kernel(
    mine, span_slot, slot_label, q_hbm, do_hbm, kg_hbm, vg_hbm, unit_ref,
    gq_ref, hdq_ref, pk_hbm, pv_hbm,
    kg, vg, qs, ds, probs, dprob, tops, stat, acck, accv, dqt, todo, sems, qsems,
):
    me = lax.axis_index("ctx")
    core = lax.rem(me, 2)
    unit = me // 2
    loads = [
        pltpu.make_async_copy(kg_hbm, kg, sems.at[0]),
        pltpu.make_async_copy(vg_hbm, vg, sems.at[1]),
    ]
    for copy in loads:
        copy.start()
    stacks = []
    for i in range(2):
        for h in range(16):
            for n, (src, dst) in enumerate(((q_hbm, qs), (do_hbm, ds))):
                stacks.append(
                    pltpu.make_async_copy(
                        src.at[pl.ds(i * CH, CH), pl.ds(h * HD, HD)],
                        dst.at[i, pl.ds(h * CH, CH)],
                        qsems.at[n, i * 16 + h],
                    )
                )
    for copy in stacks:
        copy.start()
    for copy in loads:
        copy.wait()

    def row_minus_col(width):
        rows = lax.broadcasted_iota(jnp.int32, (CH, width), 0)
        cols = lax.rem(lax.broadcasted_iota(jnp.int32, (CH, width), 1), CH)
        return rows - cols

    hcols = pl.ds(pl.multiple_of((unit // 8) * HD, HD), HD)
    ocols = pl.ds(pl.multiple_of((1 - unit // 8) * HD, HD), HD)
    label = SPANS - 2 + core
    q_unit = unit_ref[0]
    do_unit = unit_ref[1]

    def place(t):
        return pl.ds(pl.multiple_of(lax.rem(t, 4) * HD, HD), HD)

    def unit_first(t, carry):
        top, total, mix = carry
        scores = dot_nt(kg[t, 0:2 * CH, hcols], q_unit) * EXP_SCALE
        diff = row_minus_col(HD)
        low = jnp.where(diff <= (label - slot_label[2 * t]) * CH, scores[0:CH], neg_fill)
        high = jnp.where(diff <= (label - slot_label[2 * t + 1]) * CH, scores[CH:2 * CH], neg_fill)
        scores = jnp.concatenate([low, high], axis=0)
        mixed = dot_nt(vg[t, :, hcols], do_unit)
        new_top = jnp.maximum(top, jnp.max(scores, axis=0, keepdims=True))
        weights = jnp.exp2(scores - new_top)
        factor = jnp.exp2(top - new_top)
        probs[t // 4, :, place(t)] = weights
        dprob[t // 4, :, place(t)] = mixed
        tops[t, :, 0:HD] = new_top
        return (
            new_top,
            total * factor + jnp.sum(weights, axis=0, keepdims=True),
            mix * factor + jnp.sum(weights * mixed, axis=0, keepdims=True),
        )

    zero_row = jnp.zeros((1, HD), jnp.float32)
    top, total, mix = lax.fori_loop(
        0, NCTX, unit_first, (jnp.full((1, HD), neg_fill, jnp.float32), zero_row, zero_row)
    )
    over = 1.0 / total
    delta = mix * over

    def unit_second(t, acc):
        factor = jnp.exp2(tops[t, :, 0:HD] - top) * over
        weights = probs[t // 4, :, place(t)] * factor
        dscore = (weights * (dprob[t // 4, :, place(t)] - delta)).astype(jnp.bfloat16)
        accv[t, :, hcols] = dot_nn(weights.astype(jnp.bfloat16), do_unit)
        acck[t, :, hcols] = dot_nn(dscore, q_unit)
        accv[t, :, ocols] = jnp.zeros((2 * CH, HD), jnp.float32)
        acck[t, :, ocols] = jnp.zeros((2 * CH, HD), jnp.float32)
        return acc + dot_tn(kg[t, 0:2 * CH, hcols], dscore)

    acc = lax.fori_loop(0, NCTX, unit_second, jnp.zeros((HD, CH), jnp.float32))
    hdq_ref[...] = (acc * SCALE).T.astype(jnp.bfloat16)

    for copy in stacks:
        copy.wait()

    def span_work(i, carry):
        own_slot = 2 * me + i
        own_label = slot_label[own_slot]

        @pl.when(own_label < SPANS - 2)
        def _():
            todo[0] = own_slot

            def note(c, n):
                todo[n] = span_slot[c]
                wanted = jnp.logical_and(mine[i * SPANS + c] > 0, c != own_label)
                return n + wanted.astype(jnp.int32)

            count = lax.fori_loop(0, SPANS, note, jnp.int32(1))
            todo[count] = own_slot

            def block_of(ref, slot, cols):
                return ref[slot // 2, pl.ds(pl.multiple_of(lax.rem(slot, 2) * CH, CH), CH), cols]

            def both(ref, t, cols):
                return jnp.concatenate(
                    [block_of(ref, todo[2 * t], cols), block_of(ref, todo[2 * t + 1], cols)], axis=0
                )

            def combo(m, inner):
                cols = pl.ds(pl.multiple_of((m // 2) * HD, HD), HD)
                rows = pl.ds(pl.multiple_of(m * QB, QB), QB)
                stat[0:1, :] = jnp.full((1, QB), neg_fill, jnp.float32)
                stat[1:2, :] = jnp.zeros((1, QB), jnp.float32)
                stat[2:3, :] = jnp.zeros((1, QB), jnp.float32)

                def first(t, limits=None):
                    scores = dot_nt(both(kg, t, cols), qs[i, rows, :]) * EXP_SCALE
                    if limits is not None:
                        diff = row_minus_col(QB)
                        low = jnp.where(diff <= limits[0], scores[0:CH], neg_fill)
                        high = jnp.where(diff <= limits[1], scores[CH:2 * CH], neg_fill)
                        scores = jnp.concatenate([low, high], axis=0)
                    mixed = dot_nt(both(vg, t, cols), ds[i, rows, :])
                    old_top = stat[0:1, :]
                    new_top = jnp.maximum(old_top, jnp.max(scores, axis=0, keepdims=True))
                    weights = jnp.exp2(scores - new_top)
                    factor = jnp.exp2(old_top - new_top)
                    probs[t] = weights
                    dprob[t] = mixed
                    tops[t] = new_top
                    stat[0:1, :] = new_top
                    stat[1:2, :] = stat[1:2, :] * factor + jnp.sum(weights, axis=0, keepdims=True)
                    stat[2:3, :] = stat[2:3, :] * factor + jnp.sum(weights * mixed, axis=0, keepdims=True)

                first(0, (0, jnp.where(count >= 2, CH, -CH)))

                def plain(t, c):
                    first(t)
                    return c

                lax.fori_loop(1, count // 2, plain, 0)

                @pl.when(jnp.logical_and(lax.rem(count, 2) == 1, count > 1))
                def _():
                    first(count // 2, (CH, -CH))

                top_row = stat[0:1, :]
                over_row = 1.0 / stat[1:2, :]
                delta_row = stat[2:3, :] * over_row
                dqt[...] = jnp.zeros_like(dqt)

                def second(t, c):
                    factor = jnp.exp2(tops[t] - top_row) * over_row
                    weights = probs[t] * factor
                    dscore = (weights * (dprob[t] - delta_row)).astype(jnp.bfloat16)
                    value_part = dot_nn(weights.astype(jnp.bfloat16), ds[i, rows, :])
                    key_part = dot_nn(dscore, qs[i, rows, :])
                    for u in range(2):
                        slot = todo[2 * t + u]
                        at = pl.ds(pl.multiple_of(lax.rem(slot, 2) * CH, CH), CH)
                        accv[slot // 2, at, cols] += value_part[u * CH:(u + 1) * CH]
                        acck[slot // 2, at, cols] += key_part[u * CH:(u + 1) * CH]
                    dqt[...] += dot_tn(both(kg, t, cols), dscore)
                    return c

                lax.fori_loop(0, (count + 1) // 2, second, 0)
                for r in range(QB // CH):
                    part = (dqt[:, r * CH:(r + 1) * CH] * SCALE).T
                    gq_ref[
                        pl.ds(pl.multiple_of(i * CH, CH), CH),
                        pl.ds(pl.multiple_of(m * QB + r * HD, HD), HD),
                    ] = part.astype(jnp.bfloat16)
                return inner

            lax.fori_loop(0, 16 * CH // QB, combo, 0)

        return carry

    lax.fori_loop(0, 2, span_work, 0)

    stores = []
    step = 8
    for s in range(NCTX // step):
        def narrow(t, carry):
            kg[t, 0:2 * CH, :] = acck[t].astype(jnp.bfloat16)
            vg[t] = accv[t].astype(jnp.bfloat16)
            return carry

        lax.fori_loop(s * step, (s + 1) * step, narrow, 0)
        part = pl.ds(s * step, step)
        stores.append(pltpu.make_async_copy(kg.at[part, pl.ds(0, 2 * CH)], pk_hbm.at[part], qsems.at[0, s]))
        stores.append(pltpu.make_async_copy(vg.at[part], pv_hbm.at[part], qsems.at[1, s]))
        stores[-1].start()
        stores[-2].start()
    for copy in stores:
        copy.wait()


def attend(mine, span_slot, slot_label, queries, d_out, kg, vg, unit):
    vmem = pl.BlockSpec(memory_space=pltpu.VMEM)
    smem = pl.BlockSpec(memory_space=pltpu.SMEM)
    anyspace = pl.BlockSpec(memory_space=pl.ANY)
    blk = jnp.bfloat16
    return pl.pallas_call(
        attend_kernel,
        out_shape=(
            jax.ShapeDtypeStruct((2 * CH, 16 * HD), blk),
            jax.ShapeDtypeStruct((CH, HD), blk),
            jax.ShapeDtypeStruct((NCTX, 2 * CH, 2 * HD), blk),
            jax.ShapeDtypeStruct((NCTX, 2 * CH, 2 * HD), blk),
        ),
        in_specs=[smem, smem, smem, anyspace, anyspace, anyspace, anyspace, vmem],
        out_specs=(vmem, vmem, anyspace, anyspace),
        scratch_shapes=[
            pltpu.VMEM(kg.shape, blk),
            pltpu.VMEM(vg.shape, blk),
            pltpu.VMEM((2, 16 * CH, HD), blk),
            pltpu.VMEM((2, 16 * CH, HD), blk),
            pltpu.VMEM((31, 2 * CH, QB), jnp.float32),
            pltpu.VMEM((31, 2 * CH, QB), jnp.float32),
            pltpu.VMEM((32, 1, QB), jnp.float32),
            pltpu.VMEM((8, QB), jnp.float32),
            pltpu.VMEM((NCTX, 2 * CH, 2 * HD), jnp.float32),
            pltpu.VMEM((NCTX, 2 * CH, 2 * HD), jnp.float32),
            pltpu.VMEM((HD, QB), jnp.float32),
            pltpu.SMEM((SPANS + 8,), jnp.int32),
            pltpu.SemaphoreType.DMA((2,)),
            pltpu.SemaphoreType.DMA((2, 32)),
        ],
        compiler_params=pltpu.CompilerParams(vmem_limit_bytes=63 * MIB),
        cost_estimate=pl.CostEstimate(flops=8 * 10**9, bytes_accessed=32 * 10**6, transcendentals=4 * 10**6),
        name="attend",
    )(mine, span_slot, slot_label, queries, d_out, kg, vg, unit)


def plus(a, b):
    return (a.astype(jnp.float32) + b.astype(jnp.float32)).astype(jnp.bfloat16)


class Scatter:
    def __init__(self, first, parts, cross_in, near, full, near_b, full_b, send, recv):
        self.plane = Plane(first)
        self.parts, self.cross_in = parts, cross_in
        self.near, self.full, self.near_b, self.full_b = near, full, near_b, full_b
        self.copies = Copies(send, recv)

    def dev(self, da, db, flip=False):
        return {"ctx": self.plane.at(da, db, flip)}

    def cross(self, q):
        for e in range(4):
            self.copies.start(
                self.parts.at[self.plane.at(e, q, True)], self.cross_in.at[q, e], 4 * q + e, self.dev(0, 0, True)
            )

    def add_cross(self, q, e):
        self.copies.landed(self.cross_in.at[q, e], 4 * q + e, self.dev(0, 0, True))
        self.cross_in[q, e] = plus(self.cross_in[q, e], self.parts[self.plane.at(e, q)])

    def far(self, q):
        self.add_cross(q, 2)
        self.copies.start(self.cross_in.at[q, 2, pl.ds(0, CH)], self.near.at[q, 0], 16 + 4 * q, self.dev(1, 0))
        self.copies.start(self.cross_in.at[q, 2, pl.ds(CH, CH)], self.near.at[q, 1], 17 + 4 * q, self.dev(-1, 0))

    def next(self, q):
        self.add_cross(q, 1)
        self.add_cross(q, 3)
        self.copies.landed(self.near.at[q, 0], 16 + 4 * q, self.dev(-1, 0))
        self.cross_in[q, 1, 0:CH] = plus(self.cross_in[q, 1, 0:CH], self.near[q, 0])
        self.copies.start(self.cross_in.at[q, 1], self.full.at[q, 0], 18 + 4 * q, self.dev(1, 0))
        self.copies.landed(self.near.at[q, 1], 17 + 4 * q, self.dev(1, 0))
        self.cross_in[q, 3, CH:2 * CH] = plus(self.cross_in[q, 3, CH:2 * CH], self.near[q, 1])
        self.copies.start(self.cross_in.at[q, 3], self.full.at[q, 1], 19 + 4 * q, self.dev(-1, 0))

    def last(self, q):
        self.add_cross(q, 0)
        self.copies.landed(self.full.at[q, 0], 18 + 4 * q, self.dev(-1, 0))
        self.copies.landed(self.full.at[q, 1], 19 + 4 * q, self.dev(1, 0))
        return (
            self.cross_in[q, 0].astype(jnp.float32)
            + self.full[q, 0].astype(jnp.float32)
            + self.full[q, 1].astype(jnp.float32)
        )

    def last_far(self):
        self.cross_in[2, 0] = self.last(2).astype(jnp.bfloat16)
        self.copies.start(self.cross_in.at[2, 0, pl.ds(0, CH)], self.near_b.at[0], 32, self.dev(0, 1))
        self.copies.start(self.cross_in.at[2, 0, pl.ds(CH, CH)], self.near_b.at[1], 33, self.dev(0, -1))

    def last_near(self, q):
        index = 0 if q == 1 else 1
        step = 1 if q == 1 else -1
        rows = slice(index * CH, (index + 1) * CH)
        total = self.last(q)
        self.copies.landed(self.near_b.at[index], 32 + index, self.dev(0, -step))
        self.cross_in[q, 0] = total.astype(jnp.bfloat16)
        self.cross_in[q, 0, rows] = (total[rows] + self.near_b[index].astype(jnp.float32)).astype(jnp.bfloat16)
        self.copies.start(self.cross_in.at[q, 0], self.full_b.at[index], 34 + index, self.dev(0, step))

    def finish(self):
        total = self.last(0)
        self.copies.landed(self.full_b.at[0], 34, self.dev(0, -1))
        self.copies.landed(self.full_b.at[1], 35, self.dev(0, 1))
        return total + self.full_b[0].astype(jnp.float32) + self.full_b[1].astype(jnp.float32)


def scatter_kernel(
    pk_ref, pv_ref, gk_ref, gv_ref,
    k_cross, k_near, k_full, k_near_b, k_full_b,
    v_cross, v_near, v_full, v_near_b, v_full_b,
    k_send, k_recv, v_send, v_recv,
):
    barrier_with(ctx_targets())
    ways = [
        Scatter("y", pk_ref, k_cross, k_near, k_full, k_near_b, k_full_b, k_send, k_recv),
        Scatter("x", pv_ref, v_cross, v_near, v_full, v_near_b, v_full_b, v_send, v_recv),
    ]
    order = (2, 1, 3, 0)
    for q in order:
        for way in ways:
            way.cross(q)
    for q in order:
        for way in ways:
            way.far(q)
    for q in order:
        for way in ways:
            way.next(q)
    for way in ways:
        way.last_far()
    for way in ways:
        way.last_near(1)
    for way in ways:
        way.last_near(3)
    gk_ref[...] = (ways[0].finish() * SCALE).astype(jnp.bfloat16)
    gv_ref[...] = ways[1].finish().astype(jnp.bfloat16)
    for way in ways:
        way.copies.finish()


def scatter_sums(pk, pv):
    vmem = pl.BlockSpec(memory_space=pltpu.VMEM)
    blk = jnp.bfloat16
    one = [
        pltpu.VMEM((4, 4, 2 * CH, 2 * HD), blk),
        pltpu.VMEM((4, 2, CH, 2 * HD), blk),
        pltpu.VMEM((4, 2, 2 * CH, 2 * HD), blk),
        pltpu.VMEM((2, CH, 2 * HD), blk),
        pltpu.VMEM((2, 2 * CH, 2 * HD), blk),
    ]
    return pl.pallas_call(
        scatter_kernel,
        out_shape=(jax.ShapeDtypeStruct((2 * CH, 2 * HD), blk),) * 2,
        in_specs=[vmem] * 2,
        out_specs=(vmem,) * 2,
        scratch_shapes=one + one + [pltpu.SemaphoreType.DMA((36,))] * 4,
        compiler_params=pltpu.CompilerParams(
            collective_id=1, has_side_effects=True, vmem_limit_bytes=40 * MIB
        ),
        name="scatter_dkv",
    )(pk, pv)


def project_kernel(
    gk_ref, gv_ref, hdq_ref, wk_hbm, wv_hbm, r1, r2, r3, s1, s2, s3, gx_ref, hg_ref,
    grads, weights, total, half, g_send, g_recv, o_send, o_recv, h_send, h_recv, w_sem, own_sem,
):
    me_z = lax.axis_index("head")
    y, x, core = ctx_coords()
    plane = Plane("x")
    barrier_with(
        [{"head": turn(me_z, d, NZ)} for d in (1, 2, 3)] + ctx_targets()
    )
    width = weights.shape[2]
    piece = width // 2
    sends = Copies(g_send, g_recv)
    for d in (1, 2, 3):
        sends.start(gk_ref, grads.at[d, 0], 2 * d - 2, {"head": turn(me_z, d, NZ)})
        sends.start(gv_ref, grads.at[d, 1], 2 * d - 1, {"head": turn(me_z, d, NZ)})

    units = Copies(h_send, h_recv)
    me = plane.at(0, 0)
    rows = [pl.ds(0, CH // 2), pl.ds(CH // 2, CH // 2)]
    own_copy = pltpu.make_async_copy(hdq_ref, hg_ref.at[y, x, core], own_sem.at[4])
    own_copy.start()
    own_copy.wait()
    for d in (1, 2, 3):
        for n, (da, db) in enumerate(((d, 0), (0, d))):
            units.start(
                hg_ref.at[y, x, core, rows[n]], hg_ref.at[y, x, core, rows[n]], 2 * d - 2 + n,
                {"ctx": plane.at(da, db)},
            )

    wrows = pl.ds(pl.multiple_of(me_z * width, width), width)
    fetches = [[
        pltpu.make_async_copy(wk_hbm.at[wrows], weights.at[0, 0], w_sem.at[0]),
        pltpu.make_async_copy(wv_hbm.at[wrows], weights.at[0, 1], w_sem.at[1]),
    ]]
    mine_rows = pl.ds(pl.multiple_of(core * piece, piece), piece)
    other_rows = pl.ds(pl.multiple_of((1 - core) * piece, piece), piece)
    for d, (near, far) in enumerate(((r1, s1), (r2, s2), (r3, s3)), start=1):
        fetches.append([
            pltpu.make_async_copy(near, weights.at[d, :, mine_rows], w_sem.at[2 * d]),
            pltpu.make_async_copy(far, weights.at[d, :, other_rows], w_sem.at[2 * d + 1]),
        ])
    for pair in fetches:
        for copy in pair:
            copy.start()

    def partial(d, cols):
        left = (gk_ref[...], gv_ref[...]) if d == 0 else (grads[d, 0], grads[d, 1])
        return dot_nt(left[0], weights[d, 0, cols, :]) + dot_nt(left[1], weights[d, 1, cols, :])

    step = 512
    for copy in fetches[0]:
        copy.wait()

    def own_part(n, carry):
        cols = pl.ds(pl.multiple_of(n * step, step), step)
        total[:, cols] = partial(0, cols)
        return carry

    lax.fori_loop(0, width // step, own_part, 0)

    for d in (1, 2, 3):
        for n, (da, db) in enumerate(((-d, 0), (0, -d))):
            at = hg_ref.at[turn(y, db, NY), turn(x, da, NX), core, rows[n]]
            units.landed(at, 2 * d - 2 + n, {"ctx": plane.at(da, db)})
    for d in (1, 2, 3):
        units.start(
            hg_ref.at[y, :, core, rows[0]], hg_ref.at[y, :, core, rows[0]], 4 + 2 * d, {"ctx": plane.at(0, d)}
        )
        units.start(
            hg_ref.at[:, x, core, rows[1]], hg_ref.at[:, x, core, rows[1]], 5 + 2 * d, {"ctx": plane.at(d, 0)}
        )

    for d in (1, 3):
        for n in range(2):
            sends.landed(grads.at[d, n], 2 * d - 2 + n, {"head": turn(me_z, -d, NZ)})
        for copy in fetches[d]:
            copy.wait()

        def next_part(n, carry):
            cols = pl.ds(pl.multiple_of(n * step, step), step)
            total[:, cols] += partial(d, cols)
            return carry

        lax.fori_loop(0, width // step, next_part, 0)

    for n in range(2):
        sends.landed(grads.at[2, n], 2 + n, {"head": turn(me_z, -2, NZ)})
    for copy in fetches[2]:
        copy.wait()
    outs = Copies(o_send, o_recv)
    quarter = half.shape[0] // NZ
    own_copies = []
    for n in range(width // step):
        cols = pl.ds(n * step, step)
        half[:, n * step:(n + 1) * step] = (total[:, n * step:(n + 1) * step] + partial(2, cols)).astype(jnp.bfloat16)
        out_cols = pl.ds(pl.multiple_of(me_z * width + n * step, step), step)
        for d in (1, 2, 3):
            to = turn(me_z, d, NZ)
            outs.start(
                half.at[pl.ds(pl.multiple_of(to * quarter, quarter), quarter), cols],
                gx_ref.at[:, out_cols], 4 * (d - 1) + n, {"head": to},
            )
        own = pltpu.make_async_copy(
            half.at[pl.ds(pl.multiple_of(me_z * quarter, quarter), quarter), cols],
            gx_ref.at[:, out_cols], own_sem.at[n],
        )
        own.start()
        own_copies.append(own)

    for d in (1, 2, 3):
        units.landed(
            hg_ref.at[turn(y, -d, NY), :, core, rows[0]], 4 + 2 * d, {"ctx": plane.at(0, -d)}
        )
        units.landed(
            hg_ref.at[:, turn(x, -d, NX), core, rows[1]], 5 + 2 * d, {"ctx": plane.at(-d, 0)}
        )
    sibling = {"ctx": plane.at(0, 0, True)}
    units.start(hg_ref.at[:, :, core], hg_ref.at[:, :, core], 12, sibling)
    units.landed(hg_ref.at[:, :, 1 - core], 12, sibling)

    for n in range(width // step):
        for d in (1, 2, 3):
            origin = turn(me_z, -d, NZ)
            out_cols = pl.ds(pl.multiple_of(origin * width + n * step, step), step)
            outs.landed(gx_ref.at[:, out_cols], 4 * (d - 1) + n, {"head": origin})
    sends.finish()
    outs.finish()
    units.finish()
    for copy in own_copies:
        copy.wait()


def project(gk, gv, hdq, w_key, w_value, near, far):
    vmem = pl.BlockSpec(memory_space=pltpu.VMEM)
    anyspace = pl.BlockSpec(memory_space=pl.ANY)
    blk = jnp.bfloat16
    depth = w_key.shape[0]
    width = depth // NZ
    return pl.pallas_call(
        project_kernel,
        out_shape=(
            jax.ShapeDtypeStruct((2 * CH // NZ, depth), blk),
            jax.ShapeDtypeStruct((NY, NX, 2, CH, HD), blk),
        ),
        in_specs=[vmem, vmem, vmem] + [anyspace] * 8,
        out_specs=(vmem, vmem),
        scratch_shapes=[
            pltpu.VMEM((NZ, 2, 2 * CH, 2 * HD), blk),
            pltpu.VMEM((NZ, 2, width, 2 * HD), blk),
            pltpu.VMEM((2 * CH, width), jnp.float32),
            pltpu.VMEM((2 * CH, width), blk),
            pltpu.SemaphoreType.DMA((6,)),
            pltpu.SemaphoreType.DMA((6,)),
            pltpu.SemaphoreType.DMA((12,)),
            pltpu.SemaphoreType.DMA((12,)),
            pltpu.SemaphoreType.DMA((13,)),
            pltpu.SemaphoreType.DMA((13,)),
            pltpu.SemaphoreType.DMA((8,)),
            pltpu.SemaphoreType.DMA((5,)),
        ],
        compiler_params=pltpu.CompilerParams(
            collective_id=2, has_side_effects=True, vmem_limit_bytes=40 * MIB
        ),
        name="project",
    )(gk, gv, hdq, w_key, w_value, *near, *far)


def per_device(queries, keys, values, d_out, w_key, w_value, pair_list, span_slot):
    me = lax.axis_index("ctx")
    me_z = lax.axis_index("head")
    core = lax.rem(me, 2)
    depth = w_key.shape[0]
    width = depth // NZ
    piece = width // 2

    near, far = [], []
    for d in (1, 2, 3):
        start = lax.rem(me_z + d, NZ) * width + core * piece
        block = jnp.stack([
            lax.dynamic_slice_in_dim(w_key, start, piece, 0),
            lax.dynamic_slice_in_dim(w_value, start, piece, 0),
        ])
        got = lax.ppermute(block, "head", [(i, (i + d) % NZ) for i in range(NZ)])
        near.append(got)
        far.append(lax.ppermute(got, "ctx", [(i, i ^ 1) for i in range(NCTX)]))

    label_ids = jnp.arange(SPANS, dtype=jnp.int32)
    slot_label = jnp.sum(
        jnp.where(span_slot[None, :] == label_ids[:, None], label_ids[None, :], 0), axis=1, dtype=jnp.int32
    )
    own_slots = 2 * me + jnp.arange(2, dtype=jnp.int32)
    own_labels = jnp.sum(
        jnp.where(span_slot[None, :] == own_slots[:, None], label_ids[None, :], 0), axis=1, dtype=jnp.int32
    )
    dense = jnp.arange(SPANS - 2, SPANS, dtype=jnp.int32)
    select = jnp.broadcast_to(
        (own_labels[None, :, None] == dense[:, None, None]).astype(jnp.bfloat16), (2, 2, HD)
    )
    pair_rows = jnp.pad(pair_list.astype(jnp.bfloat16), ((0, 0), (0, keys.shape[1] - 2)))
    keys_pad = jnp.concatenate([keys, pair_rows], axis=0)
    kg, vg, unit = gather_all(keys_pad, values, queries, d_out, select)
    pairs = kg[:, 2 * CH:, :2].reshape(-1, 2).astype(jnp.int32)
    mine = jnp.max(
        jnp.where(
            jnp.logical_and(
                pairs[None, None, :, 0] == own_labels[:, None, None],
                pairs[None, None, :, 1] == label_ids[None, :, None],
            ),
            1, 0,
        ).astype(jnp.int32),
        axis=2,
    ).reshape(-1)
    gq, hdq, pk, pv = attend(mine, span_slot, slot_label, queries, d_out, kg, vg, unit)
    grad_k, grad_v = scatter_sums(pk, pv)
    grad_x, units = project(grad_k, grad_v, hdq, w_key, w_value, near, far)
    heads = units.reshape(NX * NY, 2, CH, HD)
    rows = []
    for i in range(2):
        which = jnp.clip(own_labels[i] - (SPANS - 2), 0, 1)
        picked = lax.dynamic_index_in_dim(heads, which, 1, keepdims=False)
        picked = picked.transpose(1, 0, 2).reshape(CH, NX * NY * HD)
        rows.append(jnp.where(own_labels[i] >= SPANS - 2, picked, gq[i * CH:(i + 1) * CH]))
    grad_q = jnp.concatenate(rows, axis=0)
    return (grad_q, grad_k, grad_v, grad_x)


def solution(mesh):
    return jax.shard_map(
        per_device,
        mesh=mesh,
        in_specs=(
            P("ctx", "head"),
            P("ctx", "head"),
            P("ctx", "head"),
            P("ctx", "head"),
            P(None, "head"),
            P(None, "head"),
            P("ctx", None),
            P(),
        ),
        out_specs=(P("ctx", "head"), P("ctx", "head"), P("ctx", "head"), P(("ctx", "head"), None)),
        check_vma=False,
    )
```

```python
import functools

import jax
import jax.numpy as jnp
from jax import lax
from jax.experimental import pallas as pl
from jax.experimental.pallas import tpu as pltpu
from jax.sharding import PartitionSpec as P

MESH = pl.DeviceIdType.MESH
HD = 128
CH = 128
SPANS = 64
NX = 4
NY = 4
NZ = 4
NCTX = NX * NY * 2
NPAD = 16
SCALE = HD ** -0.5
EXP_SCALE = SCALE * 1.4426950408889634
neg_fill = -1e30
QB = 1024
MIB = 1024 * 1024
VMEM_MIB = 62


def ctx_coords():
    me = lax.axis_index("ctx")
    return me // (2 * NX), lax.rem(me // 2, NX), lax.rem(me, 2)


def ctx_id(y, x, core):
    return (y * NX + x) * 2 + core


def turn(pos, step, size):
    return lax.rem(pos + step + size, size)


class Plane:
    def __init__(self, first):
        self.y, self.x, self.core = ctx_coords()
        self.first = first

    def at(self, da, db, flip=False):
        dy, dx = (da, db) if self.first == "y" else (db, da)
        core = 1 - self.core if flip else self.core
        return ctx_id(turn(self.y, dy, NY), turn(self.x, dx, NX), core)


def barrier_with(targets):
    barrier = pltpu.get_barrier_semaphore()
    for device in targets:
        pl.semaphore_signal(barrier, inc=1, device_id=device, device_id_type=MESH)
    pl.semaphore_wait(barrier, len(targets))


def ctx_targets():
    plane = Plane("x")
    steps = [(1, 0), (2, 0), (3, 0), (0, 1), (0, 2), (0, 3)]
    return [{"ctx": plane.at(da, db)} for da, db in steps] + [{"ctx": plane.at(0, 0, True)}]


def head_targets(steps):
    me_z = lax.axis_index("head")
    return [{"head": turn(me_z, d, NZ)} for d in steps]


class Copies:
    def __init__(self, send, recv):
        self.send, self.recv, self.started = send, recv, []

    def start(self, src, dst, index, device):
        copy = pltpu.make_async_remote_copy(
            src_ref=src, dst_ref=dst, send_sem=self.send.at[index], recv_sem=self.recv.at[index],
            device_id=device, device_id_type=MESH,
        )
        copy.start()
        self.started.append(copy)

    def landed(self, dst, index, device):
        pltpu.make_async_remote_copy(
            src_ref=dst, dst_ref=dst, send_sem=self.send.at[index], recv_sem=self.recv.at[index],
            device_id=device, device_id_type=MESH,
        ).wait_recv()

    def finish(self):
        for copy in self.started:
            copy.wait_send()


DA_OF = (0, -1, 1, 2)


class Gather:
    def __init__(self, first, own, out, send, recv, half):
        self.plane = Plane(first)
        self.own, self.out, self.half = own, out, half
        self.copies = Copies(send, recv)
        self.rows = out.shape[1]

    def dev(self, da, db, flip=False):
        return {"ctx": self.plane.at(da, db, flip)}

    def region(self, da, db, flip=False):
        return self.out.at[self.plane.at(da, db, flip)]

    def part(self, ref, which):
        return ref.at[pl.ds(0, self.half)] if which == 0 else ref.at[pl.ds(self.half, self.rows - self.half)]

    def spread(self, m, src):
        dst = self.region(DA_OF[m], 0)
        self.copies.start(src, dst, 4 + 4 * m, self.dev(0, 1))
        self.copies.start(src, dst, 5 + 4 * m, self.dev(0, -1))
        self.cross(m, 0, src)

    def cross(self, m, db, src):
        dst = self.region(DA_OF[m], db)
        self.copies.start(src, dst, 20 + 4 * m + (db % 4), self.dev(0, 0, True))

    def begin(self):
        dst = self.region(0, 0)
        self.copies.start(self.own, dst, 0, self.dev(1, 0))
        self.copies.start(self.own, dst, 1, self.dev(-1, 0))
        self.spread(0, self.own)

    def got_a(self, step):
        index = 0 if step < 0 else 1
        region = self.region(step, 0)
        self.copies.landed(region, index, self.dev(step, 0))
        piece = self.part(region, index)
        self.copies.start(piece, piece, 2 + index, self.dev(-step, 0))
        self.spread(1 + index, region)

    def got_a_far(self):
        region = self.region(2, 0)
        self.copies.landed(self.part(region, 0), 2, self.dev(-1, 0))
        self.copies.landed(self.part(region, 1), 3, self.dev(1, 0))
        self.spread(3, region)

    def got_b(self, m, step):
        index = 0 if step < 0 else 1
        region = self.region(DA_OF[m], step)
        self.copies.landed(region, 4 + 4 * m + index, self.dev(0, step))
        piece = self.part(region, index)
        self.copies.start(piece, piece, 6 + 4 * m + index, self.dev(0, -step))
        self.cross(m, step, region)

    def got_b_far(self, m):
        region = self.region(DA_OF[m], 2)
        self.copies.landed(self.part(region, 0), 6 + 4 * m, self.dev(0, -1))
        self.copies.landed(self.part(region, 1), 7 + 4 * m, self.dev(0, 1))
        self.cross(m, 2, region)

    def got_cross(self):
        for m in range(4):
            for db in (0, -1, 1, 2):
                self.copies.landed(self.region(DA_OF[m], db, True), 20 + 4 * m + (db % 4), self.dev(0, 0, True))


def gather_kernel(
    keys_ref, values_ref, q_ref, do_ref, sel_ref, wk_hbm, wv_hbm, kg_ref, vg_ref, unit_ref, near_ref, relay_ref,
    give, held, from_core, first_in, mid, last_in,
    k_send, k_recv, v_send, v_recv, u_send, u_recv, w_send, w_recv, own_sem,
):
    barrier_with(ctx_targets() + head_targets((1, 3)))
    y, x, core = ctx_coords()
    plane = Plane("x")
    gathers = [
        Gather("x", keys_ref, kg_ref, k_send, k_recv, 144),
        Gather("y", values_ref, vg_ref, v_send, v_recv, 128),
    ]
    for gather in gathers:
        gather.begin()
    me = plane.at(0, 0)
    own_copies = [
        pltpu.make_async_copy(keys_ref, kg_ref.at[me], own_sem.at[0]),
        pltpu.make_async_copy(values_ref, vg_ref.at[me], own_sem.at[1]),
    ]
    for copy in own_copies:
        copy.start()

    me_z = lax.axis_index("head")
    piece = near_ref.shape[2]
    moves = Copies(w_send, w_recv)
    for n, ref in enumerate((wk_hbm, wv_hbm)):
        for side, step in enumerate((1, -1)):
            to = turn(me_z, step, NZ)
            start = pl.multiple_of((2 * to + core) * piece, piece)
            moves.start(ref.at[pl.ds(start, piece)], near_ref.at[side, n], 2 * side + n, {"head": to})
    for n, ref in enumerate((wk_hbm, wv_hbm)):
        for side, step in enumerate((1, -1)):
            start = (2 * turn(me_z, 2, NZ) + core) * piece + side * (piece // 2)
            start = pl.multiple_of(start, piece // 2)
            moves.start(
                ref.at[pl.ds(start, piece // 2)], relay_ref.at[side, n], 4 + 2 * side + n,
                {"head": turn(me_z, step, NZ)},
            )

    def pick(dst, which):
        first = sel_ref[which, 0:1, :]
        second = sel_ref[which, 1:2, :]

        def head(j, carry):
            cols = pl.ds(pl.multiple_of(j * HD, HD), HD)
            for n, ref in enumerate((q_ref, do_ref)):
                dst[n, j // NX, lax.rem(j, NX)] = ref[0:CH, cols] * first + ref[CH:2 * CH, cols] * second
            return carry

        lax.fori_loop(0, NX * NY, head, 0)

    units = Copies(u_send, u_recv)
    pick(give, 1 - core)
    sibling = {"ctx": plane.at(0, 0, True)}
    units.start(give, from_core, 0, sibling)
    pick(held, core)

    for gather in gathers:
        gather.got_a(-1)
        gather.got_a(1)

    units.landed(from_core, 0, sibling)

    def add_core(j, carry):
        for n in range(2):
            held[n, j // NX, lax.rem(j, NX)] += from_core[n, j // NX, lax.rem(j, NX)]
        return carry

    lax.fori_loop(0, NX * NY, add_core, 0)
    for d in (1, 2, 3):
        far_x, far_y = turn(x, d, NX), turn(y, d, NY)
        units.start(held.at[0, :, far_x], first_in.at[0, d - 1], d, {"ctx": plane.at(d, 0)})
        units.start(held.at[1, far_y], first_in.at[1, d - 1], 3 + d, {"ctx": plane.at(0, d)})

    for gather in gathers:
        gather.got_b(0, -1)
        gather.got_b(0, 1)
    for gather in gathers:
        gather.got_a_far()

    for d in (1, 2, 3):
        units.landed(first_in.at[0, d - 1], d, {"ctx": plane.at(-d, 0)})
        units.landed(first_in.at[1, d - 1], 3 + d, {"ctx": plane.at(0, -d)})
    for n in range(4):
        mid[0, n] = held[0, n, x] + first_in[0, 0, n] + first_in[0, 1, n] + first_in[0, 2, n]
        mid[1, n] = held[1, y, n] + first_in[1, 0, n] + first_in[1, 1, n] + first_in[1, 2, n]
    for d in (1, 2, 3):
        units.start(mid.at[0, turn(y, d, NY)], last_in.at[0, d - 1], 6 + d, {"ctx": plane.at(0, d)})
        units.start(mid.at[1, turn(x, d, NX)], last_in.at[1, d - 1], 9 + d, {"ctx": plane.at(d, 0)})

    for m in (1, 2, 3):
        for gather in gathers:
            gather.got_b(m, -1)
            gather.got_b(m, 1)

    for d in (1, 2, 3):
        units.landed(last_in.at[0, d - 1], 6 + d, {"ctx": plane.at(0, -d)})
        units.landed(last_in.at[1, d - 1], 9 + d, {"ctx": plane.at(-d, 0)})
    unit_ref[0] = mid[0, y] + last_in[0, 0] + last_in[0, 1] + last_in[0, 2]
    unit_ref[1] = mid[1, x] + last_in[1, 0] + last_in[1, 1] + last_in[1, 2]

    for m in range(4):
        for gather in gathers:
            gather.got_b_far(m)
    for gather in gathers:
        gather.got_cross()
    for n in range(2):
        for side, step in enumerate((1, -1)):
            origin = {"head": turn(me_z, -step, NZ)}
            moves.landed(near_ref.at[side, n], 2 * side + n, origin)
            moves.landed(relay_ref.at[side, n], 4 + 2 * side + n, origin)
    for gather in gathers:
        gather.copies.finish()
    units.finish()
    moves.finish()
    for copy in own_copies:
        copy.wait()


def gather_all(keys_pad, values, queries, d_out, select, w_key, w_value):
    vmem = pl.BlockSpec(memory_space=pltpu.VMEM)
    anyspace = pl.BlockSpec(memory_space=pl.ANY)
    hbm = pl.BlockSpec(memory_space=pl.ANY)
    blk = jnp.bfloat16
    piece = w_key.shape[0] // NZ // 2
    return pl.pallas_call(
        gather_kernel,
        out_shape=(
            jax.ShapeDtypeStruct((NCTX,) + keys_pad.shape, blk),
            jax.ShapeDtypeStruct((NCTX,) + values.shape, blk),
            jax.ShapeDtypeStruct((2, CH, HD), blk),
            jax.ShapeDtypeStruct((2, 2, piece) + w_key.shape[1:], blk),
            jax.ShapeDtypeStruct((2, 2, piece // 2) + w_key.shape[1:], blk),
        ),
        in_specs=[anyspace, anyspace, vmem, vmem, vmem, hbm, hbm],
        out_specs=(hbm, hbm, vmem, hbm, hbm),
        scratch_shapes=[
            pltpu.VMEM((2, NY, NX, CH, HD), blk),
            pltpu.VMEM((2, NY, NX, CH, HD), blk),
            pltpu.VMEM((2, NY, NX, CH, HD), blk),
            pltpu.VMEM((2, 3, 4, CH, HD), blk),
            pltpu.VMEM((2, 4, CH, HD), blk),
            pltpu.VMEM((2, 3, CH, HD), blk),
            pltpu.SemaphoreType.DMA((36,)),
            pltpu.SemaphoreType.DMA((36,)),
            pltpu.SemaphoreType.DMA((36,)),
            pltpu.SemaphoreType.DMA((36,)),
            pltpu.SemaphoreType.DMA((13,)),
            pltpu.SemaphoreType.DMA((13,)),
            pltpu.SemaphoreType.DMA((8,)),
            pltpu.SemaphoreType.DMA((8,)),
            pltpu.SemaphoreType.DMA((2,)),
        ],
        compiler_params=pltpu.CompilerParams(
            collective_id=0, has_side_effects=True, vmem_limit_bytes=VMEM_MIB * MIB
        ),
        name="gather_kv",
    )(keys_pad, values, queries, d_out, select, w_key, w_value)


def dot_nt(a, b):
    return lax.dot_general(a, b, (((1,), (1,)), ((), ())), preferred_element_type=jnp.float32)


def dot_nn(a, b):
    return lax.dot_general(a, b, (((1,), (0,)), ((), ())), preferred_element_type=jnp.float32)


def dot_tn(a, b):
    return lax.dot_general(a, b, (((0,), (0,)), ((), ())), preferred_element_type=jnp.float32)


def attend_kernel(
    span_slot, q_hbm, do_hbm, kg_hbm, vg_hbm, unit_ref,
    gq_ref, hdq_ref, pk_hbm, pv_hbm,
    kg, vg, qs, ds, tops, stat, acck, accv, dqt, found, flags, slot_label, todo, flag_sem, qsems, load_sems, store_sems,
):
    me = lax.axis_index("ctx")
    core = lax.rem(me, 2)
    unit = me // 2
    hcols = pl.ds(pl.multiple_of((unit // 8) * HD, HD), HD)
    ocols = pl.ds(pl.multiple_of((1 - unit // 8) * HD, HD), HD)
    quarter = NCTX // 4
    pair_copy = pltpu.make_async_copy(
        kg_hbm.at[:, pl.ds(2 * CH, NPAD)], kg.at[:, pl.ds(2 * CH, NPAD)], load_sems.at[4, 0]
    )
    pair_copy.start()
    loads, late = [], []
    for n in range(4):
        part = pl.ds(n * quarter, quarter)
        for side, (src, dst) in enumerate(((kg_hbm, kg), (vg_hbm, vg))):
            at = (part, pl.ds(0, 2 * CH), hcols)
            loads.append(pltpu.make_async_copy(src.at[at], dst.at[at], load_sems.at[n, side]))
            loads[-1].start()
    for side, (src, dst) in enumerate(((kg_hbm, kg), (vg_hbm, vg))):
        at = (slice(None), pl.ds(0, 2 * CH), ocols)
        late.append(pltpu.make_async_copy(src.at[at], dst.at[at], load_sems.at[5, side]))
    stacks = []
    for i in range(2):
        for h in range(16):
            for n, (src, dst) in enumerate(((q_hbm, qs), (do_hbm, ds))):
                stacks.append(
                    pltpu.make_async_copy(
                        src.at[pl.ds(i * CH, CH), pl.ds(h * HD, HD)],
                        dst.at[i, pl.ds(h * CH, CH)],
                        qsems.at[n, i * 16 + h],
                    )
                )
    for copy in stacks + late:
        copy.start()

    def name_slot(c, carry):
        slot_label[span_slot[c]] = c
        return carry

    lax.fori_loop(0, SPANS, name_slot, 0)

    pair_copy.wait()
    pair_rows = kg[:, 2 * CH:2 * CH + NPAD, 0:HD].reshape(NCTX * NPAD, HD).astype(jnp.float32)
    lanes = lax.broadcasted_iota(jnp.int32, (1, HD), 1).astype(jnp.float32)
    for i in range(2):
        own = slot_label[2 * me + i].astype(jnp.float32)
        hit = jnp.logical_and(pair_rows[:, 0:1] == own, pair_rows[:, 1:2] == lanes)
        found[i:i + 1, :] = jnp.max(jnp.where(hit, 1.0, 0.0), axis=0, keepdims=True).astype(jnp.int32)
    flag_copy = pltpu.make_async_copy(found, flags, flag_sem.at[0])
    flag_copy.start()

    label = SPANS - 2 + core
    q_unit = unit_ref[0]
    do_unit = unit_ref[1]

    def four(ref, t, cols):
        return jnp.concatenate([ref[2 * t, 0:2 * CH, cols], ref[2 * t + 1, 0:2 * CH, cols]], axis=0)

    def unit_first(t, carry):
        top, total, mix = carry
        scores = dot_nt(four(kg, t, hcols), q_unit) * EXP_SCALE
        mixed = dot_nt(four(vg, t, hcols), do_unit)
        diff = lax.broadcasted_iota(jnp.int32, (CH, HD), 0) - lax.broadcasted_iota(jnp.int32, (CH, HD), 1)
        scores = jnp.concatenate([
            jnp.where(diff <= (label - slot_label[4 * t + u]) * CH, scores[u * CH:(u + 1) * CH], neg_fill)
            for u in range(4)
        ], axis=0)
        new_top = jnp.maximum(top, jnp.max(scores, axis=0, keepdims=True))
        weights = jnp.exp2(scores - new_top)
        factor = jnp.exp2(top - new_top)
        for u in range(2):
            acck[2 * t + u, :, ocols] = weights[2 * u * CH:2 * (u + 1) * CH]
            accv[2 * t + u, :, ocols] = mixed[2 * u * CH:2 * (u + 1) * CH]
        tops[t] = new_top
        return (
            new_top,
            total * factor + jnp.sum(weights, axis=0, keepdims=True),
            mix * factor + jnp.sum(weights * mixed, axis=0, keepdims=True),
        )

    zero_row = jnp.zeros((1, HD), jnp.float32)
    state = (jnp.full((1, HD), neg_fill, jnp.float32), zero_row, zero_row)
    for n in range(4):
        for copy in loads[2 * n:2 * n + 2]:
            copy.wait()
        state = lax.fori_loop(n * quarter // 2, (n + 1) * quarter // 2, unit_first, state)
    top, total, mix = state
    over = 1.0 / total
    delta = mix * over

    def unit_second(t, acc):
        factor = jnp.exp2(tops[t] - top) * over
        weights = four(acck, t, ocols) * factor
        mixed = four(accv, t, ocols)
        dscore = (weights * (mixed - delta)).astype(jnp.bfloat16)
        value_part = dot_nn(weights.astype(jnp.bfloat16), do_unit)
        key_part = dot_nn(dscore, q_unit)
        for u in range(2):
            accv[2 * t + u, :, hcols] = value_part[2 * u * CH:2 * (u + 1) * CH]
            acck[2 * t + u, :, hcols] = key_part[2 * u * CH:2 * (u + 1) * CH]
            accv[2 * t + u, :, ocols] = jnp.zeros((2 * CH, HD), jnp.float32)
            acck[2 * t + u, :, ocols] = jnp.zeros((2 * CH, HD), jnp.float32)
        return acc + dot_tn(four(kg, t, hcols), dscore)

    acc = lax.fori_loop(0, NCTX // 2, unit_second, jnp.zeros((HD, CH), jnp.float32))
    hdq_ref[...] = (acc * SCALE).T.astype(jnp.bfloat16)

    flag_copy.wait()
    for copy in stacks + late:
        copy.wait()

    def span_work(i, carry):
        own_slot = 2 * me + i
        own_label = slot_label[own_slot]

        @pl.when(own_label < SPANS - 2)
        def _():
            todo[0] = own_slot

            def note(c, n):
                todo[n] = span_slot[c]
                wanted = jnp.logical_and(flags[i, c] > 0, c != own_label)
                return n + wanted.astype(jnp.int32)

            count = lax.fori_loop(0, SPANS, note, jnp.int32(1))
            todo[count] = own_slot

            def rows_at(slot):
                return pl.ds(pl.multiple_of(lax.rem(slot, 2) * CH, CH), CH)

            def both(ref, t, cols):
                a, b = todo[2 * t], todo[2 * t + 1]
                return jnp.concatenate([ref[a // 2, rows_at(a), cols], ref[b // 2, rows_at(b), cols]], axis=0)

            cols = [pl.ds(g * HD, HD) for g in range(2)]
            rows = [pl.ds(g * QB, QB) for g in range(2)]
            limits = (0, jnp.where(count >= 2, CH, -CH))
            tail = (CH, -CH)
            odd = jnp.logical_and(lax.rem(count, 2) == 1, count > 1)

            def dots(t, limits):
                out = []
                for g in range(2):
                    scores = dot_nt(both(kg, t, cols[g]), qs[i, rows[g], :]) * EXP_SCALE
                    if limits is not None:
                        diff = lax.broadcasted_iota(jnp.int32, (CH, QB), 0) - lax.rem(
                            lax.broadcasted_iota(jnp.int32, (CH, QB), 1), CH
                        )
                        scores = jnp.concatenate([
                            jnp.where(diff <= limits[u], scores[u * CH:(u + 1) * CH], neg_fill) for u in range(2)
                        ], axis=0)
                    out.append((scores, dot_nt(both(vg, t, cols[g]), ds[i, rows[g], :])))
                return out

            def first(t, limits=None):
                for g, (scores, mixed) in enumerate(dots(t, limits)):
                    old_top = stat[g, 0:1, :]
                    new_top = jnp.maximum(old_top, jnp.max(scores, axis=0, keepdims=True))
                    weights = jnp.exp2(scores - new_top)
                    factor = jnp.exp2(old_top - new_top)
                    stat[g, 0:1, :] = new_top
                    stat[g, 1:2, :] = stat[g, 1:2, :] * factor + jnp.sum(weights, axis=0, keepdims=True)
                    stat[g, 2:3, :] = stat[g, 2:3, :] * factor + jnp.sum(weights * mixed, axis=0, keepdims=True)

            def second(t, limits=None):
                for g, (scores, mixed) in enumerate(dots(t, limits)):
                    weights = jnp.exp2(scores - stat[g, 3:4, :])
                    dscore = (weights * (mixed - stat[g, 4:5, :])).astype(jnp.bfloat16)
                    value_part = dot_nn(weights.astype(jnp.bfloat16), ds[i, rows[g], :])
                    key_part = dot_nn(dscore, qs[i, rows[g], :])
                    for u in range(2):
                        slot = todo[2 * t + u]
                        accv[slot // 2, rows_at(slot), cols[g]] += value_part[u * CH:(u + 1) * CH]
                        acck[slot // 2, rows_at(slot), cols[g]] += key_part[u * CH:(u + 1) * CH]
                    dqt[g] += dot_tn(both(kg, t, cols[g]), dscore)

            def sweep(work):
                work(0, limits)

                def plain(t, c):
                    work(t)
                    return c

                lax.fori_loop(1, count // 2, plain, 0)

                @pl.when(odd)
                def _():
                    work(count // 2, tail)

            for g in range(2):
                stat[g, 0:1, :] = jnp.full((1, QB), neg_fill, jnp.float32)
                stat[g, 1:3, :] = jnp.zeros((2, QB), jnp.float32)
            sweep(first)
            for g in range(2):
                total_row = stat[g, 1:2, :]
                stat[g, 3:4, :] = stat[g, 0:1, :] + jnp.log2(total_row)
                stat[g, 4:5, :] = stat[g, 2:3, :] / total_row
                dqt[g] = jnp.zeros((HD, QB), jnp.float32)
            sweep(second)
            for g in range(2):
                for r in range(QB // CH):
                    gq_ref[
                        pl.ds(pl.multiple_of(i * CH, CH), CH), pl.ds(g * QB + r * HD, HD),
                    ] = (dqt[g, :, r * CH:(r + 1) * CH] * SCALE).T.astype(jnp.bfloat16)

        return carry

    lax.fori_loop(0, 2, span_work, 0)

    stores = []
    for n in range(4):
        part = pl.ds(n * quarter, quarter)

        def narrow(t, carry):
            kg[t, 0:2 * CH, :] = acck[t].astype(jnp.bfloat16)
            vg[t] = accv[t].astype(jnp.bfloat16)
            return carry

        lax.fori_loop(n * quarter, (n + 1) * quarter, narrow, 0)
        for side, (src, dst) in enumerate(((kg.at[part, pl.ds(0, 2 * CH)], pk_hbm), (vg.at[part], pv_hbm))):
            stores.append(pltpu.make_async_copy(src, dst.at[part], store_sems.at[n, side]))
            stores[-1].start()
    for copy in stores:
        copy.wait()


def attend(span_slot, queries, d_out, kg, vg, unit):
    vmem = pl.BlockSpec(memory_space=pltpu.VMEM)
    smem = pl.BlockSpec(memory_space=pltpu.SMEM)
    anyspace = pl.BlockSpec(memory_space=pl.ANY)
    blk = jnp.bfloat16
    return pl.pallas_call(
        attend_kernel,
        out_shape=(
            jax.ShapeDtypeStruct((2 * CH, 16 * HD), blk),
            jax.ShapeDtypeStruct((CH, HD), blk),
            jax.ShapeDtypeStruct((NCTX, 2 * CH, 2 * HD), blk),
            jax.ShapeDtypeStruct((NCTX, 2 * CH, 2 * HD), blk),
        ),
        in_specs=[smem, anyspace, anyspace, anyspace, anyspace, vmem],
        out_specs=(vmem, vmem, anyspace, anyspace),
        scratch_shapes=[
            pltpu.VMEM(kg.shape, blk),
            pltpu.VMEM(vg.shape, blk),
            pltpu.VMEM((2, 16 * CH, HD), blk),
            pltpu.VMEM((2, 16 * CH, HD), blk),
            pltpu.VMEM((16, 1, HD), jnp.float32),
            pltpu.VMEM((2, 8, QB), jnp.float32),
            pltpu.VMEM((NCTX, 2 * CH, 2 * HD), jnp.float32),
            pltpu.VMEM((NCTX, 2 * CH, 2 * HD), jnp.float32),
            pltpu.VMEM((2, HD, QB), jnp.float32),
            pltpu.VMEM((8, HD), jnp.int32),
            pltpu.SMEM((8, HD), jnp.int32),
            pltpu.SMEM((SPANS,), jnp.int32),
            pltpu.SMEM((SPANS + 8,), jnp.int32),
            pltpu.SemaphoreType.DMA((1,)),
            pltpu.SemaphoreType.DMA((2, 32)),
            pltpu.SemaphoreType.DMA((6, 2)),
            pltpu.SemaphoreType.DMA((4, 2)),
        ],
        compiler_params=pltpu.CompilerParams(vmem_limit_bytes=VMEM_MIB * MIB),
        cost_estimate=pl.CostEstimate(flops=8 * 10**9, bytes_accessed=32 * 10**6, transcendentals=4 * 10**6),
        name="attend",
    )(span_slot, queries, d_out, kg, vg, unit)


def plus(a, b):
    return (a.astype(jnp.float32) + b.astype(jnp.float32)).astype(jnp.bfloat16)


class Scatter:
    def __init__(self, first, parts, own, cross_in, near, full, near_b, full_b, send, recv, own_sem):
        self.plane = Plane(first)
        self.parts, self.own, self.cross_in, self.own_sem = parts, own, cross_in, own_sem
        self.near, self.full, self.near_b, self.full_b = near, full, near_b, full_b
        self.copies = Copies(send, recv)

    def dev(self, da, db, flip=False):
        return {"ctx": self.plane.at(da, db, flip)}

    def cross(self, q):
        for e in range(4):
            self.copies.start(
                self.parts.at[self.plane.at(e, q, True)], self.cross_in.at[q, e], 4 * q + e, self.dev(0, 0, True)
            )
            self.own_copy(q, e).start()

    def own_copy(self, q, e):
        return pltpu.make_async_copy(
            self.parts.at[self.plane.at(e, q)], self.own.at[q, e], self.own_sem.at[4 * q + e]
        )

    def add_cross(self, q, e):
        self.copies.landed(self.cross_in.at[q, e], 4 * q + e, self.dev(0, 0, True))
        self.own_copy(q, e).wait()
        self.cross_in[q, e] = plus(self.cross_in[q, e], self.own[q, e])

    def far(self, q):
        self.add_cross(q, 2)
        self.copies.start(self.cross_in.at[q, 2, pl.ds(0, CH)], self.near.at[q, 0], 16 + 4 * q, self.dev(1, 0))
        self.copies.start(self.cross_in.at[q, 2, pl.ds(CH, CH)], self.near.at[q, 1], 17 + 4 * q, self.dev(-1, 0))

    def next(self, q):
        self.add_cross(q, 1)
        self.add_cross(q, 3)
        self.copies.landed(self.near.at[q, 0], 16 + 4 * q, self.dev(-1, 0))
        self.cross_in[q, 1, 0:CH] = plus(self.cross_in[q, 1, 0:CH], self.near[q, 0])
        self.copies.start(self.cross_in.at[q, 1], self.full.at[q, 0], 18 + 4 * q, self.dev(1, 0))
        self.copies.landed(self.near.at[q, 1], 17 + 4 * q, self.dev(1, 0))
        self.cross_in[q, 3, CH:2 * CH] = plus(self.cross_in[q, 3, CH:2 * CH], self.near[q, 1])
        self.copies.start(self.cross_in.at[q, 3], self.full.at[q, 1], 19 + 4 * q, self.dev(-1, 0))

    def last(self, q):
        self.add_cross(q, 0)
        self.copies.landed(self.full.at[q, 0], 18 + 4 * q, self.dev(-1, 0))
        self.copies.landed(self.full.at[q, 1], 19 + 4 * q, self.dev(1, 0))
        return (
            self.cross_in[q, 0].astype(jnp.float32)
            + self.full[q, 0].astype(jnp.float32)
            + self.full[q, 1].astype(jnp.float32)
        )

    def last_far(self):
        self.cross_in[2, 0] = self.last(2).astype(jnp.bfloat16)
        self.copies.start(self.cross_in.at[2, 0, pl.ds(0, CH)], self.near_b.at[0], 32, self.dev(0, 1))
        self.copies.start(self.cross_in.at[2, 0, pl.ds(CH, CH)], self.near_b.at[1], 33, self.dev(0, -1))

    def last_near(self, q):
        index = 0 if q == 1 else 1
        step = 1 if q == 1 else -1
        rows = slice(index * CH, (index + 1) * CH)
        total = self.last(q)
        self.copies.landed(self.near_b.at[index], 32 + index, self.dev(0, -step))
        self.cross_in[q, 0] = total.astype(jnp.bfloat16)
        self.cross_in[q, 0, rows] = (total[rows] + self.near_b[index].astype(jnp.float32)).astype(jnp.bfloat16)
        self.copies.start(self.cross_in.at[q, 0], self.full_b.at[index], 34 + index, self.dev(0, step))

    def finish(self):
        total = self.last(0)
        self.copies.landed(self.full_b.at[0], 34, self.dev(0, -1))
        self.copies.landed(self.full_b.at[1], 35, self.dev(0, 1))
        return total + self.full_b[0].astype(jnp.float32) + self.full_b[1].astype(jnp.float32)


def scatter_kernel(
    pk_ref, pv_ref, near_ref, relay_ref, gk_ref, gv_ref, mid_ref, far_ref,
    k_own, k_cross, k_near, k_full, k_near_b, k_full_b,
    v_own, v_cross, v_near, v_full, v_near_b, v_full_b,
    k_send, k_recv, v_send, v_recv, w_send, w_recv, own_sems,
):
    barrier_with(ctx_targets() + head_targets((1, 3)))
    ways = [
        Scatter("y", pk_ref, k_own, k_cross, k_near, k_full, k_near_b, k_full_b, k_send, k_recv, own_sems.at[0]),
        Scatter("x", pv_ref, v_own, v_cross, v_near, v_full, v_near_b, v_full_b, v_send, v_recv, own_sems.at[1]),
    ]
    order = (2, 1, 3, 0)
    for q in order:
        for way in ways:
            way.cross(q)
    me_z = lax.axis_index("head")
    piece = relay_ref.shape[2]
    halves = [mid_ref.at[:, pl.ds(side * piece, piece)] for side in range(2)]
    sibling = {"ctx": Plane("x").at(0, 0, True)}
    moves = Copies(w_send, w_recv)
    for side, step in enumerate((1, -1)):
        moves.start(relay_ref.at[side], halves[side], side, {"head": turn(me_z, step, NZ)})
        moves.start(near_ref.at[side], far_ref.at[2 * side], 2 + side, sibling)
    for q in order:
        for way in ways:
            way.far(q)
    for q in order:
        for way in ways:
            way.next(q)
    for side, step in enumerate((1, -1)):
        moves.landed(halves[side], side, {"head": turn(me_z, -step, NZ)})
    moves.start(mid_ref, far_ref.at[1], 4, sibling)
    for way in ways:
        way.last_far()
    for way in ways:
        way.last_near(1)
    for way in ways:
        way.last_near(3)
    gk_ref[...] = (ways[0].finish() * SCALE).astype(jnp.bfloat16)
    gv_ref[...] = ways[1].finish().astype(jnp.bfloat16)
    for side in range(2):
        moves.landed(far_ref.at[2 * side], 2 + side, sibling)
    moves.landed(far_ref.at[1], 4, sibling)
    for way in ways:
        way.copies.finish()
    moves.finish()


def scatter_sums(pk, pv, near, relay):
    vmem = pl.BlockSpec(memory_space=pltpu.VMEM)
    hbm = pl.BlockSpec(memory_space=pl.ANY)
    blk = jnp.bfloat16
    one = [
        pltpu.VMEM((4, 4, 2 * CH, 2 * HD), blk),
        pltpu.VMEM((4, 4, 2 * CH, 2 * HD), blk),
        pltpu.VMEM((4, 2, CH, 2 * HD), blk),
        pltpu.VMEM((4, 2, 2 * CH, 2 * HD), blk),
        pltpu.VMEM((2, CH, 2 * HD), blk),
        pltpu.VMEM((2, 2 * CH, 2 * HD), blk),
    ]
    return pl.pallas_call(
        scatter_kernel,
        out_shape=(jax.ShapeDtypeStruct((2 * CH, 2 * HD), blk),) * 2 + (
            jax.ShapeDtypeStruct(near.shape[1:], blk),
            jax.ShapeDtypeStruct((3,) + near.shape[1:], blk),
        ),
        in_specs=[hbm] * 4,
        out_specs=(vmem,) * 2 + (hbm,) * 2,
        scratch_shapes=one + one + [pltpu.SemaphoreType.DMA((36,))] * 4 + [pltpu.SemaphoreType.DMA((5,))] * 2
        + [pltpu.SemaphoreType.DMA((2, 16))],
        compiler_params=pltpu.CompilerParams(
            collective_id=1, has_side_effects=True, vmem_limit_bytes=VMEM_MIB * MIB
        ),
        name="scatter_dkv",
    )(pk, pv, near, relay)


def project_kernel(
    gk_ref, gv_ref, hdq_ref, wk_hbm, wv_hbm, near_ref, mid_ref, far_ref, gx_ref, hg_ref,
    grads, weights, total, half, g_send, g_recv, o_send, o_recv, h_send, h_recv, w_sem, own_sem,
):
    me_z = lax.axis_index("head")
    y, x, core = ctx_coords()
    plane = Plane("x")
    barrier_with(
        [{"head": turn(me_z, d, NZ)} for d in (1, 2, 3)] + ctx_targets()
    )
    width = weights.shape[2]
    piece = width // 2
    sends = Copies(g_send, g_recv)
    for d in (1, 2, 3):
        sends.start(gk_ref, grads.at[d, 0], 2 * d - 2, {"head": turn(me_z, d, NZ)})
        sends.start(gv_ref, grads.at[d, 1], 2 * d - 1, {"head": turn(me_z, d, NZ)})

    units = Copies(h_send, h_recv)
    me = plane.at(0, 0)
    rows = [pl.ds(0, CH // 2), pl.ds(CH // 2, CH // 2)]
    own_copy = pltpu.make_async_copy(hdq_ref, hg_ref.at[y, x, core], own_sem.at[4])
    own_copy.start()
    own_copy.wait()
    for d in (1, 2, 3):
        for n, (da, db) in enumerate(((d, 0), (0, d))):
            units.start(
                hg_ref.at[y, x, core, rows[n]], hg_ref.at[y, x, core, rows[n]], 2 * d - 2 + n,
                {"ctx": plane.at(da, db)},
            )

    wrows = pl.ds(pl.multiple_of(me_z * width, width), width)
    fetches = [[
        pltpu.make_async_copy(wk_hbm.at[wrows], weights.at[0, 0], w_sem.at[0]),
        pltpu.make_async_copy(wv_hbm.at[wrows], weights.at[0, 1], w_sem.at[1]),
    ]]
    mine_rows = pl.ds(pl.multiple_of(core * piece, piece), piece)
    other_rows = pl.ds(pl.multiple_of((1 - core) * piece, piece), piece)
    nears = (near_ref.at[0], mid_ref, near_ref.at[1])
    for d, near in enumerate(nears, start=1):
        far = far_ref.at[d - 1]
        fetches.append([
            pltpu.make_async_copy(near, weights.at[d, :, mine_rows], w_sem.at[2 * d]),
            pltpu.make_async_copy(far, weights.at[d, :, other_rows], w_sem.at[2 * d + 1]),
        ])
    for pair in fetches:
        for copy in pair:
            copy.start()

    def partial(d, cols):
        left = (gk_ref[...], gv_ref[...]) if d == 0 else (grads[d, 0], grads[d, 1])
        return dot_nt(left[0], weights[d, 0, cols, :]) + dot_nt(left[1], weights[d, 1, cols, :])

    step = 512
    for copy in fetches[0]:
        copy.wait()

    def own_part(n, carry):
        cols = pl.ds(pl.multiple_of(n * step, step), step)
        total[:, cols] = partial(0, cols)
        return carry

    lax.fori_loop(0, width // step, own_part, 0)

    for d in (1, 2, 3):
        for n, (da, db) in enumerate(((-d, 0), (0, -d))):
            at = hg_ref.at[turn(y, db, NY), turn(x, da, NX), core, rows[n]]
            units.landed(at, 2 * d - 2 + n, {"ctx": plane.at(da, db)})
    for d in (1, 2, 3):
        units.start(
            hg_ref.at[y, :, core, rows[0]], hg_ref.at[y, :, core, rows[0]], 4 + 2 * d, {"ctx": plane.at(0, d)}
        )
        units.start(
            hg_ref.at[:, x, core, rows[1]], hg_ref.at[:, x, core, rows[1]], 5 + 2 * d, {"ctx": plane.at(d, 0)}
        )

    for d in (1, 3):
        for n in range(2):
            sends.landed(grads.at[d, n], 2 * d - 2 + n, {"head": turn(me_z, -d, NZ)})
        for copy in fetches[d]:
            copy.wait()

        def next_part(n, carry):
            cols = pl.ds(pl.multiple_of(n * step, step), step)
            total[:, cols] += partial(d, cols)
            return carry

        lax.fori_loop(0, width // step, next_part, 0)

    for n in range(2):
        sends.landed(grads.at[2, n], 2 + n, {"head": turn(me_z, -2, NZ)})
    for copy in fetches[2]:
        copy.wait()
    outs = Copies(o_send, o_recv)
    quarter = half.shape[0] // NZ
    own_copies = []
    for n in range(width // step):
        cols = pl.ds(n * step, step)
        half[:, n * step:(n + 1) * step] = (total[:, n * step:(n + 1) * step] + partial(2, cols)).astype(jnp.bfloat16)
        out_cols = pl.ds(pl.multiple_of(me_z * width + n * step, step), step)
        for d in (1, 2, 3):
            to = turn(me_z, d, NZ)
            outs.start(
                half.at[pl.ds(pl.multiple_of(to * quarter, quarter), quarter), cols],
                gx_ref.at[:, out_cols], 4 * (d - 1) + n, {"head": to},
            )
        own = pltpu.make_async_copy(
            half.at[pl.ds(pl.multiple_of(me_z * quarter, quarter), quarter), cols],
            gx_ref.at[:, out_cols], own_sem.at[n],
        )
        own.start()
        own_copies.append(own)

    for d in (1, 2, 3):
        units.landed(
            hg_ref.at[turn(y, -d, NY), :, core, rows[0]], 4 + 2 * d, {"ctx": plane.at(0, -d)}
        )
        units.landed(
            hg_ref.at[:, turn(x, -d, NX), core, rows[1]], 5 + 2 * d, {"ctx": plane.at(-d, 0)}
        )
    sibling = {"ctx": plane.at(0, 0, True)}
    units.start(hg_ref.at[:, :, core], hg_ref.at[:, :, core], 12, sibling)
    units.landed(hg_ref.at[:, :, 1 - core], 12, sibling)

    for n in range(width // step):
        for d in (1, 2, 3):
            origin = turn(me_z, -d, NZ)
            out_cols = pl.ds(pl.multiple_of(origin * width + n * step, step), step)
            outs.landed(gx_ref.at[:, out_cols], 4 * (d - 1) + n, {"head": origin})
    sends.finish()
    outs.finish()
    units.finish()
    for copy in own_copies:
        copy.wait()


def project(gk, gv, hdq, w_key, w_value, near, mid, far):
    vmem = pl.BlockSpec(memory_space=pltpu.VMEM)
    hbm = pl.BlockSpec(memory_space=pl.ANY)
    blk = jnp.bfloat16
    depth = w_key.shape[0]
    width = depth // NZ
    return pl.pallas_call(
        project_kernel,
        out_shape=(
            jax.ShapeDtypeStruct((2 * CH // NZ, depth), blk),
            jax.ShapeDtypeStruct((NY, NX, 2, CH, HD), blk),
        ),
        in_specs=[vmem, vmem, vmem] + [hbm] * 5,
        out_specs=(vmem, vmem),
        scratch_shapes=[
            pltpu.VMEM((NZ, 2, 2 * CH, 2 * HD), blk),
            pltpu.VMEM((NZ, 2, width, 2 * HD), blk),
            pltpu.VMEM((2 * CH, width), jnp.float32),
            pltpu.VMEM((2 * CH, width), blk),
            pltpu.SemaphoreType.DMA((6,)),
            pltpu.SemaphoreType.DMA((6,)),
            pltpu.SemaphoreType.DMA((12,)),
            pltpu.SemaphoreType.DMA((12,)),
            pltpu.SemaphoreType.DMA((13,)),
            pltpu.SemaphoreType.DMA((13,)),
            pltpu.SemaphoreType.DMA((8,)),
            pltpu.SemaphoreType.DMA((5,)),
        ],
        compiler_params=pltpu.CompilerParams(
            collective_id=2, has_side_effects=True, vmem_limit_bytes=VMEM_MIB * MIB
        ),
        name="project",
    )(gk, gv, hdq, w_key, w_value, near, mid, far)


def per_device(queries, keys, values, d_out, w_key, w_value, pair_list, span_slot):
    me = lax.axis_index("ctx")
    label_ids = jnp.arange(SPANS, dtype=jnp.int32)
    own_slots = 2 * me + jnp.arange(2, dtype=jnp.int32)
    own_labels = jnp.sum(
        jnp.where(span_slot[None, :] == own_slots[:, None], label_ids[None, :], 0), axis=1, dtype=jnp.int32
    )
    dense = jnp.arange(SPANS - 2, SPANS, dtype=jnp.int32)
    select = jnp.broadcast_to(
        (own_labels[None, :, None] == dense[:, None, None]).astype(jnp.bfloat16), (2, 2, HD)
    )
    pair_rows = jnp.pad(pair_list.astype(jnp.bfloat16), ((0, 0), (0, keys.shape[1] - 2)))
    keys_pad = jnp.concatenate([keys, pair_rows], axis=0)
    kg, vg, unit, near, relay = gather_all(keys_pad, values, queries, d_out, select, w_key, w_value)
    gq, hdq, pk, pv = attend(span_slot, queries, d_out, kg, vg, unit)
    grad_k, grad_v, mid, far = scatter_sums(pk, pv, near, relay)
    grad_x, units = project(grad_k, grad_v, hdq, w_key, w_value, near, mid, far)
    heads = units.reshape(NX * NY, 2, CH, HD)
    rows = []
    for i in range(2):
        which = jnp.clip(own_labels[i] - (SPANS - 2), 0, 1)
        picked = lax.dynamic_index_in_dim(heads, which, 1, keepdims=False)
        picked = picked.transpose(1, 0, 2).reshape(CH, NX * NY * HD)
        rows.append(jnp.where(own_labels[i] >= SPANS - 2, picked, gq[i * CH:(i + 1) * CH]))
    grad_q = jnp.concatenate(rows, axis=0)
    return (grad_q, grad_k, grad_v, grad_x)


def solution(mesh):
    return jax.shard_map(
        per_device,
        mesh=mesh,
        in_specs=(
            P("ctx", "head"),
            P("ctx", "head"),
            P("ctx", "head"),
            P("ctx", "head"),
            P(None, "head"),
            P(None, "head"),
            P("ctx", None),
            P(),
        ),
        out_specs=(P("ctx", "head"), P("ctx", "head"), P("ctx", "head"), P(("ctx", "head"), None)),
        check_vma=False,
    )
```

```python
import functools

import jax
import jax.numpy as jnp
from jax import lax
from jax.experimental import pallas as pl
from jax.experimental.pallas import tpu as pltpu
from jax.sharding import PartitionSpec as P

MESH = pl.DeviceIdType.MESH
HD = 128
CH = 128
SPANS = 64
NX = 4
NY = 4
NZ = 4
NCTX = NX * NY * 2
CHIPS = NX * NY
GROUP = 8
NPAD = 16
SCALE = HD ** -0.5
EXP_SCALE = SCALE * 1.4426950408889634
neg_fill = -1e30
QB = 1024
MIB = 1024 * 1024
VMEM_MIB = 62


def ctx_coords():
    me = lax.axis_index("ctx")
    return me // (2 * NX), lax.rem(me // 2, NX), lax.rem(me, 2)


def ctx_id(y, x, core):
    return (y * NX + x) * 2 + core


def turn(pos, step, size):
    return lax.rem(pos + step + size, size)


class Plane:
    def __init__(self, first):
        self.y, self.x, self.core = ctx_coords()
        self.first = first

    def at(self, da, db, flip=False):
        dy, dx = (da, db) if self.first == "y" else (db, da)
        core = 1 - self.core if flip else self.core
        return ctx_id(turn(self.y, dy, NY), turn(self.x, dx, NX), core)

    def chip(self, da, db):
        dy, dx = (da, db) if self.first == "y" else (db, da)
        return turn(self.y, dy, NY) * NX + turn(self.x, dx, NX)


def barrier_with(targets):
    barrier = pltpu.get_barrier_semaphore()
    for device in targets:
        pl.semaphore_signal(barrier, inc=1, device_id=device, device_id_type=MESH)
    pl.semaphore_wait(barrier, len(targets))


def ctx_targets():
    plane = Plane("x")
    steps = [(1, 0), (2, 0), (3, 0), (0, 1), (0, 2), (0, 3)]
    return [{"ctx": plane.at(da, db)} for da, db in steps] + [{"ctx": plane.at(0, 0, True)}]


def head_targets(steps):
    me_z = lax.axis_index("head")
    return [{"head": turn(me_z, d, NZ)} for d in steps]


class Copies:
    def __init__(self, send, recv):
        self.send, self.recv, self.started = send, recv, []

    def start(self, src, dst, index, device):
        copy = pltpu.make_async_remote_copy(
            src_ref=src, dst_ref=dst, send_sem=self.send.at[index], recv_sem=self.recv.at[index],
            device_id=device, device_id_type=MESH,
        )
        copy.start()
        self.started.append(copy)

    def landed(self, dst, index, device):
        pltpu.make_async_remote_copy(
            src_ref=dst, dst_ref=dst, send_sem=self.send.at[index], recv_sem=self.recv.at[index],
            device_id=device, device_id_type=MESH,
        ).wait_recv()

    def finish(self):
        for copy in self.started:
            copy.wait_send()


DA_OF = (0, -1, 1, 2)


class Gather:
    def __init__(self, first, out, send, recv):
        self.plane = Plane(first)
        self.out = out
        self.copies = Copies(send, recv)

    def dev(self, da, db):
        return {"ctx": self.plane.at(da, db)}

    def region(self, da, db):
        return self.out.at[self.plane.chip(da, db)]

    def send(self, region, index, da, db):
        self.copies.start(region, region, index, self.dev(da, db))

    def begin_a(self):
        self.send(self.region(0, 0), 0, 1, 0)
        self.send(self.region(0, 0), 1, -1, 0)

    def spread(self, m):
        region = self.region(DA_OF[m], 0)
        self.send(region, 4 + 4 * m, 0, 1)
        self.send(region, 5 + 4 * m, 0, -1)

    def got_a(self, step):
        index = 0 if step < 0 else 1
        region = self.region(step, 0)
        self.copies.landed(region, index, self.dev(step, 0))
        self.send(region.at[index], 2 + index, -step, 0)

    def got_a_far(self):
        region = self.region(2, 0)
        self.copies.landed(region.at[0], 2, self.dev(-1, 0))
        self.copies.landed(region.at[1], 3, self.dev(1, 0))

    def got_b(self, m, step):
        index = 0 if step < 0 else 1
        region = self.region(DA_OF[m], step)
        self.copies.landed(region, 4 + 4 * m + index, self.dev(0, step))
        self.send(region.at[index], 6 + 4 * m + index, 0, -step)

    def got_b_far(self, m):
        region = self.region(DA_OF[m], 2)
        self.copies.landed(region.at[0], 6 + 4 * m, self.dev(0, -1))
        self.copies.landed(region.at[1], 7 + 4 * m, self.dev(0, 1))


def gather_kernel(
    keys_ref, values_ref, q_ref, do_ref, sel_ref, wk_hbm, wv_hbm,
    kg_ref, vg_ref, unit_ref, qx_ref, dox_ref, near_ref,
    give, held, from_core, first_in, mid, last_in,
    k_send, k_recv, v_send, v_recv, u_send, u_recv, w_send, w_recv, c_send, c_recv, own_sem,
):
    barrier_with(ctx_targets() + head_targets((1, 3)))
    y, x, core = ctx_coords()
    plane = Plane("x")
    chip = plane.chip(0, 0)
    sibling = {"ctx": plane.at(0, 0, True)}
    gathers = [
        Gather("x", kg_ref, k_send, k_recv),
        Gather("y", vg_ref, v_send, v_recv),
    ]

    def group_cols(which, width):
        return pl.ds(pl.multiple_of(which * width, width), width)

    cross = Copies(c_send, c_recv)
    other = group_cols(1 - core, HD)
    cross.start(keys_ref.at[:, other], kg_ref.at[chip, core], 0, sibling)
    cross.start(values_ref.at[:, other], vg_ref.at[chip, core], 1, sibling)
    mine = group_cols(core, HD)
    own_copies = [
        pltpu.make_async_copy(keys_ref.at[:, mine], kg_ref.at[chip, core], own_sem.at[0]),
        pltpu.make_async_copy(values_ref.at[:, mine], vg_ref.at[chip, core], own_sem.at[1]),
    ]
    for copy in own_copies:
        copy.start()

    def pick(dst, group):
        def unit(j, carry):
            cols = pl.ds(pl.multiple_of((group * GROUP + lax.rem(j, GROUP)) * HD, HD), HD)
            first = sel_ref[j // GROUP, 0:1, :]
            second = sel_ref[j // GROUP, 1:2, :]
            for n, ref in enumerate((q_ref, do_ref)):
                dst[n, j // NX, lax.rem(j, NX)] = ref[0:CH, cols] * first + ref[CH:2 * CH, cols] * second
            return carry

        lax.fori_loop(0, CHIPS, unit, 0)

    units = Copies(u_send, u_recv)
    pick(give, 1 - core)
    units.start(give, from_core, 0, sibling)

    for copy in own_copies:
        copy.wait()
    cross.landed(kg_ref.at[chip, 1 - core], 0, sibling)
    cross.landed(vg_ref.at[chip, 1 - core], 1, sibling)
    for gather in gathers:
        gather.begin_a()
    for gather in gathers:
        gather.spread(0)

    me_z = lax.axis_index("head")
    piece = near_ref.shape[2]
    moves = Copies(w_send, w_recv)
    for n, ref in enumerate((wk_hbm, wv_hbm)):
        for side, step in enumerate((1, -1)):
            to = turn(me_z, step, NZ)
            start = pl.multiple_of((2 * to + core) * piece, piece)
            moves.start(ref.at[pl.ds(start, piece)], near_ref.at[side, n], 2 * side + n, {"head": to})

    qcols = group_cols(1 - core, GROUP * HD)
    cross.start(q_ref.at[:, qcols], qx_ref, 2, sibling)
    cross.start(do_ref.at[:, qcols], dox_ref, 3, sibling)

    pick(held, core)
    units.landed(from_core, 0, sibling)

    def add_core(j, carry):
        for n in range(2):
            held[n, j // NX, lax.rem(j, NX)] += from_core[n, j // NX, lax.rem(j, NX)]
        return carry

    lax.fori_loop(0, CHIPS, add_core, 0)
    for d in (1, 2, 3):
        far_x, far_y = turn(x, d, NX), turn(y, d, NY)
        units.start(held.at[0, :, far_x], first_in.at[0, d - 1], d, {"ctx": plane.at(d, 0)})
        units.start(held.at[1, far_y], first_in.at[1, d - 1], 3 + d, {"ctx": plane.at(0, d)})

    for gather in gathers:
        gather.got_a(-1)
        gather.got_a(1)
    for gather in gathers:
        gather.spread(1)
        gather.spread(2)
    for gather in gathers:
        gather.got_b(0, -1)
        gather.got_b(0, 1)
    for gather in gathers:
        gather.got_a_far()
        gather.spread(3)

    for d in (1, 2, 3):
        units.landed(first_in.at[0, d - 1], d, {"ctx": plane.at(-d, 0)})
        units.landed(first_in.at[1, d - 1], 3 + d, {"ctx": plane.at(0, -d)})
    for n in range(4):
        mid[0, n] = held[0, n, x] + first_in[0, 0, n] + first_in[0, 1, n] + first_in[0, 2, n]
        mid[1, n] = held[1, y, n] + first_in[1, 0, n] + first_in[1, 1, n] + first_in[1, 2, n]
    for d in (1, 2, 3):
        units.start(mid.at[0, turn(y, d, NY)], last_in.at[0, d - 1], 6 + d, {"ctx": plane.at(0, d)})
        units.start(mid.at[1, turn(x, d, NX)], last_in.at[1, d - 1], 9 + d, {"ctx": plane.at(d, 0)})

    for m in (1, 2, 3):
        for gather in gathers:
            gather.got_b(m, -1)
            gather.got_b(m, 1)

    for d in (1, 2, 3):
        units.landed(last_in.at[0, d - 1], 6 + d, {"ctx": plane.at(0, -d)})
        units.landed(last_in.at[1, d - 1], 9 + d, {"ctx": plane.at(-d, 0)})
    unit_ref[0] = mid[0, y] + last_in[0, 0] + last_in[0, 1] + last_in[0, 2]
    unit_ref[1] = mid[1, x] + last_in[1, 0] + last_in[1, 1] + last_in[1, 2]

    cross.landed(qx_ref, 2, sibling)
    cross.landed(dox_ref, 3, sibling)
    for n in range(2):
        for side, step in enumerate((1, -1)):
            moves.landed(near_ref.at[side, n], 2 * side + n, {"head": turn(me_z, -step, NZ)})
    for m in range(4):
        for gather in gathers:
            gather.got_b_far(m)
    for gather in gathers:
        gather.copies.finish()
    cross.finish()
    units.finish()
    moves.finish()


def gather_all(keys_pad, values, queries, d_out, select, w_key, w_value):
    vmem = pl.BlockSpec(memory_space=pltpu.VMEM)
    anyspace = pl.BlockSpec(memory_space=pl.ANY)
    blk = jnp.bfloat16
    piece = w_key.shape[0] // NZ // 2
    return pl.pallas_call(
        gather_kernel,
        out_shape=(
            jax.ShapeDtypeStruct((CHIPS, 2, keys_pad.shape[0], HD), blk),
            jax.ShapeDtypeStruct((CHIPS, 2, values.shape[0], HD), blk),
            jax.ShapeDtypeStruct((2, CH, HD), blk),
            jax.ShapeDtypeStruct((2 * CH, GROUP * HD), blk),
            jax.ShapeDtypeStruct((2 * CH, GROUP * HD), blk),
            jax.ShapeDtypeStruct((2, 2, piece) + w_key.shape[1:], blk),
        ),
        in_specs=[vmem] * 5 + [anyspace] * 2,
        out_specs=(anyspace, anyspace, vmem, anyspace, anyspace, anyspace),
        scratch_shapes=[
            pltpu.VMEM((2, NY, NX, CH, HD), blk),
            pltpu.VMEM((2, NY, NX, CH, HD), blk),
            pltpu.VMEM((2, NY, NX, CH, HD), blk),
            pltpu.VMEM((2, 3, 4, CH, HD), blk),
            pltpu.VMEM((2, 4, CH, HD), blk),
            pltpu.VMEM((2, 3, CH, HD), blk),
            pltpu.SemaphoreType.DMA((20,)),
            pltpu.SemaphoreType.DMA((20,)),
            pltpu.SemaphoreType.DMA((20,)),
            pltpu.SemaphoreType.DMA((20,)),
            pltpu.SemaphoreType.DMA((13,)),
            pltpu.SemaphoreType.DMA((13,)),
            pltpu.SemaphoreType.DMA((4,)),
            pltpu.SemaphoreType.DMA((4,)),
            pltpu.SemaphoreType.DMA((4,)),
            pltpu.SemaphoreType.DMA((4,)),
            pltpu.SemaphoreType.DMA((2,)),
        ],
        compiler_params=pltpu.CompilerParams(
            collective_id=0, has_side_effects=True, vmem_limit_bytes=VMEM_MIB * MIB
        ),
        name="gather_kv",
    )(keys_pad, values, queries, d_out, select, w_key, w_value)


def dot_nt(a, b):
    return lax.dot_general(a, b, (((1,), (1,)), ((), ())), preferred_element_type=jnp.float32)


def dot_nn(a, b):
    return lax.dot_general(a, b, (((1,), (0,)), ((), ())), preferred_element_type=jnp.float32)


def dot_tn(a, b):
    return lax.dot_general(a, b, (((0,), (0,)), ((), ())), preferred_element_type=jnp.float32)


def attend_kernel(
    span_slot, q_hbm, do_hbm, qx_hbm, dox_hbm, kg_hbm, vg_hbm, unit_ref,
    gq_ref, gqx_ref, hdq_ref, pk_hbm, pv_hbm,
    kg, vg, qs, ds, gq_all, probs, dprob, tops, stat, acck, accv, dqt, found, flags, slot_label, todo,
    flag_sem, qsems, load_sems, store_sems,
):
    me = lax.axis_index("ctx")
    core = lax.rem(me, 2)
    unit = me // 2
    quarter = NCTX // 4
    pair_copy = pltpu.make_async_copy(
        kg_hbm.at[:, pl.ds(2 * CH, NPAD)], kg.at[:, pl.ds(2 * CH, NPAD)], load_sems.at[4, 0]
    )
    pair_copy.start()
    loads = []
    for n in range(4):
        part = pl.ds(n * quarter, quarter)
        for side, (src, dst) in enumerate(((kg_hbm, kg), (vg_hbm, vg))):
            at = (part, pl.ds(0, 2 * CH))
            loads.append(pltpu.make_async_copy(src.at[at], dst.at[at], load_sems.at[n, side]))
            loads[-1].start()
    stacks = []
    for u in range(4):
        for r in range(GROUP):
            rows = pl.ds((u % 2) * CH, CH)
            own_cols = pl.ds(pl.multiple_of((core * GROUP + r) * HD, HD), HD)
            for n, (own, other, dst) in enumerate(((q_hbm, qx_hbm, qs), (do_hbm, dox_hbm, ds))):
                src = own.at[rows, own_cols] if u < 2 else other.at[rows, pl.ds(r * HD, HD)]
                stacks.append(pltpu.make_async_copy(src, dst.at[u, pl.ds(r * CH, CH)], qsems.at[n, u * GROUP + r]))
    for copy in stacks:
        copy.start()

    def name_slot(c, carry):
        slot_label[span_slot[c]] = c
        return carry

    lax.fori_loop(0, SPANS, name_slot, 0)

    def slot_of(u):
        return 2 * (2 * unit + lax.rem(core + u // 2, 2)) + lax.rem(u, 2)

    pair_copy.wait()
    pair_rows = kg[:, 2 * CH:2 * CH + NPAD, :].reshape(NCTX * NPAD, HD).astype(jnp.float32)
    lanes = lax.broadcasted_iota(jnp.int32, (1, HD), 1).astype(jnp.float32)
    for u in range(4):
        own = slot_label[slot_of(u)].astype(jnp.float32)
        hit = jnp.logical_and(pair_rows[:, 0:1] == own, pair_rows[:, 1:2] == lanes)
        found[u:u + 1, :] = jnp.max(jnp.where(hit, 1.0, 0.0), axis=0, keepdims=True).astype(jnp.int32)
    flag_copy = pltpu.make_async_copy(found, flags, flag_sem.at[0])
    flag_copy.start()

    label = SPANS - 2 + unit // GROUP
    q_unit = unit_ref[0]
    do_unit = unit_ref[1]

    def four(ref, t):
        return jnp.concatenate([ref[2 * t, 0:2 * CH, :], ref[2 * t + 1, 0:2 * CH, :]], axis=0)

    def unit_first(t, carry):
        top, total, mix = carry
        scores = dot_nt(four(kg, t), q_unit) * EXP_SCALE
        mixed = dot_nt(four(vg, t), do_unit)
        diff = lax.broadcasted_iota(jnp.int32, (CH, HD), 0) - lax.broadcasted_iota(jnp.int32, (CH, HD), 1)
        scores = jnp.concatenate([
            jnp.where(diff <= (label - slot_label[4 * t + u]) * CH, scores[u * CH:(u + 1) * CH], neg_fill)
            for u in range(4)
        ], axis=0)
        new_top = jnp.maximum(top, jnp.max(scores, axis=0, keepdims=True))
        weights = jnp.exp2(scores - new_top)
        factor = jnp.exp2(top - new_top)
        probs[t] = weights
        dprob[t] = mixed
        tops[t] = new_top
        return (
            new_top,
            total * factor + jnp.sum(weights, axis=0, keepdims=True),
            mix * factor + jnp.sum(weights * mixed, axis=0, keepdims=True),
        )

    zero_row = jnp.zeros((1, HD), jnp.float32)
    state = (jnp.full((1, HD), neg_fill, jnp.float32), zero_row, zero_row)
    for n in range(4):
        for copy in loads[2 * n:2 * n + 2]:
            copy.wait()
        state = lax.fori_loop(n * quarter // 2, (n + 1) * quarter // 2, unit_first, state)
    top, total, mix = state
    over = 1.0 / total
    delta = mix * over

    def unit_second(t, acc):
        factor = jnp.exp2(tops[t] - top) * over
        weights = probs[t] * factor
        dscore = (weights * (dprob[t] - delta)).astype(jnp.bfloat16)
        value_part = dot_nn(weights.astype(jnp.bfloat16), do_unit)
        key_part = dot_nn(dscore, q_unit)
        for u in range(2):
            accv[2 * t + u] = value_part[2 * u * CH:2 * (u + 1) * CH]
            acck[2 * t + u] = key_part[2 * u * CH:2 * (u + 1) * CH]
        return acc + dot_tn(four(kg, t), dscore)

    acc = lax.fori_loop(0, NCTX // 2, unit_second, jnp.zeros((HD, CH), jnp.float32))
    hdq_ref[...] = (acc * SCALE).T.astype(jnp.bfloat16)

    flag_copy.wait()
    for copy in stacks:
        copy.wait()

    def span_work(u, carry):
        own_slot = slot_of(u)
        own_label = slot_label[own_slot]

        @pl.when(own_label < SPANS - 2)
        def _():
            todo[0] = own_slot

            def note(c, n):
                todo[n] = span_slot[c]
                wanted = jnp.logical_and(flags[u, c] > 0, c != own_label)
                return n + wanted.astype(jnp.int32)

            count = lax.fori_loop(0, SPANS, note, jnp.int32(1))
            todo[count] = own_slot

            def rows_at(slot):
                return pl.ds(pl.multiple_of(lax.rem(slot, 2) * CH, CH), CH)

            def both(ref, t):
                a, b = todo[2 * t], todo[2 * t + 1]
                return jnp.concatenate([ref[a // 2, rows_at(a), :], ref[b // 2, rows_at(b), :]], axis=0)

            limits = (0, jnp.where(count >= 2, CH, -CH))
            tail = (CH, -CH)
            odd = jnp.logical_and(lax.rem(count, 2) == 1, count > 1)

            def dots(t, limits):
                scores = dot_nt(both(kg, t), qs[u]) * EXP_SCALE
                if limits is not None:
                    diff = lax.broadcasted_iota(jnp.int32, (CH, QB), 0) - lax.rem(
                        lax.broadcasted_iota(jnp.int32, (CH, QB), 1), CH
                    )
                    scores = jnp.concatenate([
                        jnp.where(diff <= limits[v], scores[v * CH:(v + 1) * CH], neg_fill) for v in range(2)
                    ], axis=0)
                return scores, dot_nt(both(vg, t), ds[u])

            def first(t, limits=None):
                scores, mixed = dots(t, limits)
                old_top = stat[0:1, :]
                new_top = jnp.maximum(old_top, jnp.max(scores, axis=0, keepdims=True))
                weights = jnp.exp2(scores - new_top)
                factor = jnp.exp2(old_top - new_top)
                stat[0:1, :] = new_top
                stat[1:2, :] = stat[1:2, :] * factor + jnp.sum(weights, axis=0, keepdims=True)
                stat[2:3, :] = stat[2:3, :] * factor + jnp.sum(weights * mixed, axis=0, keepdims=True)

            def second(t, limits=None):
                scores, mixed = dots(t, limits)
                weights = jnp.exp2(scores - stat[3:4, :])
                dscore = (weights * (mixed - stat[4:5, :])).astype(jnp.bfloat16)
                value_part = dot_nn(weights.astype(jnp.bfloat16), ds[u])
                key_part = dot_nn(dscore, qs[u])
                for v in range(2):
                    slot = todo[2 * t + v]
                    accv[slot // 2, rows_at(slot), :] += value_part[v * CH:(v + 1) * CH]
                    acck[slot // 2, rows_at(slot), :] += key_part[v * CH:(v + 1) * CH]
                dqt[...] += dot_tn(both(kg, t), dscore)

            def sweep(work):
                work(0, limits)

                def plain(t, c):
                    work(t)
                    return c

                lax.fori_loop(1, count // 2, plain, 0)

                @pl.when(odd)
                def _():
                    work(count // 2, tail)

            stat[0:1, :] = jnp.full((1, QB), neg_fill, jnp.float32)
            stat[1:3, :] = jnp.zeros((2, QB), jnp.float32)
            sweep(first)
            total_row = stat[1:2, :]
            stat[3:4, :] = stat[0:1, :] + jnp.log2(total_row)
            stat[4:5, :] = stat[2:3, :] / total_row
            dqt[...] = jnp.zeros_like(dqt)
            sweep(second)
            for r in range(GROUP):
                gq_all[pl.ds(pl.multiple_of(u * CH, CH), CH), r * HD:(r + 1) * HD] = (
                    (dqt[:, r * CH:(r + 1) * CH] * SCALE).T.astype(jnp.bfloat16)
                )

        return carry

    lax.fori_loop(0, 4, span_work, 0)

    stores = [
        pltpu.make_async_copy(gq_all.at[pl.ds(0, 2 * CH)], gq_ref, store_sems.at[4, 0]),
        pltpu.make_async_copy(gq_all.at[pl.ds(2 * CH, 2 * CH)], gqx_ref, store_sems.at[4, 1]),
    ]
    for copy in stores:
        copy.start()
    for n in range(4):
        part = pl.ds(n * quarter, quarter)

        def narrow(t, carry):
            kg[t, 0:2 * CH, :] = acck[t].astype(jnp.bfloat16)
            vg[t] = accv[t].astype(jnp.bfloat16)
            return carry

        lax.fori_loop(n * quarter, (n + 1) * quarter, narrow, 0)
        for side, (src, dst) in enumerate(((kg.at[part, pl.ds(0, 2 * CH)], pk_hbm), (vg.at[part], pv_hbm))):
            stores.append(pltpu.make_async_copy(src, dst.at[part], store_sems.at[n, side]))
            stores[-1].start()
    for copy in stores:
        copy.wait()


def attend(span_slot, queries, d_out, qx, dox, kg, vg, unit):
    vmem = pl.BlockSpec(memory_space=pltpu.VMEM)
    smem = pl.BlockSpec(memory_space=pltpu.SMEM)
    anyspace = pl.BlockSpec(memory_space=pl.ANY)
    blk = jnp.bfloat16
    return pl.pallas_call(
        attend_kernel,
        out_shape=(
            jax.ShapeDtypeStruct((2 * CH, GROUP * HD), blk),
            jax.ShapeDtypeStruct((2 * CH, GROUP * HD), blk),
            jax.ShapeDtypeStruct((CH, HD), blk),
            jax.ShapeDtypeStruct((NCTX, 2 * CH, HD), blk),
            jax.ShapeDtypeStruct((NCTX, 2 * CH, HD), blk),
        ),
        in_specs=[smem] + [anyspace] * 6 + [vmem],
        out_specs=(anyspace, anyspace, vmem, anyspace, anyspace),
        scratch_shapes=[
            pltpu.VMEM(kg.shape, blk),
            pltpu.VMEM(vg.shape, blk),
            pltpu.VMEM((4, GROUP * CH, HD), blk),
            pltpu.VMEM((4, GROUP * CH, HD), blk),
            pltpu.VMEM((4 * CH, GROUP * HD), blk),
            pltpu.VMEM((NCTX // 2, 4 * CH, HD), jnp.float32),
            pltpu.VMEM((NCTX // 2, 4 * CH, HD), jnp.float32),
            pltpu.VMEM((NCTX // 2, 1, HD), jnp.float32),
            pltpu.VMEM((8, QB), jnp.float32),
            pltpu.VMEM((NCTX, 2 * CH, HD), jnp.float32),
            pltpu.VMEM((NCTX, 2 * CH, HD), jnp.float32),
            pltpu.VMEM((HD, QB), jnp.float32),
            pltpu.VMEM((8, HD), jnp.int32),
            pltpu.SMEM((8, HD), jnp.int32),
            pltpu.SMEM((SPANS,), jnp.int32),
            pltpu.SMEM((SPANS + 8,), jnp.int32),
            pltpu.SemaphoreType.DMA((1,)),
            pltpu.SemaphoreType.DMA((2, 32)),
            pltpu.SemaphoreType.DMA((5, 2)),
            pltpu.SemaphoreType.DMA((5, 2)),
        ],
        compiler_params=pltpu.CompilerParams(vmem_limit_bytes=VMEM_MIB * MIB),
        cost_estimate=pl.CostEstimate(flops=8 * 10**9, bytes_accessed=32 * 10**6, transcendentals=4 * 10**6),
        name="attend",
    )(span_slot, queries, d_out, qx, dox, kg, vg, unit)


def plus(a, b):
    return (a.astype(jnp.float32) + b.astype(jnp.float32)).astype(jnp.bfloat16)


class Scatter:
    def __init__(self, first, parts, own, near, full, near_b, full_b, send, recv, own_sem):
        self.plane = Plane(first)
        self.parts, self.own, self.own_sem = parts, own, own_sem
        self.near, self.full, self.near_b, self.full_b = near, full, near_b, full_b
        self.copies = Copies(send, recv)

    def dev(self, da, db):
        return {"ctx": self.plane.at(da, db)}

    def load(self, q, e):
        return pltpu.make_async_copy(self.parts.at[self.plane.chip(e, q)], self.own.at[q, e], self.own_sem.at[4 * q + e])

    def far(self, q):
        block = self.parts.at[self.plane.chip(2, q)]
        self.copies.start(block.at[0], self.near.at[q, 0], 4 * q, self.dev(1, 0))
        self.copies.start(block.at[1], self.near.at[q, 1], 4 * q + 1, self.dev(-1, 0))

    def next(self, q):
        for side, step in enumerate((1, -1)):
            e = step % 4
            self.load(q, e).wait()
            self.copies.landed(self.near.at[q, side], 4 * q + side, self.dev(-step, 0))
            self.own[q, e, side] = plus(self.own[q, e, side], self.near[q, side])
            self.copies.start(self.own.at[q, e], self.full.at[q, side], 4 * q + 2 + side, self.dev(step, 0))

    def last(self, q):
        self.load(q, 0).wait()
        self.copies.landed(self.full.at[q, 0], 4 * q + 2, self.dev(-1, 0))
        self.copies.landed(self.full.at[q, 1], 4 * q + 3, self.dev(1, 0))
        return (
            self.own[q, 0].astype(jnp.float32)
            + self.full[q, 0].astype(jnp.float32)
            + self.full[q, 1].astype(jnp.float32)
        )

    def last_far(self):
        self.own[2, 0] = self.last(2).astype(jnp.bfloat16)
        for side, step in enumerate((1, -1)):
            self.copies.start(self.own.at[2, 0, side], self.near_b.at[side], 16 + side, self.dev(0, step))

    def last_near(self, side):
        step = (1, -1)[side]
        q = step % 4
        total = self.last(q)
        self.copies.landed(self.near_b.at[side], 16 + side, self.dev(0, -step))
        self.own[q, 0, 1 - side] = total[1 - side].astype(jnp.bfloat16)
        self.own[q, 0, side] = (total[side] + self.near_b[side].astype(jnp.float32)).astype(jnp.bfloat16)
        self.copies.start(self.own.at[q, 0], self.full_b.at[side], 18 + side, self.dev(0, step))

    def finish(self):
        total = self.last(0)
        self.copies.landed(self.full_b.at[0], 18, self.dev(0, -1))
        self.copies.landed(self.full_b.at[1], 19, self.dev(0, 1))
        return total + self.full_b[0].astype(jnp.float32) + self.full_b[1].astype(jnp.float32)


def scatter_kernel(
    pk_ref, pv_ref, near_ref, gqx_ref, wk_hbm, wv_hbm, gk_ref, gv_ref, gqo_ref, mid_ref, far_ref,
    k_own, k_near, k_full, k_near_b, k_full_b,
    v_own, v_near, v_full, v_near_b, v_full_b, sums, swap, swap_in,
    k_send, k_recv, v_send, v_recv, w_send, w_recv, c_send, c_recv, own_sems,
):
    barrier_with(ctx_targets() + head_targets((1, 2, 3)))
    core = lax.rem(lax.axis_index("ctx"), 2)
    sibling = {"ctx": Plane("x").at(0, 0, True)}
    ways = [
        Scatter("y", pk_ref, k_own, k_near, k_full, k_near_b, k_full_b, k_send, k_recv, own_sems.at[0]),
        Scatter("x", pv_ref, v_own, v_near, v_full, v_near_b, v_full_b, v_send, v_recv, own_sems.at[1]),
    ]
    order = (2, 1, 3, 0)
    for q in order:
        for way in ways:
            way.far(q)
    for e in (1, 3, 0):
        for q in order:
            for way in ways:
                way.load(q, e).start()

    me_z = lax.axis_index("head")
    piece = mid_ref.shape[1]
    moves = Copies(w_send, w_recv)
    two = turn(me_z, 2, NZ)
    start = pl.multiple_of((2 * two + core) * piece, piece)
    for n, ref in enumerate((wk_hbm, wv_hbm)):
        moves.start(ref.at[pl.ds(start, piece)], mid_ref.at[n], n, {"head": two})
    cross = Copies(c_send, c_recv)
    cross.start(gqx_ref, gqo_ref, 0, sibling)
    for side in range(2):
        cross.start(near_ref.at[side], far_ref.at[2 * side], 1 + side, sibling)

    for q in order:
        for way in ways:
            way.next(q)
    for way in ways:
        way.last_far()
    for side in range(2):
        for way in ways:
            way.last_near(side)
    cross.landed(gqo_ref, 0, sibling)
    for side in range(2):
        cross.landed(far_ref.at[2 * side], 1 + side, sibling)
    for n, (way, factor) in enumerate(zip(ways, (SCALE, 1.0))):
        sums[...] = way.finish() * factor
        swap[n] = sums[1 - core].astype(jnp.bfloat16)
        cross.start(swap.at[n], swap_in.at[n], 4 + n, sibling)
        out = (gk_ref, gv_ref)[n]
        out[:, pl.ds(pl.multiple_of(core * HD, HD), HD)] = sums[core].astype(jnp.bfloat16)
    for n in range(2):
        moves.landed(mid_ref.at[n], n, {"head": two})
    cross.start(mid_ref, far_ref.at[1], 3, sibling)
    for n, out in enumerate((gk_ref, gv_ref)):
        cross.landed(swap_in.at[n], 4 + n, sibling)
        out[:, pl.ds(pl.multiple_of((1 - core) * HD, HD), HD)] = swap_in[n]
    cross.landed(far_ref.at[1], 3, sibling)
    for way in ways:
        way.copies.finish()
    moves.finish()
    cross.finish()


def scatter_sums(pk, pv, near, gqx, w_key, w_value):
    vmem = pl.BlockSpec(memory_space=pltpu.VMEM)
    anyspace = pl.BlockSpec(memory_space=pl.ANY)
    blk = jnp.bfloat16
    block = (2, 2 * CH, HD)
    one = [
        pltpu.VMEM((4, 4) + block, blk),
        pltpu.VMEM((4,) + block, blk),
        pltpu.VMEM((4, 2) + block, blk),
        pltpu.VMEM(block, blk),
        pltpu.VMEM((2,) + block, blk),
    ]
    return pl.pallas_call(
        scatter_kernel,
        out_shape=(jax.ShapeDtypeStruct((2 * CH, 2 * HD), blk),) * 2 + (
            jax.ShapeDtypeStruct(gqx.shape, blk),
            jax.ShapeDtypeStruct(near.shape[1:], blk),
            jax.ShapeDtypeStruct((3,) + near.shape[1:], blk),
        ),
        in_specs=[anyspace] * 6,
        out_specs=(vmem,) * 2 + (anyspace,) * 3,
        scratch_shapes=one + one
        + [pltpu.VMEM(block, jnp.float32), pltpu.VMEM(block, blk), pltpu.VMEM(block, blk)]
        + [pltpu.SemaphoreType.DMA((20,))] * 4
        + [pltpu.SemaphoreType.DMA((2,))] * 2
        + [pltpu.SemaphoreType.DMA((6,))] * 2
        + [pltpu.SemaphoreType.DMA((2, 16))],
        compiler_params=pltpu.CompilerParams(
            collective_id=1, has_side_effects=True, vmem_limit_bytes=VMEM_MIB * MIB
        ),
        name="scatter_dkv",
    )(pk, pv, near, gqx, w_key, w_value)


def project_kernel(
    gk_ref, gv_ref, hdq_ref, wk_hbm, wv_hbm, near_ref, mid_ref, far_ref, gx_ref, hg_ref,
    grads, weights, total, half, g_send, g_recv, o_send, o_recv, h_send, h_recv, w_sem, own_sem,
):
    me_z = lax.axis_index("head")
    y, x, core = ctx_coords()
    plane = Plane("x")
    barrier_with(
        [{"head": turn(me_z, d, NZ)} for d in (1, 2, 3)] + ctx_targets()
    )
    width = weights.shape[2]
    piece = width // 2
    sends = Copies(g_send, g_recv)
    for d in (1, 2, 3):
        sends.start(gk_ref, grads.at[d, 0], 2 * d - 2, {"head": turn(me_z, d, NZ)})
        sends.start(gv_ref, grads.at[d, 1], 2 * d - 1, {"head": turn(me_z, d, NZ)})

    units = Copies(h_send, h_recv)
    me = plane.at(0, 0)
    rows = [pl.ds(0, CH // 2), pl.ds(CH // 2, CH // 2)]
    own_copy = pltpu.make_async_copy(hdq_ref, hg_ref.at[y, x, core], own_sem.at[4])
    own_copy.start()
    own_copy.wait()
    for d in (1, 2, 3):
        for n, (da, db) in enumerate(((d, 0), (0, d))):
            units.start(
                hg_ref.at[y, x, core, rows[n]], hg_ref.at[y, x, core, rows[n]], 2 * d - 2 + n,
                {"ctx": plane.at(da, db)},
            )

    wrows = pl.ds(pl.multiple_of(me_z * width, width), width)
    fetches = [[
        pltpu.make_async_copy(wk_hbm.at[wrows], weights.at[0, 0], w_sem.at[0]),
        pltpu.make_async_copy(wv_hbm.at[wrows], weights.at[0, 1], w_sem.at[1]),
    ]]
    mine_rows = pl.ds(pl.multiple_of(core * piece, piece), piece)
    other_rows = pl.ds(pl.multiple_of((1 - core) * piece, piece), piece)
    nears = (near_ref.at[0], mid_ref, near_ref.at[1])
    for d, near in enumerate(nears, start=1):
        far = far_ref.at[d - 1]
        fetches.append([
            pltpu.make_async_copy(near, weights.at[d, :, mine_rows], w_sem.at[2 * d]),
            pltpu.make_async_copy(far, weights.at[d, :, other_rows], w_sem.at[2 * d + 1]),
        ])
    for pair in fetches:
        for copy in pair:
            copy.start()

    def partial(d, cols):
        left = (gk_ref[...], gv_ref[...]) if d == 0 else (grads[d, 0], grads[d, 1])
        return dot_nt(left[0], weights[d, 0, cols, :]) + dot_nt(left[1], weights[d, 1, cols, :])

    step = 512
    for copy in fetches[0]:
        copy.wait()

    def own_part(n, carry):
        cols = pl.ds(pl.multiple_of(n * step, step), step)
        total[:, cols] = partial(0, cols)
        return carry

    lax.fori_loop(0, width // step, own_part, 0)

    for d in (1, 2, 3):
        for n, (da, db) in enumerate(((-d, 0), (0, -d))):
            at = hg_ref.at[turn(y, db, NY), turn(x, da, NX), core, rows[n]]
            units.landed(at, 2 * d - 2 + n, {"ctx": plane.at(da, db)})
    for d in (1, 2, 3):
        units.start(
            hg_ref.at[y, :, core, rows[0]], hg_ref.at[y, :, core, rows[0]], 4 + 2 * d, {"ctx": plane.at(0, d)}
        )
        units.start(
            hg_ref.at[:, x, core, rows[1]], hg_ref.at[:, x, core, rows[1]], 5 + 2 * d, {"ctx": plane.at(d, 0)}
        )

    for d in (1, 3):
        for n in range(2):
            sends.landed(grads.at[d, n], 2 * d - 2 + n, {"head": turn(me_z, -d, NZ)})
        for copy in fetches[d]:
            copy.wait()

        def next_part(n, carry):
            cols = pl.ds(pl.multiple_of(n * step, step), step)
            total[:, cols] += partial(d, cols)
            return carry

        lax.fori_loop(0, width // step, next_part, 0)

    for n in range(2):
        sends.landed(grads.at[2, n], 2 + n, {"head": turn(me_z, -2, NZ)})
    for copy in fetches[2]:
        copy.wait()
    outs = Copies(o_send, o_recv)
    quarter = half.shape[0] // NZ
    own_copies = []
    for n in range(width // step):
        cols = pl.ds(n * step, step)
        half[:, n * step:(n + 1) * step] = (total[:, n * step:(n + 1) * step] + partial(2, cols)).astype(jnp.bfloat16)
        out_cols = pl.ds(pl.multiple_of(me_z * width + n * step, step), step)
        for d in (1, 2, 3):
            to = turn(me_z, d, NZ)
            outs.start(
                half.at[pl.ds(pl.multiple_of(to * quarter, quarter), quarter), cols],
                gx_ref.at[:, out_cols], 4 * (d - 1) + n, {"head": to},
            )
        own = pltpu.make_async_copy(
            half.at[pl.ds(pl.multiple_of(me_z * quarter, quarter), quarter), cols],
            gx_ref.at[:, out_cols], own_sem.at[n],
        )
        own.start()
        own_copies.append(own)

    for d in (1, 2, 3):
        units.landed(
            hg_ref.at[turn(y, -d, NY), :, core, rows[0]], 4 + 2 * d, {"ctx": plane.at(0, -d)}
        )
        units.landed(
            hg_ref.at[:, turn(x, -d, NX), core, rows[1]], 5 + 2 * d, {"ctx": plane.at(-d, 0)}
        )
    sibling = {"ctx": plane.at(0, 0, True)}
    units.start(hg_ref.at[:, :, core], hg_ref.at[:, :, core], 12, sibling)
    units.landed(hg_ref.at[:, :, 1 - core], 12, sibling)

    for n in range(width // step):
        for d in (1, 2, 3):
            origin = turn(me_z, -d, NZ)
            out_cols = pl.ds(pl.multiple_of(origin * width + n * step, step), step)
            outs.landed(gx_ref.at[:, out_cols], 4 * (d - 1) + n, {"head": origin})
    sends.finish()
    outs.finish()
    units.finish()
    for copy in own_copies:
        copy.wait()


def project(gk, gv, hdq, w_key, w_value, near, mid, far):
    vmem = pl.BlockSpec(memory_space=pltpu.VMEM)
    hbm = pl.BlockSpec(memory_space=pl.ANY)
    blk = jnp.bfloat16
    depth = w_key.shape[0]
    width = depth // NZ
    return pl.pallas_call(
        project_kernel,
        out_shape=(
            jax.ShapeDtypeStruct((2 * CH // NZ, depth), blk),
            jax.ShapeDtypeStruct((NY, NX, 2, CH, HD), blk),
        ),
        in_specs=[vmem, vmem, vmem] + [hbm] * 5,
        out_specs=(vmem, vmem),
        scratch_shapes=[
            pltpu.VMEM((NZ, 2, 2 * CH, 2 * HD), blk),
            pltpu.VMEM((NZ, 2, width, 2 * HD), blk),
            pltpu.VMEM((2 * CH, width), jnp.float32),
            pltpu.VMEM((2 * CH, width), blk),
            pltpu.SemaphoreType.DMA((6,)),
            pltpu.SemaphoreType.DMA((6,)),
            pltpu.SemaphoreType.DMA((12,)),
            pltpu.SemaphoreType.DMA((12,)),
            pltpu.SemaphoreType.DMA((13,)),
            pltpu.SemaphoreType.DMA((13,)),
            pltpu.SemaphoreType.DMA((8,)),
            pltpu.SemaphoreType.DMA((5,)),
        ],
        compiler_params=pltpu.CompilerParams(
            collective_id=2, has_side_effects=True, vmem_limit_bytes=VMEM_MIB * MIB
        ),
        name="project",
    )(gk, gv, hdq, w_key, w_value, near, mid, far)


def finish_kernel(span_slot, gq_hbm, gqo_hbm, hg_hbm, gk_hbm, gv_hbm, gx_hbm, oq, ok, ov, ox, vq, vk, vv, vx, sems, head_sems):
    me = lax.axis_index("ctx")
    core = lax.rem(me, 2)
    ways = ((gx_hbm, vx, ox), (gk_hbm, vk, ok), (gv_hbm, vv, ov))
    loads = [pltpu.make_async_copy(src, mid, sems.at[n]) for n, (src, mid, _) in enumerate(ways)]
    for copy in loads:
        copy.start()
    for i in range(2):
        rows = pl.ds(i * CH, CH)
        dense = [span_slot[SPANS - 2 + s] == 2 * me + i for s in range(2)]
        light = jnp.logical_not(jnp.logical_or(dense[0], dense[1]))

        @pl.when(light)
        def _():
            pair = []
            for n, (src, which) in enumerate(((gq_hbm, core), (gqo_hbm, 1 - core))):
                cols = pl.ds(pl.multiple_of(which * GROUP * HD, GROUP * HD), GROUP * HD)
                pair.append(pltpu.make_async_copy(src.at[rows], vq.at[rows, cols], head_sems.at[n]))
                pair[-1].start()
            for copy in pair:
                copy.wait()

        for s in range(2):
            @pl.when(dense[s])
            def _():
                heads = []
                for h in range(2 * GROUP):
                    chip = s * GROUP + h % GROUP
                    heads.append(pltpu.make_async_copy(
                        hg_hbm.at[chip // NX, chip % NX, h // GROUP], vq.at[rows, pl.ds(h * HD, HD)], head_sems.at[h]
                    ))
                    heads[-1].start()
                for copy in heads:
                    copy.wait()

    stores = [pltpu.make_async_copy(vq, oq, sems.at[3])]
    stores[0].start()
    for n, (_, mid, dst) in enumerate(ways):
        loads[n].wait()
        stores.append(pltpu.make_async_copy(mid, dst, sems.at[n]))
        stores[-1].start()
    for copy in stores:
        copy.wait()


def finish(span_slot, gq, gqo, units, grad_k, grad_v, grad_x):
    anyspace = pl.BlockSpec(memory_space=pl.ANY)
    return pl.pallas_call(
        finish_kernel,
        out_shape=(
            jax.ShapeDtypeStruct((2 * CH, 2 * GROUP * HD), gq.dtype),
            jax.ShapeDtypeStruct(grad_k.shape, grad_k.dtype),
            jax.ShapeDtypeStruct(grad_v.shape, grad_v.dtype),
            jax.ShapeDtypeStruct(grad_x.shape, grad_x.dtype),
        ),
        in_specs=[pl.BlockSpec(memory_space=pltpu.SMEM)] + [anyspace] * 6,
        out_specs=(anyspace,) * 4,
        scratch_shapes=[
            pltpu.VMEM((2 * CH, 2 * GROUP * HD), gq.dtype),
            pltpu.VMEM(grad_k.shape, grad_k.dtype),
            pltpu.VMEM(grad_v.shape, grad_v.dtype),
            pltpu.VMEM(grad_x.shape, grad_x.dtype),
            pltpu.SemaphoreType.DMA((4,)),
            pltpu.SemaphoreType.DMA((2 * GROUP,)),
        ],
        compiler_params=pltpu.CompilerParams(vmem_limit_bytes=VMEM_MIB * MIB),
        name="finish",
    )(span_slot, gq, gqo, units, grad_k, grad_v, grad_x)


def per_device(queries, keys, values, d_out, w_key, w_value, pair_list, span_slot):
    me = lax.axis_index("ctx")
    own_slots = 2 * me + jnp.arange(2, dtype=jnp.int32)
    select = jnp.broadcast_to(
        (span_slot[SPANS - 2:, None, None] == own_slots[None, :, None]).astype(jnp.bfloat16), (2, 2, HD)
    )
    pair_rows = jnp.pad(pair_list.astype(jnp.bfloat16), ((0, 0), (0, HD - 2)))
    keys_pad = jnp.concatenate([keys, jnp.concatenate([pair_rows, pair_rows], axis=1)], axis=0)
    kg, vg, unit, qx, dox, near = gather_all(keys_pad, values, queries, d_out, select, w_key, w_value)
    kg = kg.reshape((NCTX,) + kg.shape[2:])
    vg = vg.reshape((NCTX,) + vg.shape[2:])
    gq, gqx, hdq, pk, pv = attend(span_slot, queries, d_out, qx, dox, kg, vg, unit)
    pk = pk.reshape((CHIPS, 2) + pk.shape[1:])
    pv = pv.reshape((CHIPS, 2) + pv.shape[1:])
    grad_k, grad_v, gqo, mid, far = scatter_sums(pk, pv, near, gqx, w_key, w_value)
    grad_x, units = project(grad_k, grad_v, hdq, w_key, w_value, near, mid, far)
    return finish(span_slot, gq, gqo, units, grad_k, grad_v, grad_x)


def solution(mesh):
    return jax.shard_map(
        per_device,
        mesh=mesh,
        in_specs=(
            P("ctx", "head"),
            P("ctx", "head"),
            P("ctx", "head"),
            P("ctx", "head"),
            P(None, "head"),
            P(None, "head"),
            P("ctx", None),
            P(),
        ),
        out_specs=(P("ctx", "head"), P("ctx", "head"), P("ctx", "head"), P(("ctx", "head"), None)),
        check_vma=False,
    )
```

```python
import functools

import jax
import jax.numpy as jnp
from jax import lax
from jax.experimental import pallas as pl
from jax.experimental.pallas import tpu as pltpu
from jax.sharding import PartitionSpec as P

MESH = pl.DeviceIdType.MESH
HD = 128
CH = 128
SPANS = 64
NX = 4
NY = 4
NZ = 4
NCTX = NX * NY * 2
CHIPS = NX * NY
GROUP = 8
PARTS = 2
WIDE = 4
NPAD = 16
SCALE = HD ** -0.5
EXP_SCALE = SCALE * 1.4426950408889634
neg_fill = -1e30
QB = 1024
MIB = 1024 * 1024
VMEM_MIB = 62


def ctx_coords():
    me = lax.axis_index("ctx")
    return me // (2 * NX), lax.rem(me // 2, NX), lax.rem(me, 2)


def ctx_id(y, x, core):
    return (y * NX + x) * 2 + core


def turn(pos, step, size):
    return lax.rem(pos + step + size, size)


class Plane:
    def __init__(self, first):
        self.y, self.x, self.core = ctx_coords()
        self.first = first

    def at(self, da, db, flip=False):
        dy, dx = (da, db) if self.first == "y" else (db, da)
        core = 1 - self.core if flip else self.core
        return ctx_id(turn(self.y, dy, NY), turn(self.x, dx, NX), core)

    def chip(self, da, db):
        dy, dx = (da, db) if self.first == "y" else (db, da)
        return turn(self.y, dy, NY) * NX + turn(self.x, dx, NX)


def barrier_with(targets):
    barrier = pltpu.get_barrier_semaphore()
    for device in targets:
        pl.semaphore_signal(barrier, inc=1, device_id=device, device_id_type=MESH)
    pl.semaphore_wait(barrier, len(targets))


def ctx_targets():
    plane = Plane("x")
    steps = [(1, 0), (2, 0), (3, 0), (0, 1), (0, 2), (0, 3)]
    return [{"ctx": plane.at(da, db)} for da, db in steps] + [{"ctx": plane.at(0, 0, True)}]


def head_targets(steps):
    me_z = lax.axis_index("head")
    return [{"head": turn(me_z, d, NZ)} for d in steps]


class Copies:
    def __init__(self, send, recv):
        self.send, self.recv, self.started = send, recv, []

    def start(self, src, dst, index, device):
        copy = pltpu.make_async_remote_copy(
            src_ref=src, dst_ref=dst, send_sem=self.send.at[index], recv_sem=self.recv.at[index],
            device_id=device, device_id_type=MESH,
        )
        copy.start()
        self.started.append(copy)

    def landed(self, dst, index, device):
        pltpu.make_async_remote_copy(
            src_ref=dst, dst_ref=dst, send_sem=self.send.at[index], recv_sem=self.recv.at[index],
            device_id=device, device_id_type=MESH,
        ).wait_recv()

    def finish(self):
        for copy in self.started:
            copy.wait_send()


DA_OF = (0, -1, 1, 2)


class Gather:
    def __init__(self, first, out, send, recv):
        self.plane = Plane(first)
        self.out = out
        self.copies = Copies(send, recv)

    def dev(self, da, db):
        return {"ctx": self.plane.at(da, db)}

    def region(self, da, db):
        return self.out.at[self.plane.chip(da, db)]

    def send(self, region, index, da, db):
        self.copies.start(region, region, index, self.dev(da, db))

    def begin_a(self):
        self.send(self.region(0, 0), 0, 1, 0)
        self.send(self.region(0, 0), 1, -1, 0)

    def spread(self, m):
        region = self.region(DA_OF[m], 0)
        self.send(region, 4 + 4 * m, 0, 1)
        self.send(region, 5 + 4 * m, 0, -1)

    def got_a(self, step):
        index = 0 if step < 0 else 1
        region = self.region(step, 0)
        self.copies.landed(region, index, self.dev(step, 0))
        self.send(region.at[index], 2 + index, -step, 0)

    def got_a_far(self):
        region = self.region(2, 0)
        self.copies.landed(region.at[0], 2, self.dev(-1, 0))
        self.copies.landed(region.at[1], 3, self.dev(1, 0))

    def got_b(self, m, step):
        index = 0 if step < 0 else 1
        region = self.region(DA_OF[m], step)
        self.copies.landed(region, 4 + 4 * m + index, self.dev(0, step))
        self.send(region.at[index], 6 + 4 * m + index, 0, -step)

    def got_b_far(self, m):
        region = self.region(DA_OF[m], 2)
        self.copies.landed(region.at[0], 6 + 4 * m, self.dev(0, -1))
        self.copies.landed(region.at[1], 7 + 4 * m, self.dev(0, 1))


def gather_kernel(
    span_slot, pairs_ref, keys_ref, values_ref, q_ref, do_ref, wk_hbm, wv_hbm,
    kg_ref, vg_ref, unit_ref, qx_ref, dox_ref, near_ref,
    keys_pad, give, held, from_core, first_in, mid, last_in,
    k_send, k_recv, v_send, v_recv, u_send, u_recv, w_send, w_recv, c_send, c_recv, own_sem,
):
    keys_pad[0:2 * CH, :] = keys_ref[...]
    for g in range(2):
        keys_pad[2 * CH:2 * CH + NPAD, g * HD:(g + 1) * HD] = pairs_ref[...]
    barrier_with(ctx_targets() + head_targets((1, 3)))
    y, x, core = ctx_coords()
    plane = Plane("x")
    chip = plane.chip(0, 0)
    sibling = {"ctx": plane.at(0, 0, True)}
    gathers = [
        Gather("x", kg_ref, k_send, k_recv),
        Gather("y", vg_ref, v_send, v_recv),
    ]

    def group_cols(which, width):
        return pl.ds(pl.multiple_of(which * width, width), width)

    cross = Copies(c_send, c_recv)
    other = group_cols(1 - core, HD)
    cross.start(keys_pad.at[:, other], kg_ref.at[chip, core], 0, sibling)
    cross.start(values_ref.at[:, other], vg_ref.at[chip, core], 1, sibling)
    mine = group_cols(core, HD)
    own_copies = [
        pltpu.make_async_copy(keys_pad.at[:, mine], kg_ref.at[chip, core], own_sem.at[0]),
        pltpu.make_async_copy(values_ref.at[:, mine], vg_ref.at[chip, core], own_sem.at[1]),
    ]
    for copy in own_copies:
        copy.start()

    def pick(dst, group):
        def unit(j, carry):
            cols = pl.ds(pl.multiple_of((group * GROUP + lax.rem(j, GROUP)) * HD, HD), HD)
            dense = span_slot[SPANS - 2 + j // GROUP]
            first, second = [
                jnp.full((1, HD), (dense == 4 * chip + 2 * core + i).astype(jnp.float32)).astype(jnp.bfloat16)
                for i in range(2)
            ]
            for n, ref in enumerate((q_ref, do_ref)):
                dst[n, j // NX, lax.rem(j, NX)] = ref[0:CH, cols] * first + ref[CH:2 * CH, cols] * second
            return carry

        lax.fori_loop(0, CHIPS, unit, 0)

    units = Copies(u_send, u_recv)
    pick(give, 1 - core)
    units.start(give, from_core, 0, sibling)

    for copy in own_copies:
        copy.wait()
    cross.landed(kg_ref.at[chip, 1 - core], 0, sibling)
    cross.landed(vg_ref.at[chip, 1 - core], 1, sibling)
    for gather in gathers:
        gather.begin_a()
    for gather in gathers:
        gather.spread(0)

    me_z = lax.axis_index("head")
    piece = near_ref.shape[2]
    moves = Copies(w_send, w_recv)
    for n, ref in enumerate((wk_hbm, wv_hbm)):
        for side, step in enumerate((1, -1)):
            to = turn(me_z, step, NZ)
            start = pl.multiple_of((2 * to + core) * piece, piece)
            moves.start(ref.at[pl.ds(start, piece)], near_ref.at[side, n], 2 * side + n, {"head": to})
    qcols = group_cols(1 - core, GROUP * HD)
    cross.start(q_ref.at[:, qcols], qx_ref, 2, sibling)
    cross.start(do_ref.at[:, qcols], dox_ref, 3, sibling)

    pick(held, core)
    units.landed(from_core, 0, sibling)

    def add_core(j, carry):
        for n in range(2):
            held[n, j // NX, lax.rem(j, NX)] += from_core[n, j // NX, lax.rem(j, NX)]
        return carry

    lax.fori_loop(0, CHIPS, add_core, 0)
    for d in (1, 2, 3):
        far_x, far_y = turn(x, d, NX), turn(y, d, NY)
        units.start(held.at[0, :, far_x], first_in.at[0, d - 1], d, {"ctx": plane.at(d, 0)})
        units.start(held.at[1, far_y], first_in.at[1, d - 1], 3 + d, {"ctx": plane.at(0, d)})

    for gather in gathers:
        gather.got_a(-1)
        gather.got_a(1)
    for gather in gathers:
        gather.spread(1)
        gather.spread(2)
    for gather in gathers:
        gather.got_b(0, -1)
        gather.got_b(0, 1)
    for gather in gathers:
        gather.got_a_far()
        gather.spread(3)

    for d in (1, 2, 3):
        units.landed(first_in.at[0, d - 1], d, {"ctx": plane.at(-d, 0)})
        units.landed(first_in.at[1, d - 1], 3 + d, {"ctx": plane.at(0, -d)})
    for n in range(4):
        mid[0, n] = held[0, n, x] + first_in[0, 0, n] + first_in[0, 1, n] + first_in[0, 2, n]
        mid[1, n] = held[1, y, n] + first_in[1, 0, n] + first_in[1, 1, n] + first_in[1, 2, n]
    for d in (1, 2, 3):
        units.start(mid.at[0, turn(y, d, NY)], last_in.at[0, d - 1], 6 + d, {"ctx": plane.at(0, d)})
        units.start(mid.at[1, turn(x, d, NX)], last_in.at[1, d - 1], 9 + d, {"ctx": plane.at(d, 0)})

    for m in (1, 2, 3):
        for gather in gathers:
            gather.got_b(m, -1)
            gather.got_b(m, 1)

    for d in (1, 2, 3):
        units.landed(last_in.at[0, d - 1], 6 + d, {"ctx": plane.at(0, -d)})
        units.landed(last_in.at[1, d - 1], 9 + d, {"ctx": plane.at(-d, 0)})
    unit_ref[0] = mid[0, y] + last_in[0, 0] + last_in[0, 1] + last_in[0, 2]
    unit_ref[1] = mid[1, x] + last_in[1, 0] + last_in[1, 1] + last_in[1, 2]

    cross.landed(qx_ref, 2, sibling)
    cross.landed(dox_ref, 3, sibling)
    for n in range(2):
        for side, step in enumerate((1, -1)):
            origin = {"head": turn(me_z, -step, NZ)}
            moves.landed(near_ref.at[side, n], 2 * side + n, origin)
    for m in range(4):
        for gather in gathers:
            gather.got_b_far(m)
    for gather in gathers:
        gather.copies.finish()
    cross.finish()
    units.finish()
    moves.finish()


def gather_all(span_slot, pair_rows, keys, values, queries, d_out, w_key, w_value):
    vmem = pl.BlockSpec(memory_space=pltpu.VMEM)
    anyspace = pl.BlockSpec(memory_space=pl.ANY)
    blk = jnp.bfloat16
    piece = w_key.shape[0] // NZ // 2
    return pl.pallas_call(
        gather_kernel,
        out_shape=(
            jax.ShapeDtypeStruct((CHIPS, 2, keys.shape[0] + NPAD, HD), blk),
            jax.ShapeDtypeStruct((CHIPS, 2, values.shape[0], HD), blk),
            jax.ShapeDtypeStruct((2, CH, HD), blk),
            jax.ShapeDtypeStruct((2 * CH, GROUP * HD), blk),
            jax.ShapeDtypeStruct((2 * CH, GROUP * HD), blk),
            jax.ShapeDtypeStruct((2, 2, piece) + w_key.shape[1:], blk),
        ),
        in_specs=[pl.BlockSpec(memory_space=pltpu.SMEM)] + [vmem] * 5 + [anyspace] * 2,
        out_specs=(anyspace, anyspace, vmem) + (anyspace,) * 3,
        scratch_shapes=[
            pltpu.VMEM((keys.shape[0] + NPAD, keys.shape[1]), blk),
            pltpu.VMEM((2, NY, NX, CH, HD), blk),
            pltpu.VMEM((2, NY, NX, CH, HD), blk),
            pltpu.VMEM((2, NY, NX, CH, HD), blk),
            pltpu.VMEM((2, 3, 4, CH, HD), blk),
            pltpu.VMEM((2, 4, CH, HD), blk),
            pltpu.VMEM((2, 3, CH, HD), blk),
            pltpu.SemaphoreType.DMA((20,)),
            pltpu.SemaphoreType.DMA((20,)),
            pltpu.SemaphoreType.DMA((20,)),
            pltpu.SemaphoreType.DMA((20,)),
            pltpu.SemaphoreType.DMA((13,)),
            pltpu.SemaphoreType.DMA((13,)),
            pltpu.SemaphoreType.DMA((8,)),
            pltpu.SemaphoreType.DMA((8,)),
            pltpu.SemaphoreType.DMA((4,)),
            pltpu.SemaphoreType.DMA((4,)),
            pltpu.SemaphoreType.DMA((2,)),
        ],
        compiler_params=pltpu.CompilerParams(
            collective_id=0, has_side_effects=True, vmem_limit_bytes=VMEM_MIB * MIB
        ),
        name="gather_kv",
    )(span_slot, pair_rows, keys, values, queries, d_out, w_key, w_value)


def dot_nt(a, b):
    return lax.dot_general(a, b, (((1,), (1,)), ((), ())), preferred_element_type=jnp.float32)


def dot_nn(a, b):
    return lax.dot_general(a, b, (((1,), (0,)), ((), ())), preferred_element_type=jnp.float32)


def dot_tn(a, b):
    return lax.dot_general(a, b, (((0,), (0,)), ((), ())), preferred_element_type=jnp.float32)


def attend_kernel(
    span_slot, q_hbm, do_hbm, qx_hbm, dox_hbm, kg_hbm, vg_hbm, unit_ref,
    gq_ref, gqx_ref, hdq_ref, pk_hbm, pv_hbm,
    kg, vg, qs, ds, gq_all, stage, probs, dprob, tops, stat, acck, accv, dqt, found, flags, slot_label, todo,
    flag_sem, qsems, load_sems, store_sems,
):
    me = lax.axis_index("ctx")
    core = lax.rem(me, 2)
    unit = me // 2
    quarter = NCTX // 4
    pair_copy = pltpu.make_async_copy(
        kg_hbm.at[:, pl.ds(2 * CH, NPAD)], kg.at[:, pl.ds(2 * CH, NPAD)], load_sems.at[4, 0]
    )
    pair_copy.start()
    loads = []
    for n in range(4):
        part = pl.ds(n * quarter, quarter)
        for side, (src, dst) in enumerate(((kg_hbm, kg), (vg_hbm, vg))):
            at = (part, pl.ds(0, 2 * CH))
            loads.append(pltpu.make_async_copy(src.at[at], dst.at[at], load_sems.at[n, side]))
            loads[-1].start()
    stacks = []
    for u in range(4):
        for r in range(GROUP):
            rows = pl.ds((u % 2) * CH, CH)
            own_cols = pl.ds(pl.multiple_of((core * GROUP + r) * HD, HD), HD)
            for n, (own, other, dst) in enumerate(((q_hbm, qx_hbm, qs), (do_hbm, dox_hbm, ds))):
                src = own.at[rows, own_cols] if u < 2 else other.at[rows, pl.ds(r * HD, HD)]
                stacks.append(pltpu.make_async_copy(src, dst.at[u, pl.ds(r * CH, CH)], qsems.at[n, u * GROUP + r]))
    for copy in stacks:
        copy.start()

    def name_slot(c, carry):
        slot_label[span_slot[c]] = c
        return carry

    lax.fori_loop(0, SPANS, name_slot, 0)

    def slot_of(u):
        return 2 * (2 * unit + lax.rem(core + u // 2, 2)) + lax.rem(u, 2)

    pair_copy.wait()
    pair_rows = kg[:, 2 * CH:2 * CH + NPAD, :].reshape(NCTX * NPAD, HD).astype(jnp.float32)
    lanes = lax.broadcasted_iota(jnp.int32, (1, HD), 1).astype(jnp.float32)
    for u in range(4):
        own = slot_label[slot_of(u)].astype(jnp.float32)
        hit = jnp.logical_and(pair_rows[:, 0:1] == own, pair_rows[:, 1:2] == lanes)
        found[u:u + 1, :] = jnp.max(jnp.where(hit, 1.0, 0.0), axis=0, keepdims=True).astype(jnp.int32)
    flag_copy = pltpu.make_async_copy(found, flags, flag_sem.at[0])
    flag_copy.start()

    label = SPANS - 2 + unit // GROUP
    q_unit = unit_ref[0]
    do_unit = unit_ref[1]

    steps = NCTX // WIDE

    def many(ref, t):
        return jnp.concatenate([ref[WIDE * t + u, 0:2 * CH, :] for u in range(WIDE)], axis=0)

    def unit_first(t, carry):
        top, total, mix = carry
        scores = dot_nt(many(kg, t), q_unit) * EXP_SCALE
        mixed = dot_nt(many(vg, t), do_unit)
        diff = lax.broadcasted_iota(jnp.int32, (CH, HD), 0) - lax.broadcasted_iota(jnp.int32, (CH, HD), 1)
        scores = jnp.concatenate([
            jnp.where(diff <= (label - slot_label[2 * WIDE * t + u]) * CH, scores[u * CH:(u + 1) * CH], neg_fill)
            for u in range(2 * WIDE)
        ], axis=0)
        new_top = jnp.maximum(top, jnp.max(scores, axis=0, keepdims=True))
        weights = jnp.exp2(scores - new_top)
        factor = jnp.exp2(top - new_top)
        probs[t] = weights
        dprob[t] = mixed
        tops[t] = new_top
        return (
            new_top,
            total * factor + jnp.sum(weights, axis=0, keepdims=True),
            mix * factor + jnp.sum(weights * mixed, axis=0, keepdims=True),
        )

    zero_row = jnp.zeros((1, HD), jnp.float32)
    state = (jnp.full((1, HD), neg_fill, jnp.float32), zero_row, zero_row)
    for n in range(4):
        for copy in loads[2 * n:2 * n + 2]:
            copy.wait()
        state = lax.fori_loop(n * steps // 4, (n + 1) * steps // 4, unit_first, state)
    top, total, mix = state
    over = 1.0 / total
    delta = mix * over

    def unit_second(t, acc):
        factor = jnp.exp2(tops[t] - top) * over
        weights = probs[t] * factor
        dscore = (weights * (dprob[t] - delta)).astype(jnp.bfloat16)
        value_part = dot_nn(weights.astype(jnp.bfloat16), do_unit)
        key_part = dot_nn(dscore, q_unit)
        for u in range(WIDE):
            accv[WIDE * t + u] = value_part[2 * u * CH:2 * (u + 1) * CH]
            acck[WIDE * t + u] = key_part[2 * u * CH:2 * (u + 1) * CH]
        return acc + dot_tn(many(kg, t), dscore)

    acc = lax.fori_loop(0, steps, unit_second, jnp.zeros((HD, CH), jnp.float32))
    hdq_ref[...] = (acc * SCALE).T.astype(jnp.bfloat16)

    flag_copy.wait()
    for copy in stacks:
        copy.wait()

    def span_work(u, carry):
        own_slot = slot_of(u)
        own_label = slot_label[own_slot]

        @pl.when(own_label < SPANS - 2)
        def _():
            todo[0] = own_slot

            def note(c, n):
                todo[n] = span_slot[c]
                wanted = jnp.logical_and(flags[u, c] > 0, c != own_label)
                return n + wanted.astype(jnp.int32)

            count = lax.fori_loop(0, SPANS, note, jnp.int32(1))
            todo[count] = own_slot

            def rows_at(slot):
                return pl.ds(pl.multiple_of(lax.rem(slot, 2) * CH, CH), CH)

            todo[count + 1] = own_slot

            def some(ref, base, size):
                slots = [todo[base + v] for v in range(size)]
                return jnp.concatenate([ref[slot // 2, rows_at(slot), :] for slot in slots], axis=0)

            def dots(base, size, masked):
                scores = dot_nt(some(kg, base, size), qs[u]) * EXP_SCALE
                if masked:
                    diff = lax.broadcasted_iota(jnp.int32, (CH, QB), 0) - lax.rem(
                        lax.broadcasted_iota(jnp.int32, (CH, QB), 1), CH
                    )
                    limits = [
                        jnp.where(base + v == 0, 0, jnp.where(base + v < count, CH, -CH)) for v in range(size)
                    ]
                    scores = jnp.concatenate([
                        jnp.where(diff <= limits[v], scores[v * CH:(v + 1) * CH], neg_fill) for v in range(size)
                    ], axis=0)
                return scores, dot_nt(some(vg, base, size), ds[u])

            def first(base, size, masked):
                scores, mixed = dots(base, size, masked)
                old_top = stat[0:1, :]
                new_top = jnp.maximum(old_top, jnp.max(scores, axis=0, keepdims=True))
                weights = jnp.exp2(scores - new_top)
                factor = jnp.exp2(old_top - new_top)
                stat[0:1, :] = new_top
                stat[1:2, :] = stat[1:2, :] * factor + jnp.sum(weights, axis=0, keepdims=True)
                stat[2:3, :] = stat[2:3, :] * factor + jnp.sum(weights * mixed, axis=0, keepdims=True)

            def second(base, size, masked):
                scores, mixed = dots(base, size, masked)
                weights = jnp.exp2(scores - stat[3:4, :])
                dscore = (weights * (mixed - stat[4:5, :])).astype(jnp.bfloat16)
                value_part = dot_nn(weights.astype(jnp.bfloat16), ds[u])
                key_part = dot_nn(dscore, qs[u])
                for v in range(size):
                    slot = todo[base + v]
                    accv[slot // 2, rows_at(slot), :] += value_part[v * CH:(v + 1) * CH]
                    acck[slot // 2, rows_at(slot), :] += key_part[v * CH:(v + 1) * CH]
                dqt[...] += dot_tn(some(kg, base, size), dscore)

            fours = (count + 1) // 4

            def sweep(work):
                def step(t, c):
                    masked = jnp.logical_or(t == 0, 4 * t + 4 > count)

                    @pl.when(masked)
                    def _():
                        work(4 * t, 4, True)

                    @pl.when(jnp.logical_not(masked))
                    def _():
                        work(4 * t, 4, False)

                    return c

                lax.fori_loop(0, fours, step, 0)

                @pl.when(4 * fours < count)
                def _():
                    work(4 * fours, 2, True)

            stat[0:1, :] = jnp.full((1, QB), neg_fill, jnp.float32)
            stat[1:3, :] = jnp.zeros((2, QB), jnp.float32)
            sweep(first)
            total_row = stat[1:2, :]
            stat[3:4, :] = stat[0:1, :] + jnp.log2(total_row)
            stat[4:5, :] = stat[2:3, :] / total_row
            dqt[...] = jnp.zeros_like(dqt)
            sweep(second)
            for r in range(GROUP):
                gq_all[pl.ds(pl.multiple_of(u * CH, CH), CH), r * HD:(r + 1) * HD] = (
                    (dqt[:, r * CH:(r + 1) * CH] * SCALE).T.astype(jnp.bfloat16)
                )

        return carry

    lax.fori_loop(0, 4, span_work, 0)

    stores = [
        pltpu.make_async_copy(gq_all.at[pl.ds(0, 2 * CH)], gq_ref, store_sems.at[4, 0]),
        pltpu.make_async_copy(gq_all.at[pl.ds(2 * CH, 2 * CH)], gqx_ref, store_sems.at[4, 1]),
    ]
    for copy in stores:
        copy.start()
    for n in range(4):
        part = pl.ds(n * quarter, quarter)

        def narrow(t, carry):
            for side, ref in enumerate((acck, accv)):
                rows = ref[t].astype(jnp.bfloat16).reshape(NZ, PARTS, 2 * CH // NZ // PARTS, HD)
                for m in range(PARTS):
                    stage[side, m, t] = rows[:, m]
            return carry

        lax.fori_loop(n * quarter, (n + 1) * quarter, narrow, 0)
        for side, dst in enumerate((pk_hbm, pv_hbm)):
            stores.append(
                pltpu.make_async_copy(stage.at[side, :, part], dst.at[:, part], store_sems.at[n, side])
            )
            stores[-1].start()
    for copy in stores:
        copy.wait()


def attend(span_slot, queries, d_out, qx, dox, kg, vg, unit):
    vmem = pl.BlockSpec(memory_space=pltpu.VMEM)
    smem = pl.BlockSpec(memory_space=pltpu.SMEM)
    anyspace = pl.BlockSpec(memory_space=pl.ANY)
    blk = jnp.bfloat16
    return pl.pallas_call(
        attend_kernel,
        out_shape=(
            jax.ShapeDtypeStruct((2 * CH, GROUP * HD), blk),
            jax.ShapeDtypeStruct((2 * CH, GROUP * HD), blk),
            jax.ShapeDtypeStruct((CH, HD), blk),
            jax.ShapeDtypeStruct((PARTS, NCTX, NZ, 2 * CH // NZ // PARTS, HD), blk),
            jax.ShapeDtypeStruct((PARTS, NCTX, NZ, 2 * CH // NZ // PARTS, HD), blk),
        ),
        in_specs=[smem] + [anyspace] * 6 + [vmem],
        out_specs=(anyspace, anyspace, vmem, anyspace, anyspace),
        scratch_shapes=[
            pltpu.VMEM(kg.shape, blk),
            pltpu.VMEM(vg.shape, blk),
            pltpu.VMEM((4, GROUP * CH, HD), blk),
            pltpu.VMEM((4, GROUP * CH, HD), blk),
            pltpu.VMEM((4 * CH, GROUP * HD), blk),
            pltpu.VMEM((2, PARTS, NCTX, NZ, 2 * CH // NZ // PARTS, HD), blk),
            pltpu.VMEM((NCTX // WIDE, 2 * WIDE * CH, HD), jnp.float32),
            pltpu.VMEM((NCTX // WIDE, 2 * WIDE * CH, HD), jnp.float32),
            pltpu.VMEM((NCTX // WIDE, 1, HD), jnp.float32),
            pltpu.VMEM((8, QB), jnp.float32),
            pltpu.VMEM((NCTX, 2 * CH, HD), jnp.float32),
            pltpu.VMEM((NCTX, 2 * CH, HD), jnp.float32),
            pltpu.VMEM((HD, QB), jnp.float32),
            pltpu.VMEM((8, HD), jnp.int32),
            pltpu.SMEM((8, HD), jnp.int32),
            pltpu.SMEM((SPANS,), jnp.int32),
            pltpu.SMEM((SPANS + 8,), jnp.int32),
            pltpu.SemaphoreType.DMA((1,)),
            pltpu.SemaphoreType.DMA((2, 32)),
            pltpu.SemaphoreType.DMA((5, 2)),
            pltpu.SemaphoreType.DMA((5, 2)),
        ],
        compiler_params=pltpu.CompilerParams(vmem_limit_bytes=VMEM_MIB * MIB),
        cost_estimate=pl.CostEstimate(flops=8 * 10**9, bytes_accessed=32 * 10**6, transcendentals=4 * 10**6),
        name="attend",
    )(span_slot, queries, d_out, qx, dox, kg, vg, unit)


def plus(a, b):
    return (a.astype(jnp.float32) + b.astype(jnp.float32)).astype(jnp.bfloat16)


class Scatter:
    def __init__(self, first, parts, own, near, full, near_b, full_b, send, recv, own_sem):
        self.plane = Plane(first)
        self.parts, self.own, self.own_sem = parts, own, own_sem
        self.near, self.full, self.near_b, self.full_b = near, full, near_b, full_b
        self.copies = Copies(send, recv)

    def dev(self, da, db):
        return {"ctx": self.plane.at(da, db)}

    def load(self, q, e):
        return pltpu.make_async_copy(self.parts.at[self.plane.chip(e, q)], self.own.at[q, e], self.own_sem.at[4 * q + e])

    def far(self, q):
        block = self.parts.at[self.plane.chip(2, q)]
        self.copies.start(block.at[0], self.near.at[q, 0], 4 * q, self.dev(1, 0))
        self.copies.start(block.at[1], self.near.at[q, 1], 4 * q + 1, self.dev(-1, 0))

    def next(self, q):
        for side, step in enumerate((1, -1)):
            e = step % 4
            self.load(q, e).wait()
            self.copies.landed(self.near.at[q, side], 4 * q + side, self.dev(-step, 0))
            self.own[q, e, side] = plus(self.own[q, e, side], self.near[q, side])
            self.copies.start(self.own.at[q, e], self.full.at[q, side], 4 * q + 2 + side, self.dev(step, 0))

    def last(self, q):
        self.load(q, 0).wait()
        self.copies.landed(self.full.at[q, 0], 4 * q + 2, self.dev(-1, 0))
        self.copies.landed(self.full.at[q, 1], 4 * q + 3, self.dev(1, 0))
        return (
            self.own[q, 0].astype(jnp.float32)
            + self.full[q, 0].astype(jnp.float32)
            + self.full[q, 1].astype(jnp.float32)
        )

    def last_far(self):
        self.own[2, 0] = self.last(2).astype(jnp.bfloat16)
        for side, step in enumerate((1, -1)):
            self.copies.start(self.own.at[2, 0, side], self.near_b.at[side], 16 + side, self.dev(0, step))

    def last_near(self, side):
        step = (1, -1)[side]
        q = step % 4
        total = self.last(q)
        self.copies.landed(self.near_b.at[side], 16 + side, self.dev(0, -step))
        self.own[q, 0, 1 - side] = total[1 - side].astype(jnp.bfloat16)
        self.own[q, 0, side] = (total[side] + self.near_b[side].astype(jnp.float32)).astype(jnp.bfloat16)
        self.copies.start(self.own.at[q, 0], self.full_b.at[side], 18 + side, self.dev(0, step))

    def finish(self):
        total = self.last(0)
        self.copies.landed(self.full_b.at[0], 18, self.dev(0, -1))
        self.copies.landed(self.full_b.at[1], 19, self.dev(0, 1))
        return total + self.full_b[0].astype(jnp.float32) + self.full_b[1].astype(jnp.float32)


def reduce_project_kernel(
    pk_ref, pv_ref, near_ref, gqx_ref, hdq_ref, wk_hbm, wv_hbm,
    gk_ref, gv_ref, gqo_ref, gx_ref, hg_ref,
    k_own, k_near, k_full, k_near_b, k_full_b,
    v_own, v_near, v_full, v_near_b, v_full_b,
    sums, swap, swap_in, grads, weights, total, half,
    k_send, k_recv, v_send, v_recv, w_send, w_recv, c_send, c_recv, g_send, g_recv, o_send, o_recv, h_send, h_recv,
    own_sems, w_sem, hg_sem, o_sem,
):
    barrier_with(ctx_targets() + head_targets((1, 2, 3)))
    me_z = lax.axis_index("head")
    y, x, core = ctx_coords()
    plane = Plane("x")
    sibling = {"ctx": plane.at(0, 0, True)}
    ways = [
        [
            Scatter("y", pk_ref.at[m], *(ref.at[m] for ref in (
                k_own, k_near, k_full, k_near_b, k_full_b, k_send, k_recv)), own_sems.at[m, 0]),
            Scatter("x", pv_ref.at[m], *(ref.at[m] for ref in (
                v_own, v_near, v_full, v_near_b, v_full_b, v_send, v_recv)), own_sems.at[m, 1]),
        ]
        for m in range(PARTS)
    ]
    order = (2, 1, 3, 0)

    def far(m):
        for q in order:
            for way in ways[m]:
                way.far(q)
        for e in (1, 3, 0):
            for q in order:
                for way in ways[m]:
                    way.load(q, e).start()

    def next_hop(m):
        for q in order:
            for way in ways[m]:
                way.next(q)

    def last_hop(m):
        for way in ways[m]:
            way.last_far()
        for side in range(2):
            for way in ways[m]:
                way.last_near(side)

    far(0)

    width = weights.shape[2]
    piece = width // 2
    moves = Copies(w_send, w_recv)
    two = turn(me_z, 2, NZ)
    start = pl.multiple_of((2 * two + core) * piece, piece)
    for n, ref in enumerate((wk_hbm, wv_hbm)):
        moves.start(
            ref.at[pl.ds(start, piece)], weights.at[2, n, pl.ds(pl.multiple_of(core * piece, piece), piece)], n,
            {"head": two},
        )
    mine_rows = pl.ds(pl.multiple_of(core * piece, piece), piece)
    other_rows = pl.ds(pl.multiple_of((1 - core) * piece, piece), piece)
    cross = Copies(c_send, c_recv)
    for side, d in enumerate((1, 3)):
        cross.start(near_ref.at[side], weights.at[d, :, mine_rows], side, sibling)
    cross.start(gqx_ref, gqo_ref, 2, sibling)
    wrows = pl.ds(pl.multiple_of(me_z * width, width), width)
    fetches = [
        pltpu.make_async_copy(wk_hbm.at[wrows], weights.at[0, 0], w_sem.at[0]),
        pltpu.make_async_copy(wv_hbm.at[wrows], weights.at[0, 1], w_sem.at[1]),
        pltpu.make_async_copy(near_ref.at[0], weights.at[1, :, mine_rows], w_sem.at[2]),
        pltpu.make_async_copy(near_ref.at[1], weights.at[3, :, mine_rows], w_sem.at[3]),
    ]
    for copy in fetches:
        copy.start()
    hg_copy = pltpu.make_async_copy(hdq_ref, hg_ref.at[y, x, core], hg_sem.at[0])
    hg_copy.start()

    rows_of_part = 2 * CH // NZ // PARTS
    sends = Copies(g_send, g_recv)
    outs = Copies(o_send, o_recv)
    own_outs = []

    def collect(m):
        for n, (way, factor) in enumerate(zip(ways[m], (SCALE, 1.0))):
            sums[...] = (way.finish() * factor).reshape(sums.shape)
            swap[m, n] = sums[1 - core].astype(jnp.bfloat16)
            cross.start(swap.at[m, n], swap_in.at[m, n], 4 + 2 * m + n, sibling)
            grads[m, 0, n, :, pl.ds(pl.multiple_of(core * HD, HD), HD)] = sums[core].astype(jnp.bfloat16)

    def share(m):
        for n, out in enumerate((gk_ref, gv_ref)):
            cross.landed(swap_in.at[m, n], 4 + 2 * m + n, sibling)
            grads[m, 0, n, :, pl.ds(pl.multiple_of((1 - core) * HD, HD), HD)] = swap_in[m, n]
        for d in (1, 3, 2):
            sends.start(grads.at[m, 0], grads.at[m, d], 3 * m + d - 1, {"head": turn(me_z, d, NZ)})
        for n, out in enumerate((gk_ref, gv_ref)):
            for h in range(NZ):
                at = (h * PARTS + m) * rows_of_part
                out[at:at + rows_of_part, :] = grads[m, 0, n, h * rows_of_part:(h + 1) * rows_of_part, :]

    step = 512

    def partial(m, d, cols):
        return dot_nt(grads[m, d, 0], weights[d, 0, cols, :]) + dot_nt(grads[m, d, 1], weights[d, 1, cols, :])

    def columns(n):
        return pl.ds(pl.multiple_of(n * step, step), step)

    def multiply(m, d):
        if d != 0:
            sends.landed(grads.at[m, d], 3 * m + d - 1, {"head": turn(me_z, -d, NZ)})

        def part(n, carry):
            if d == 0:
                total[m, :, columns(n)] = partial(m, d, columns(n))
            else:
                total[m, :, columns(n)] += partial(m, d, columns(n))
            return carry

        lax.fori_loop(0, width // step, part, 0)

    def deliver(m):
        sends.landed(grads.at[m, 2], 3 * m + 1, {"head": turn(me_z, -2, NZ)})
        rows_out = pl.ds(m * rows_of_part, rows_of_part)
        for n in range(width // step):
            cols = pl.ds(n * step, step)
            half[m, :, n * step:(n + 1) * step] = (
                total[m, :, n * step:(n + 1) * step] + partial(m, 2, cols)
            ).astype(jnp.bfloat16)
            out_cols = pl.ds(pl.multiple_of(me_z * width + n * step, step), step)

            def block(to):
                return half.at[m, pl.ds(pl.multiple_of(to * rows_of_part, rows_of_part), rows_of_part), cols]

            for d in (1, 3, 2):
                to = turn(me_z, d, NZ)
                outs.start(block(to), gx_ref.at[rows_out, out_cols], (m * 3 + d - 1) * 4 + n, {"head": to})
            own_outs.append(pltpu.make_async_copy(block(me_z), gx_ref.at[rows_out, out_cols], o_sem.at[m * 4 + n]))
            own_outs[-1].start()

    next_hop(0)
    far(1)
    last_hop(0)
    next_hop(1)
    collect(0)
    last_hop(1)
    share(0)

    for side, d in enumerate((1, 3)):
        cross.landed(weights.at[d, :, other_rows], side, sibling)
    for copy in fetches:
        copy.wait()
    multiply(0, 0)
    collect(1)
    share(1)

    units = Copies(h_send, h_recv)
    rows = [pl.ds(0, CH // 2), pl.ds(CH // 2, CH // 2)]
    hg_copy.wait()
    for d in (1, 2, 3):
        for n, (da, db) in enumerate(((d, 0), (0, d))):
            block = hg_ref.at[y, x, core, rows[n]]
            units.start(block, block, 2 * d - 2 + n, {"ctx": plane.at(da, db)})

    multiply(0, 1)
    multiply(0, 3)
    for n in range(2):
        moves.landed(weights.at[2, n, mine_rows], n, {"head": two})
    cross.start(weights.at[2, :, mine_rows], weights.at[2, :, mine_rows], 3, sibling)
    multiply(1, 0)
    cross.landed(weights.at[2, :, other_rows], 3, sibling)
    deliver(0)

    for d in (1, 2, 3):
        for n, (da, db) in enumerate(((-d, 0), (0, -d))):
            at = hg_ref.at[turn(y, db, NY), turn(x, da, NX), core, rows[n]]
            units.landed(at, 2 * d - 2 + n, {"ctx": plane.at(da, db)})
    for d in (1, 2, 3):
        block = hg_ref.at[y, :, core, rows[0]]
        units.start(block, block, 4 + 2 * d, {"ctx": plane.at(0, d)})
        block = hg_ref.at[:, x, core, rows[1]]
        units.start(block, block, 5 + 2 * d, {"ctx": plane.at(d, 0)})

    multiply(1, 1)
    multiply(1, 3)
    deliver(1)

    for d in (1, 2, 3):
        units.landed(hg_ref.at[turn(y, -d, NY), :, core, rows[0]], 4 + 2 * d, {"ctx": plane.at(0, -d)})
        units.landed(hg_ref.at[:, turn(x, -d, NX), core, rows[1]], 5 + 2 * d, {"ctx": plane.at(-d, 0)})
    units.start(hg_ref.at[:, :, core], hg_ref.at[:, :, core], 12, sibling)
    units.landed(hg_ref.at[:, :, 1 - core], 12, sibling)
    cross.landed(gqo_ref, 2, sibling)

    for m in range(PARTS):
        rows_out = pl.ds(m * rows_of_part, rows_of_part)
        for n in range(width // step):
            for d in (1, 3, 2):
                origin = turn(me_z, -d, NZ)
                out_cols = pl.ds(pl.multiple_of(origin * width + n * step, step), step)
                outs.landed(gx_ref.at[rows_out, out_cols], (m * 3 + d - 1) * 4 + n, {"head": origin})
    for m in range(PARTS):
        for way in ways[m]:
            way.copies.finish()
    for copies in (moves, cross, sends, outs, units):
        copies.finish()
    for copy in own_outs:
        copy.wait()


def reduce_project(pk, pv, near, gqx, hdq, w_key, w_value):
    vmem = pl.BlockSpec(memory_space=pltpu.VMEM)
    anyspace = pl.BlockSpec(memory_space=pl.ANY)
    blk = jnp.bfloat16
    depth = w_key.shape[0]
    width = depth // NZ
    rows = 2 * CH // PARTS
    block = (2, NZ, rows // NZ, HD)
    one = [
        pltpu.VMEM((PARTS, 4, 4) + block, blk),
        pltpu.VMEM((PARTS, 4) + block, blk),
        pltpu.VMEM((PARTS, 4, 2) + block, blk),
        pltpu.VMEM((PARTS,) + block, blk),
        pltpu.VMEM((PARTS, 2) + block, blk),
    ]

    def pair(*shape):
        return [pltpu.SemaphoreType.DMA(shape)] * 2

    return pl.pallas_call(
        reduce_project_kernel,
        out_shape=(
            jax.ShapeDtypeStruct((2 * CH, 2 * HD), blk),
            jax.ShapeDtypeStruct((2 * CH, 2 * HD), blk),
            jax.ShapeDtypeStruct(gqx.shape, blk),
            jax.ShapeDtypeStruct((2 * CH // NZ, depth), blk),
            jax.ShapeDtypeStruct((NY, NX, 2, CH, HD), blk),
        ),
        in_specs=[anyspace] * 4 + [vmem] + [anyspace] * 2,
        out_specs=(vmem, vmem, anyspace, vmem, vmem),
        scratch_shapes=one + one
        + [
            pltpu.VMEM((2, rows, HD), jnp.float32),
            pltpu.VMEM((PARTS, 2, rows, HD), blk),
            pltpu.VMEM((PARTS, 2, rows, HD), blk),
            pltpu.VMEM((PARTS, NZ, 2, rows, 2 * HD), blk),
            pltpu.VMEM((NZ, 2, width, 2 * HD), blk),
            pltpu.VMEM((PARTS, rows, width), jnp.float32),
            pltpu.VMEM((PARTS, rows, width), blk),
        ]
        + pair(PARTS, 20) + pair(PARTS, 20) + pair(2) + pair(8) + pair(6) + pair(24) + pair(13)
        + [
            pltpu.SemaphoreType.DMA((PARTS, 2, 16)),
            pltpu.SemaphoreType.DMA((4,)),
            pltpu.SemaphoreType.DMA((1,)),
            pltpu.SemaphoreType.DMA((8,)),
        ],
        compiler_params=pltpu.CompilerParams(
            collective_id=1, has_side_effects=True, vmem_limit_bytes=VMEM_MIB * MIB
        ),
        name="reduce_project",
    )(pk, pv, near, gqx, hdq, w_key, w_value)


def finish_kernel(span_slot, gq_hbm, gqo_hbm, hg_hbm, gk_hbm, gv_hbm, gx_hbm, oq, ok, ov, ox, vq, vk, vv, vx, sems, head_sems):
    me = lax.axis_index("ctx")
    core = lax.rem(me, 2)
    ways = ((gx_hbm, vx, ox), (gk_hbm, vk, ok), (gv_hbm, vv, ov))
    loads = [pltpu.make_async_copy(src, mid, sems.at[n]) for n, (src, mid, _) in enumerate(ways)]
    for copy in loads:
        copy.start()
    for i in range(2):
        rows = pl.ds(i * CH, CH)
        dense = [span_slot[SPANS - 2 + s] == 2 * me + i for s in range(2)]
        light = jnp.logical_not(jnp.logical_or(dense[0], dense[1]))

        @pl.when(light)
        def _():
            pair = []
            for n, (src, which) in enumerate(((gq_hbm, core), (gqo_hbm, 1 - core))):
                cols = pl.ds(pl.multiple_of(which * GROUP * HD, GROUP * HD), GROUP * HD)
                pair.append(pltpu.make_async_copy(src.at[rows], vq.at[rows, cols], head_sems.at[n]))
                pair[-1].start()
            for copy in pair:
                copy.wait()

        for s in range(2):
            @pl.when(dense[s])
            def _():
                heads = []
                for h in range(2 * GROUP):
                    chip = s * GROUP + h % GROUP
                    heads.append(pltpu.make_async_copy(
                        hg_hbm.at[chip // NX, chip % NX, h // GROUP], vq.at[rows, pl.ds(h * HD, HD)], head_sems.at[h]
                    ))
                    heads[-1].start()
                for copy in heads:
                    copy.wait()

    stores = [pltpu.make_async_copy(vq, oq, sems.at[3])]
    stores[0].start()
    for n, (_, mid, dst) in enumerate(ways):
        loads[n].wait()
        stores.append(pltpu.make_async_copy(mid, dst, sems.at[n]))
        stores[-1].start()
    for copy in stores:
        copy.wait()


def finish(span_slot, gq, gqo, units, grad_k, grad_v, grad_x):
    anyspace = pl.BlockSpec(memory_space=pl.ANY)
    return pl.pallas_call(
        finish_kernel,
        out_shape=(
            jax.ShapeDtypeStruct((2 * CH, 2 * GROUP * HD), gq.dtype),
            jax.ShapeDtypeStruct(grad_k.shape, grad_k.dtype),
            jax.ShapeDtypeStruct(grad_v.shape, grad_v.dtype),
            jax.ShapeDtypeStruct(grad_x.shape, grad_x.dtype),
        ),
        in_specs=[pl.BlockSpec(memory_space=pltpu.SMEM)] + [anyspace] * 6,
        out_specs=(anyspace,) * 4,
        scratch_shapes=[
            pltpu.VMEM((2 * CH, 2 * GROUP * HD), gq.dtype),
            pltpu.VMEM(grad_k.shape, grad_k.dtype),
            pltpu.VMEM(grad_v.shape, grad_v.dtype),
            pltpu.VMEM(grad_x.shape, grad_x.dtype),
            pltpu.SemaphoreType.DMA((4,)),
            pltpu.SemaphoreType.DMA((2 * GROUP,)),
        ],
        compiler_params=pltpu.CompilerParams(vmem_limit_bytes=VMEM_MIB * MIB),
        name="finish",
    )(span_slot, gq, gqo, units, grad_k, grad_v, grad_x)


def per_device(queries, keys, values, d_out, w_key, w_value, pair_list, span_slot):
    pair_rows = jnp.pad(pair_list.astype(jnp.bfloat16), ((0, 0), (0, HD - 2)))
    kg, vg, unit, qx, dox, near = gather_all(span_slot, pair_rows, keys, values, queries, d_out, w_key, w_value)
    kg = kg.reshape((NCTX,) + kg.shape[2:])
    vg = vg.reshape((NCTX,) + vg.shape[2:])
    gq, gqx, hdq, pk, pv = attend(span_slot, queries, d_out, qx, dox, kg, vg, unit)
    pk = pk.reshape((PARTS, CHIPS, 2) + pk.shape[2:])
    pv = pv.reshape((PARTS, CHIPS, 2) + pv.shape[2:])
    grad_k, grad_v, gqo, grad_x, units = reduce_project(pk, pv, near, gqx, hdq, w_key, w_value)
    return finish(span_slot, gq, gqo, units, grad_k, grad_v, grad_x)


def solution(mesh):
    return jax.shard_map(
        per_device,
        mesh=mesh,
        in_specs=(
            P("ctx", "head"),
            P("ctx", "head"),
            P("ctx", "head"),
            P("ctx", "head"),
            P(None, "head"),
            P(None, "head"),
            P("ctx", None),
            P(),
        ),
        out_specs=(P("ctx", "head"), P("ctx", "head"), P("ctx", "head"), P(("ctx", "head"), None)),
        check_vma=False,
    )
```

```python
import functools

import jax
import jax.numpy as jnp
from jax import lax
from jax.experimental import pallas as pl
from jax.experimental.pallas import tpu as pltpu
from jax.sharding import PartitionSpec as P

MESH = pl.DeviceIdType.MESH
HD = 128
CH = 128
SPANS = 64
NX = 4
NY = 4
NZ = 4
NCTX = NX * NY * 2
CHIPS = NX * NY
GROUP = 8
PARTS = 2
WIDE = 8
KEPT = 6
NPAD = 16
SCALE = HD ** -0.5
EXP_SCALE = SCALE * 1.4426950408889634
neg_fill = -1e30
QB = 1024
MIB = 1024 * 1024
VMEM_MIB = 62


def ctx_coords():
    me = lax.axis_index("ctx")
    return me // (2 * NX), lax.rem(me // 2, NX), lax.rem(me, 2)


def ctx_id(y, x, core):
    return (y * NX + x) * 2 + core


def turn(pos, step, size):
    return lax.rem(pos + step + size, size)


class Plane:
    def __init__(self, first):
        self.y, self.x, self.core = ctx_coords()
        self.first = first

    def at(self, da, db, flip=False):
        dy, dx = (da, db) if self.first == "y" else (db, da)
        core = 1 - self.core if flip else self.core
        return ctx_id(turn(self.y, dy, NY), turn(self.x, dx, NX), core)

    def chip(self, da, db):
        dy, dx = (da, db) if self.first == "y" else (db, da)
        return turn(self.y, dy, NY) * NX + turn(self.x, dx, NX)


def barrier_with(targets):
    barrier = pltpu.get_barrier_semaphore()
    for device in targets:
        pl.semaphore_signal(barrier, inc=1, device_id=device, device_id_type=MESH)
    pl.semaphore_wait(barrier, len(targets))


def ctx_targets():
    plane = Plane("x")
    steps = [(1, 0), (2, 0), (3, 0), (0, 1), (0, 2), (0, 3)]
    return [{"ctx": plane.at(da, db)} for da, db in steps] + [{"ctx": plane.at(0, 0, True)}]


def head_targets(steps):
    me_z = lax.axis_index("head")
    return [{"head": turn(me_z, d, NZ)} for d in steps]


class Copies:
    def __init__(self, send, recv):
        self.send, self.recv, self.started = send, recv, []

    def start(self, src, dst, index, device):
        copy = pltpu.make_async_remote_copy(
            src_ref=src, dst_ref=dst, send_sem=self.send.at[index], recv_sem=self.recv.at[index],
            device_id=device, device_id_type=MESH,
        )
        copy.start()
        self.started.append(copy)

    def landed(self, dst, index, device):
        pltpu.make_async_remote_copy(
            src_ref=dst, dst_ref=dst, send_sem=self.send.at[index], recv_sem=self.recv.at[index],
            device_id=device, device_id_type=MESH,
        ).wait_recv()

    def finish(self):
        for copy in self.started:
            copy.wait_send()


DA_OF = (0, -1, 1, 2)


class Gather:
    def __init__(self, first, out, send, recv):
        self.plane = Plane(first)
        self.out = out
        self.copies = Copies(send, recv)

    def dev(self, da, db):
        return {"ctx": self.plane.at(da, db)}

    def region(self, da, db):
        return self.out.at[self.plane.chip(da, db)]

    def send(self, region, index, da, db):
        self.copies.start(region, region, index, self.dev(da, db))

    def begin_a(self):
        self.send(self.region(0, 0), 0, 1, 0)
        self.send(self.region(0, 0), 1, -1, 0)

    def spread(self, m):
        region = self.region(DA_OF[m], 0)
        self.send(region, 4 + 4 * m, 0, 1)
        self.send(region, 5 + 4 * m, 0, -1)

    def got_a(self, step):
        index = 0 if step < 0 else 1
        region = self.region(step, 0)
        self.copies.landed(region, index, self.dev(step, 0))
        self.send(region.at[index], 2 + index, -step, 0)

    def got_a_far(self):
        region = self.region(2, 0)
        self.copies.landed(region.at[0], 2, self.dev(-1, 0))
        self.copies.landed(region.at[1], 3, self.dev(1, 0))

    def got_b(self, m, step):
        index = 0 if step < 0 else 1
        region = self.region(DA_OF[m], step)
        self.copies.landed(region, 4 + 4 * m + index, self.dev(0, step))
        self.send(region.at[index], 6 + 4 * m + index, 0, -step)

    def got_b_far(self, m):
        region = self.region(DA_OF[m], 2)
        self.copies.landed(region.at[0], 6 + 4 * m, self.dev(0, -1))
        self.copies.landed(region.at[1], 7 + 4 * m, self.dev(0, 1))


def gather_kernel(
    span_slot, pairs_ref, keys_ref, values_ref, q_ref, do_ref, wk_hbm, wv_hbm,
    kg_ref, vg_ref, unit_ref, qx_ref, dox_ref, near_ref,
    keys_pad, give, held, from_core, first_in, mid, last_in,
    k_send, k_recv, v_send, v_recv, u_send, u_recv, w_send, w_recv, c_send, c_recv, own_sem,
):
    keys_pad[0:2 * CH, :] = keys_ref[...]
    for g in range(2):
        keys_pad[2 * CH:2 * CH + NPAD, g * HD:(g + 1) * HD] = pairs_ref[...]
    barrier_with(ctx_targets() + head_targets((1, 3)))
    y, x, core = ctx_coords()
    plane = Plane("x")
    chip = plane.chip(0, 0)
    sibling = {"ctx": plane.at(0, 0, True)}
    gathers = [
        Gather("x", kg_ref, k_send, k_recv),
        Gather("y", vg_ref, v_send, v_recv),
    ]

    def group_cols(which, width):
        return pl.ds(pl.multiple_of(which * width, width), width)

    cross = Copies(c_send, c_recv)
    other = group_cols(1 - core, HD)
    cross.start(keys_pad.at[:, other], kg_ref.at[chip, core], 0, sibling)
    cross.start(values_ref.at[:, other], vg_ref.at[chip, core], 1, sibling)
    mine = group_cols(core, HD)
    own_copies = [
        pltpu.make_async_copy(keys_pad.at[:, mine], kg_ref.at[chip, core], own_sem.at[0]),
        pltpu.make_async_copy(values_ref.at[:, mine], vg_ref.at[chip, core], own_sem.at[1]),
    ]
    for copy in own_copies:
        copy.start()

    def pick(dst, group):
        def unit(j, carry):
            cols = pl.ds(pl.multiple_of((group * GROUP + lax.rem(j, GROUP)) * HD, HD), HD)
            dense = span_slot[SPANS - 2 + j // GROUP]
            first, second = [
                jnp.full((1, HD), (dense == 4 * chip + 2 * core + i).astype(jnp.float32)).astype(jnp.bfloat16)
                for i in range(2)
            ]
            for n, ref in enumerate((q_ref, do_ref)):
                dst[n, j // NX, lax.rem(j, NX)] = ref[0:CH, cols] * first + ref[CH:2 * CH, cols] * second
            return carry

        lax.fori_loop(0, CHIPS, unit, 0)

    units = Copies(u_send, u_recv)
    pick(give, 1 - core)
    units.start(give, from_core, 0, sibling)

    for copy in own_copies:
        copy.wait()
    cross.landed(kg_ref.at[chip, 1 - core], 0, sibling)
    cross.landed(vg_ref.at[chip, 1 - core], 1, sibling)
    for gather in gathers:
        gather.begin_a()
    for gather in gathers:
        gather.spread(0)

    me_z = lax.axis_index("head")
    piece = near_ref.shape[2]
    moves = Copies(w_send, w_recv)
    for n, ref in enumerate((wk_hbm, wv_hbm)):
        for side, step in enumerate((1, -1)):
            to = turn(me_z, step, NZ)
            start = pl.multiple_of((2 * to + core) * piece, piece)
            moves.start(ref.at[pl.ds(start, piece)], near_ref.at[side, n], 2 * side + n, {"head": to})
    qcols = group_cols(1 - core, GROUP * HD)
    cross.start(q_ref.at[:, qcols], qx_ref, 2, sibling)
    cross.start(do_ref.at[:, qcols], dox_ref, 3, sibling)

    pick(held, core)
    units.landed(from_core, 0, sibling)

    def add_core(j, carry):
        for n in range(2):
            held[n, j // NX, lax.rem(j, NX)] += from_core[n, j // NX, lax.rem(j, NX)]
        return carry

    lax.fori_loop(0, CHIPS, add_core, 0)
    for d in (1, 2, 3):
        far_x, far_y = turn(x, d, NX), turn(y, d, NY)
        units.start(held.at[0, :, far_x], first_in.at[0, d - 1], d, {"ctx": plane.at(d, 0)})
        units.start(held.at[1, far_y], first_in.at[1, d - 1], 3 + d, {"ctx": plane.at(0, d)})

    for gather in gathers:
        gather.got_a(-1)
        gather.got_a(1)
    for gather in gathers:
        gather.spread(1)
        gather.spread(2)
    for gather in gathers:
        gather.got_b(0, -1)
        gather.got_b(0, 1)
    for gather in gathers:
        gather.got_a_far()
        gather.spread(3)

    for d in (1, 2, 3):
        units.landed(first_in.at[0, d - 1], d, {"ctx": plane.at(-d, 0)})
        units.landed(first_in.at[1, d - 1], 3 + d, {"ctx": plane.at(0, -d)})
    for n in range(4):
        mid[0, n] = held[0, n, x] + first_in[0, 0, n] + first_in[0, 1, n] + first_in[0, 2, n]
        mid[1, n] = held[1, y, n] + first_in[1, 0, n] + first_in[1, 1, n] + first_in[1, 2, n]
    for d in (1, 2, 3):
        units.start(mid.at[0, turn(y, d, NY)], last_in.at[0, d - 1], 6 + d, {"ctx": plane.at(0, d)})
        units.start(mid.at[1, turn(x, d, NX)], last_in.at[1, d - 1], 9 + d, {"ctx": plane.at(d, 0)})

    for m in (1, 2, 3):
        for gather in gathers:
            gather.got_b(m, -1)
            gather.got_b(m, 1)

    for d in (1, 2, 3):
        units.landed(last_in.at[0, d - 1], 6 + d, {"ctx": plane.at(0, -d)})
        units.landed(last_in.at[1, d - 1], 9 + d, {"ctx": plane.at(-d, 0)})
    unit_ref[0] = mid[0, y] + last_in[0, 0] + last_in[0, 1] + last_in[0, 2]
    unit_ref[1] = mid[1, x] + last_in[1, 0] + last_in[1, 1] + last_in[1, 2]

    cross.landed(qx_ref, 2, sibling)
    cross.landed(dox_ref, 3, sibling)
    for n in range(2):
        for side, step in enumerate((1, -1)):
            origin = {"head": turn(me_z, -step, NZ)}
            moves.landed(near_ref.at[side, n], 2 * side + n, origin)
    for m in range(4):
        for gather in gathers:
            gather.got_b_far(m)
    for gather in gathers:
        gather.copies.finish()
    cross.finish()
    units.finish()
    moves.finish()


def gather_all(span_slot, pair_rows, keys, values, queries, d_out, w_key, w_value):
    vmem = pl.BlockSpec(memory_space=pltpu.VMEM)
    anyspace = pl.BlockSpec(memory_space=pl.ANY)
    blk = jnp.bfloat16
    piece = w_key.shape[0] // NZ // 2
    return pl.pallas_call(
        gather_kernel,
        out_shape=(
            jax.ShapeDtypeStruct((CHIPS, 2, keys.shape[0] + NPAD, HD), blk),
            jax.ShapeDtypeStruct((CHIPS, 2, values.shape[0], HD), blk),
            jax.ShapeDtypeStruct((2, CH, HD), blk),
            jax.ShapeDtypeStruct((2 * CH, GROUP * HD), blk),
            jax.ShapeDtypeStruct((2 * CH, GROUP * HD), blk),
            jax.ShapeDtypeStruct((2, 2, piece) + w_key.shape[1:], blk),
        ),
        in_specs=[pl.BlockSpec(memory_space=pltpu.SMEM)] + [vmem] * 5 + [anyspace] * 2,
        out_specs=(anyspace, anyspace, vmem) + (anyspace,) * 3,
        scratch_shapes=[
            pltpu.VMEM((keys.shape[0] + NPAD, keys.shape[1]), blk),
            pltpu.VMEM((2, NY, NX, CH, HD), blk),
            pltpu.VMEM((2, NY, NX, CH, HD), blk),
            pltpu.VMEM((2, NY, NX, CH, HD), blk),
            pltpu.VMEM((2, 3, 4, CH, HD), blk),
            pltpu.VMEM((2, 4, CH, HD), blk),
            pltpu.VMEM((2, 3, CH, HD), blk),
            pltpu.SemaphoreType.DMA((20,)),
            pltpu.SemaphoreType.DMA((20,)),
            pltpu.SemaphoreType.DMA((20,)),
            pltpu.SemaphoreType.DMA((20,)),
            pltpu.SemaphoreType.DMA((13,)),
            pltpu.SemaphoreType.DMA((13,)),
            pltpu.SemaphoreType.DMA((8,)),
            pltpu.SemaphoreType.DMA((8,)),
            pltpu.SemaphoreType.DMA((4,)),
            pltpu.SemaphoreType.DMA((4,)),
            pltpu.SemaphoreType.DMA((2,)),
        ],
        compiler_params=pltpu.CompilerParams(
            collective_id=0, has_side_effects=True, vmem_limit_bytes=VMEM_MIB * MIB
        ),
        name="gather_kv",
    )(span_slot, pair_rows, keys, values, queries, d_out, w_key, w_value)


def dot_nt(a, b):
    return lax.dot_general(a, b, (((1,), (1,)), ((), ())), preferred_element_type=jnp.float32)


def dot_nn(a, b):
    return lax.dot_general(a, b, (((1,), (0,)), ((), ())), preferred_element_type=jnp.float32)


def dot_tn(a, b):
    return lax.dot_general(a, b, (((0,), (0,)), ((), ())), preferred_element_type=jnp.float32)


def attend_kernel(
    span_slot, q_hbm, do_hbm, qx_hbm, dox_hbm, kg_hbm, vg_hbm, unit_ref,
    gq_ref, gqx_ref, hdq_ref, pk_hbm, pv_hbm,
    kg, vg, qs, ds, gq_all, stage, probs, dprob, tops, kept_probs, kept_dprob, kept_tops, stat, acck, accv, dqt, found, flags, slot_label, todo,
    flag_sem, qsems, load_sems, store_sems,
):
    me = lax.axis_index("ctx")
    core = lax.rem(me, 2)
    unit = me // 2
    quarter = NCTX // 4
    pair_copy = pltpu.make_async_copy(
        kg_hbm.at[:, pl.ds(2 * CH, NPAD)], kg.at[:, pl.ds(2 * CH, NPAD)], load_sems.at[4, 0]
    )
    pair_copy.start()
    loads = []
    for n in range(4):
        part = pl.ds(n * quarter, quarter)
        for side, (src, dst) in enumerate(((kg_hbm, kg), (vg_hbm, vg))):
            at = (part, pl.ds(0, 2 * CH))
            loads.append(pltpu.make_async_copy(src.at[at], dst.at[at], load_sems.at[n, side]))
            loads[-1].start()
    stacks = []
    for u in range(4):
        for r in range(GROUP):
            rows = pl.ds((u % 2) * CH, CH)
            own_cols = pl.ds(pl.multiple_of((core * GROUP + r) * HD, HD), HD)
            for n, (own, other, dst) in enumerate(((q_hbm, qx_hbm, qs), (do_hbm, dox_hbm, ds))):
                src = own.at[rows, own_cols] if u < 2 else other.at[rows, pl.ds(r * HD, HD)]
                stacks.append(pltpu.make_async_copy(src, dst.at[u, pl.ds(r * CH, CH)], qsems.at[n, u * GROUP + r]))
    for copy in stacks:
        copy.start()

    def name_slot(c, carry):
        slot_label[span_slot[c]] = c
        return carry

    lax.fori_loop(0, SPANS, name_slot, 0, unroll=8)

    def slot_of(u):
        return 2 * (2 * unit + lax.rem(core + u // 2, 2)) + lax.rem(u, 2)

    pair_copy.wait()
    pair_rows = kg[:, 2 * CH:2 * CH + NPAD, :].reshape(NCTX * NPAD, HD).astype(jnp.float32)
    lanes = lax.broadcasted_iota(jnp.int32, (1, HD), 1).astype(jnp.float32)
    for u in range(4):
        own = slot_label[slot_of(u)].astype(jnp.float32)
        hit = jnp.logical_and(pair_rows[:, 0:1] == own, pair_rows[:, 1:2] == lanes)
        found[u:u + 1, :] = jnp.max(jnp.where(hit, 1.0, 0.0), axis=0, keepdims=True).astype(jnp.int32)
    flag_copy = pltpu.make_async_copy(found, flags, flag_sem.at[0])
    flag_copy.start()

    label = SPANS - 2 + unit // GROUP
    q_unit = unit_ref[0]
    do_unit = unit_ref[1]

    steps = NCTX // WIDE

    def many(ref, t):
        return jnp.concatenate([ref[WIDE * t + u, 0:2 * CH, :] for u in range(WIDE)], axis=0)

    def unit_first(t, carry):
        top, total, mix = carry
        scores = dot_nt(many(kg, t), q_unit) * EXP_SCALE
        mixed = dot_nt(many(vg, t), do_unit)
        diff = lax.broadcasted_iota(jnp.int32, (CH, HD), 0) - lax.broadcasted_iota(jnp.int32, (CH, HD), 1)
        scores = jnp.concatenate([
            jnp.where(diff <= (label - slot_label[2 * WIDE * t + u]) * CH, scores[u * CH:(u + 1) * CH], neg_fill)
            for u in range(2 * WIDE)
        ], axis=0)
        new_top = jnp.maximum(top, jnp.max(scores, axis=0, keepdims=True))
        weights = jnp.exp2(scores - new_top)
        factor = jnp.exp2(top - new_top)
        probs[t] = weights
        dprob[t] = mixed
        tops[t] = new_top
        return (
            new_top,
            total * factor + jnp.sum(weights, axis=0, keepdims=True),
            mix * factor + jnp.sum(weights * mixed, axis=0, keepdims=True),
        )

    zero_row = jnp.zeros((1, HD), jnp.float32)
    state = (jnp.full((1, HD), neg_fill, jnp.float32), zero_row, zero_row)
    for n in range(4):
        for copy in loads[2 * n:2 * n + 2]:
            copy.wait()
        state = lax.fori_loop(n * steps // 4, (n + 1) * steps // 4, unit_first, state)
    top, total, mix = state
    over = 1.0 / total
    delta = mix * over

    def unit_second(t, acc):
        factor = jnp.exp2(tops[t] - top) * over
        weights = probs[t] * factor
        dscore = (weights * (dprob[t] - delta)).astype(jnp.bfloat16)
        value_part = dot_nn(weights.astype(jnp.bfloat16), do_unit)
        key_part = dot_nn(dscore, q_unit)
        for u in range(WIDE):
            accv[WIDE * t + u] = value_part[2 * u * CH:2 * (u + 1) * CH]
            acck[WIDE * t + u] = key_part[2 * u * CH:2 * (u + 1) * CH]
        return acc + dot_tn(many(kg, t), dscore)

    acc = lax.fori_loop(0, steps, unit_second, jnp.zeros((HD, CH), jnp.float32))
    hdq_ref[...] = (acc * SCALE).T.astype(jnp.bfloat16)

    flag_copy.wait()
    for copy in stacks:
        copy.wait()

    def span_work(u, carry):
        own_slot = slot_of(u)
        own_label = slot_label[own_slot]

        @pl.when(own_label < SPANS - 2)
        def _():
            todo[0] = own_slot

            def note(c, n):
                todo[n] = span_slot[c]
                wanted = jnp.logical_and(flags[u, c] > 0, c != own_label)
                return n + wanted.astype(jnp.int32)

            count = lax.fori_loop(0, SPANS, note, jnp.int32(1), unroll=8)
            todo[count] = own_slot

            def rows_at(slot):
                return pl.ds(pl.multiple_of(lax.rem(slot, 2) * CH, CH), CH)

            todo[count + 1] = own_slot

            def some(ref, base, size):
                slots = [todo[base + v] for v in range(size)]
                return jnp.concatenate([ref[slot // 2, rows_at(slot), :] for slot in slots], axis=0)

            def dots(base, size, masked):
                scores = dot_nt(some(kg, base, size), qs[u]) * EXP_SCALE
                if masked:
                    diff = lax.broadcasted_iota(jnp.int32, (CH, QB), 0) - lax.rem(
                        lax.broadcasted_iota(jnp.int32, (CH, QB), 1), CH
                    )
                    limits = [
                        jnp.where(base + v == 0, 0, jnp.where(base + v < count, CH, -CH)) for v in range(size)
                    ]
                    scores = jnp.concatenate([
                        jnp.where(diff <= limits[v], scores[v * CH:(v + 1) * CH], neg_fill) for v in range(size)
                    ], axis=0)
                return scores, dot_nt(some(vg, base, size), ds[u])

            def first(keep, base, size, masked):
                scores, mixed = dots(base, size, masked)
                old_top = stat[0:1, :]
                new_top = jnp.maximum(old_top, jnp.max(scores, axis=0, keepdims=True))
                weights = jnp.exp2(scores - new_top)
                factor = jnp.exp2(old_top - new_top)
                if keep:
                    kept_probs[base // 4, 0:size * CH, :] = weights
                    kept_dprob[base // 4, 0:size * CH, :] = mixed
                    kept_tops[base // 4] = new_top
                stat[0:1, :] = new_top
                stat[1:2, :] = stat[1:2, :] * factor + jnp.sum(weights, axis=0, keepdims=True)
                stat[2:3, :] = stat[2:3, :] * factor + jnp.sum(weights * mixed, axis=0, keepdims=True)

            def second(keep, base, size, masked):
                if keep:
                    weights = kept_probs[base // 4, 0:size * CH, :] * jnp.exp2(kept_tops[base // 4] - stat[3:4, :])
                    mixed = kept_dprob[base // 4, 0:size * CH, :]
                else:
                    scores, mixed = dots(base, size, masked)
                    weights = jnp.exp2(scores - stat[3:4, :])
                dscore = (weights * (mixed - stat[4:5, :])).astype(jnp.bfloat16)
                value_part = dot_nn(weights.astype(jnp.bfloat16), ds[u])
                key_part = dot_nn(dscore, qs[u])
                for v in range(size):
                    slot = todo[base + v]
                    accv[slot // 2, rows_at(slot), :] += value_part[v * CH:(v + 1) * CH]
                    acck[slot // 2, rows_at(slot), :] += key_part[v * CH:(v + 1) * CH]
                dqt[...] += dot_tn(some(kg, base, size), dscore)

            fours = (count + 1) // 4
            fits = (count + 3) // 4 <= KEPT

            def sweep(work, keep):
                def step(t, c):
                    masked = jnp.logical_or(t == 0, 4 * t + 4 > count)

                    @pl.when(masked)
                    def _():
                        work(keep, 4 * t, 4, True)

                    @pl.when(jnp.logical_not(masked))
                    def _():
                        work(keep, 4 * t, 4, False)

                    return c

                def plain(t, c):
                    work(keep, 4 * t, 4, False)
                    return c

                lax.fori_loop(0, fours, plain if keep and work is second else step, 0)

                @pl.when(4 * fours < count)
                def _():
                    work(keep, 4 * fours, 2, True)

            stat[0:1, :] = jnp.full((1, QB), neg_fill, jnp.float32)
            stat[1:3, :] = jnp.zeros((2, QB), jnp.float32)
            dqt[...] = jnp.zeros_like(dqt)

            def both_sweeps(keep):
                sweep(first, keep)
                total_row = stat[1:2, :]
                stat[3:4, :] = stat[0:1, :] + jnp.log2(total_row)
                stat[4:5, :] = stat[2:3, :] / total_row
                sweep(second, keep)

            @pl.when(fits)
            def _():
                both_sweeps(True)

            @pl.when(jnp.logical_not(fits))
            def _():
                both_sweeps(False)

            for r in range(GROUP):
                gq_all[pl.ds(pl.multiple_of(u * CH, CH), CH), r * HD:(r + 1) * HD] = (
                    (dqt[:, r * CH:(r + 1) * CH] * SCALE).T.astype(jnp.bfloat16)
                )

        return carry

    lax.fori_loop(0, 4, span_work, 0)

    stores = [
        pltpu.make_async_copy(gq_all.at[pl.ds(0, 2 * CH)], gq_ref, store_sems.at[4, 0]),
        pltpu.make_async_copy(gq_all.at[pl.ds(2 * CH, 2 * CH)], gqx_ref, store_sems.at[4, 1]),
    ]
    for copy in stores:
        copy.start()
    for n in range(4):
        part = pl.ds(n * quarter, quarter)

        def narrow(t, carry):
            for side, ref in enumerate((acck, accv)):
                rows = ref[t].astype(jnp.bfloat16).reshape(NZ, PARTS, 2 * CH // NZ // PARTS, HD)
                for m in range(PARTS):
                    stage[side, m, t] = rows[:, m]
            return carry

        lax.fori_loop(n * quarter, (n + 1) * quarter, narrow, 0)
        for side, dst in enumerate((pk_hbm, pv_hbm)):
            stores.append(
                pltpu.make_async_copy(stage.at[side, :, part], dst.at[:, part], store_sems.at[n, side])
            )
            stores[-1].start()
    for copy in stores:
        copy.wait()


def attend(span_slot, queries, d_out, qx, dox, kg, vg, unit):
    vmem = pl.BlockSpec(memory_space=pltpu.VMEM)
    smem = pl.BlockSpec(memory_space=pltpu.SMEM)
    anyspace = pl.BlockSpec(memory_space=pl.ANY)
    blk = jnp.bfloat16
    return pl.pallas_call(
        attend_kernel,
        out_shape=(
            jax.ShapeDtypeStruct((2 * CH, GROUP * HD), blk),
            jax.ShapeDtypeStruct((2 * CH, GROUP * HD), blk),
            jax.ShapeDtypeStruct((CH, HD), blk),
            jax.ShapeDtypeStruct((PARTS, NCTX, NZ, 2 * CH // NZ // PARTS, HD), blk),
            jax.ShapeDtypeStruct((PARTS, NCTX, NZ, 2 * CH // NZ // PARTS, HD), blk),
        ),
        in_specs=[smem] + [anyspace] * 6 + [vmem],
        out_specs=(anyspace, anyspace, vmem, anyspace, anyspace),
        scratch_shapes=[
            pltpu.VMEM(kg.shape, blk),
            pltpu.VMEM(vg.shape, blk),
            pltpu.VMEM((4, GROUP * CH, HD), blk),
            pltpu.VMEM((4, GROUP * CH, HD), blk),
            pltpu.VMEM((4 * CH, GROUP * HD), blk),
            pltpu.VMEM((2, PARTS, NCTX, NZ, 2 * CH // NZ // PARTS, HD), blk),
            pltpu.VMEM((NCTX // WIDE, 2 * WIDE * CH, HD), jnp.float32),
            pltpu.VMEM((NCTX // WIDE, 2 * WIDE * CH, HD), jnp.float32),
            pltpu.VMEM((NCTX // WIDE, 1, HD), jnp.float32),
            pltpu.VMEM((KEPT, 4 * CH, QB), jnp.float32),
            pltpu.VMEM((KEPT, 4 * CH, QB), jnp.float32),
            pltpu.VMEM((KEPT, 1, QB), jnp.float32),
            pltpu.VMEM((8, QB), jnp.float32),
            pltpu.VMEM((NCTX, 2 * CH, HD), jnp.float32),
            pltpu.VMEM((NCTX, 2 * CH, HD), jnp.float32),
            pltpu.VMEM((HD, QB), jnp.float32),
            pltpu.VMEM((8, HD), jnp.int32),
            pltpu.SMEM((8, HD), jnp.int32),
            pltpu.SMEM((SPANS,), jnp.int32),
            pltpu.SMEM((SPANS + 8,), jnp.int32),
            pltpu.SemaphoreType.DMA((1,)),
            pltpu.SemaphoreType.DMA((2, 32)),
            pltpu.SemaphoreType.DMA((5, 2)),
            pltpu.SemaphoreType.DMA((5, 2)),
        ],
        compiler_params=pltpu.CompilerParams(vmem_limit_bytes=VMEM_MIB * MIB),
        cost_estimate=pl.CostEstimate(flops=8 * 10**9, bytes_accessed=32 * 10**6, transcendentals=4 * 10**6),
        name="attend",
    )(span_slot, queries, d_out, qx, dox, kg, vg, unit)


def plus(a, b):
    return (a.astype(jnp.float32) + b.astype(jnp.float32)).astype(jnp.bfloat16)


class Scatter:
    def __init__(self, first, parts, own, near, full, near_b, full_b, send, recv, own_sem):
        self.plane = Plane(first)
        self.parts, self.own, self.own_sem = parts, own, own_sem
        self.near, self.full, self.near_b, self.full_b = near, full, near_b, full_b
        self.copies = Copies(send, recv)

    def dev(self, da, db):
        return {"ctx": self.plane.at(da, db)}

    def load(self, q, e):
        return pltpu.make_async_copy(self.parts.at[self.plane.chip(e, q)], self.own.at[q, e], self.own_sem.at[4 * q + e])

    def far(self, q):
        block = self.parts.at[self.plane.chip(2, q)]
        self.copies.start(block.at[0], self.near.at[q, 0], 4 * q, self.dev(1, 0))
        self.copies.start(block.at[1], self.near.at[q, 1], 4 * q + 1, self.dev(-1, 0))

    def next(self, q):
        for side, step in enumerate((1, -1)):
            e = step % 4
            self.load(q, e).wait()
            self.copies.landed(self.near.at[q, side], 4 * q + side, self.dev(-step, 0))
            self.own[q, e, side] = plus(self.own[q, e, side], self.near[q, side])
            self.copies.start(self.own.at[q, e], self.full.at[q, side], 4 * q + 2 + side, self.dev(step, 0))

    def last(self, q):
        self.load(q, 0).wait()
        self.copies.landed(self.full.at[q, 0], 4 * q + 2, self.dev(-1, 0))
        self.copies.landed(self.full.at[q, 1], 4 * q + 3, self.dev(1, 0))
        return (
            self.own[q, 0].astype(jnp.float32)
            + self.full[q, 0].astype(jnp.float32)
            + self.full[q, 1].astype(jnp.float32)
        )

    def last_far(self):
        self.own[2, 0] = self.last(2).astype(jnp.bfloat16)
        for side, step in enumerate((1, -1)):
            self.copies.start(self.own.at[2, 0, side], self.near_b.at[side], 16 + side, self.dev(0, step))

    def last_near(self, side):
        step = (1, -1)[side]
        q = step % 4
        total = self.last(q)
        self.copies.landed(self.near_b.at[side], 16 + side, self.dev(0, -step))
        self.own[q, 0, 1 - side] = total[1 - side].astype(jnp.bfloat16)
        self.own[q, 0, side] = (total[side] + self.near_b[side].astype(jnp.float32)).astype(jnp.bfloat16)
        self.copies.start(self.own.at[q, 0], self.full_b.at[side], 18 + side, self.dev(0, step))

    def finish(self):
        total = self.last(0)
        self.copies.landed(self.full_b.at[0], 18, self.dev(0, -1))
        self.copies.landed(self.full_b.at[1], 19, self.dev(0, 1))
        return total + self.full_b[0].astype(jnp.float32) + self.full_b[1].astype(jnp.float32)


def reduce_project_kernel(
    pk_ref, pv_ref, near_ref, gqx_ref, hdq_ref, wk_hbm, wv_hbm,
    gk_ref, gv_ref, gqo_ref, gx_ref, hg_ref,
    k_own, k_near, k_full, k_near_b, k_full_b,
    v_own, v_near, v_full, v_near_b, v_full_b,
    sums, swap, swap_in, grads, weights, total, half,
    k_send, k_recv, v_send, v_recv, w_send, w_recv, c_send, c_recv, g_send, g_recv, o_send, o_recv, h_send, h_recv,
    own_sems, w_sem, hg_sem, o_sem,
):
    barrier_with(ctx_targets() + head_targets((1, 2, 3)))
    me_z = lax.axis_index("head")
    y, x, core = ctx_coords()
    plane = Plane("x")
    sibling = {"ctx": plane.at(0, 0, True)}
    ways = [
        [
            Scatter("y", pk_ref.at[m], *(ref.at[m] for ref in (
                k_own, k_near, k_full, k_near_b, k_full_b, k_send, k_recv)), own_sems.at[m, 0]),
            Scatter("x", pv_ref.at[m], *(ref.at[m] for ref in (
                v_own, v_near, v_full, v_near_b, v_full_b, v_send, v_recv)), own_sems.at[m, 1]),
        ]
        for m in range(PARTS)
    ]
    order = (2, 1, 3, 0)

    def far(m):
        for q in order:
            for way in ways[m]:
                way.far(q)
        for e in (1, 3, 0):
            for q in order:
                for way in ways[m]:
                    way.load(q, e).start()

    def next_hop(m):
        for q in order:
            for way in ways[m]:
                way.next(q)

    def last_hop(m):
        for way in ways[m]:
            way.last_far()
        for side in range(2):
            for way in ways[m]:
                way.last_near(side)

    far(0)

    width = weights.shape[2]
    piece = width // 2
    moves = Copies(w_send, w_recv)
    two = turn(me_z, 2, NZ)
    start = pl.multiple_of((2 * two + core) * piece, piece)
    for n, ref in enumerate((wk_hbm, wv_hbm)):
        moves.start(
            ref.at[pl.ds(start, piece)], weights.at[2, n, pl.ds(pl.multiple_of(core * piece, piece), piece)], n,
            {"head": two},
        )
    mine_rows = pl.ds(pl.multiple_of(core * piece, piece), piece)
    other_rows = pl.ds(pl.multiple_of((1 - core) * piece, piece), piece)
    cross = Copies(c_send, c_recv)
    for side, d in enumerate((1, 3)):
        cross.start(near_ref.at[side], weights.at[d, :, mine_rows], side, sibling)
    cross.start(gqx_ref, gqo_ref, 2, sibling)
    wrows = pl.ds(pl.multiple_of(me_z * width, width), width)
    fetches = [
        pltpu.make_async_copy(wk_hbm.at[wrows], weights.at[0, 0], w_sem.at[0]),
        pltpu.make_async_copy(wv_hbm.at[wrows], weights.at[0, 1], w_sem.at[1]),
        pltpu.make_async_copy(near_ref.at[0], weights.at[1, :, mine_rows], w_sem.at[2]),
        pltpu.make_async_copy(near_ref.at[1], weights.at[3, :, mine_rows], w_sem.at[3]),
    ]
    for copy in fetches:
        copy.start()
    hg_copy = pltpu.make_async_copy(hdq_ref, hg_ref.at[y, x, core], hg_sem.at[0])
    hg_copy.start()

    rows_of_part = 2 * CH // NZ // PARTS
    sends = Copies(g_send, g_recv)
    outs = Copies(o_send, o_recv)
    own_outs = []

    def collect(m):
        for n, (way, factor) in enumerate(zip(ways[m], (SCALE, 1.0))):
            sums[...] = (way.finish() * factor).reshape(sums.shape)
            swap[m, n] = sums[1 - core].astype(jnp.bfloat16)
            cross.start(swap.at[m, n], swap_in.at[m, n], 4 + 2 * m + n, sibling)
            grads[m, 0, n, :, pl.ds(pl.multiple_of(core * HD, HD), HD)] = sums[core].astype(jnp.bfloat16)

    def share(m):
        for n, out in enumerate((gk_ref, gv_ref)):
            cross.landed(swap_in.at[m, n], 4 + 2 * m + n, sibling)
            grads[m, 0, n, :, pl.ds(pl.multiple_of((1 - core) * HD, HD), HD)] = swap_in[m, n]
        for d in (1, 3, 2):
            sends.start(grads.at[m, 0], grads.at[m, d], 3 * m + d - 1, {"head": turn(me_z, d, NZ)})
        for n, out in enumerate((gk_ref, gv_ref)):
            for h in range(NZ):
                at = (h * PARTS + m) * rows_of_part
                out[at:at + rows_of_part, :] = grads[m, 0, n, h * rows_of_part:(h + 1) * rows_of_part, :]

    step = 512

    def partial(m, d, cols):
        return dot_nt(grads[m, d, 0], weights[d, 0, cols, :]) + dot_nt(grads[m, d, 1], weights[d, 1, cols, :])

    def columns(n):
        return pl.ds(pl.multiple_of(n * step, step), step)

    def multiply(m, d):
        if d != 0:
            sends.landed(grads.at[m, d], 3 * m + d - 1, {"head": turn(me_z, -d, NZ)})

        def part(n, carry):
            if d == 0:
                total[m, :, columns(n)] = partial(m, d, columns(n))
            else:
                total[m, :, columns(n)] += partial(m, d, columns(n))
            return carry

        lax.fori_loop(0, width // step, part, 0)

    def deliver(m):
        sends.landed(grads.at[m, 2], 3 * m + 1, {"head": turn(me_z, -2, NZ)})
        rows_out = pl.ds(m * rows_of_part, rows_of_part)
        for n in range(width // step):
            cols = pl.ds(n * step, step)
            half[m, :, n * step:(n + 1) * step] = (
                total[m, :, n * step:(n + 1) * step] + partial(m, 2, cols)
            ).astype(jnp.bfloat16)
            out_cols = pl.ds(pl.multiple_of(me_z * width + n * step, step), step)

            def block(to):
                return half.at[m, pl.ds(pl.multiple_of(to * rows_of_part, rows_of_part), rows_of_part), cols]

            for d in (1, 3, 2):
                to = turn(me_z, d, NZ)
                outs.start(block(to), gx_ref.at[rows_out, out_cols], (m * 3 + d - 1) * 4 + n, {"head": to})
            own_outs.append(pltpu.make_async_copy(block(me_z), gx_ref.at[rows_out, out_cols], o_sem.at[m * 4 + n]))
            own_outs[-1].start()

    next_hop(0)
    far(1)
    last_hop(0)
    next_hop(1)
    collect(0)
    last_hop(1)
    share(0)

    for side, d in enumerate((1, 3)):
        cross.landed(weights.at[d, :, other_rows], side, sibling)
    for copy in fetches:
        copy.wait()
    multiply(0, 0)
    collect(1)
    share(1)

    units = Copies(h_send, h_recv)
    rows = [pl.ds(0, CH // 2), pl.ds(CH // 2, CH // 2)]
    hg_copy.wait()
    for d in (1, 2, 3):
        for n, (da, db) in enumerate(((d, 0), (0, d))):
            block = hg_ref.at[y, x, core, rows[n]]
            units.start(block, block, 2 * d - 2 + n, {"ctx": plane.at(da, db)})

    multiply(0, 1)
    multiply(0, 3)
    for n in range(2):
        moves.landed(weights.at[2, n, mine_rows], n, {"head": two})
    cross.start(weights.at[2, :, mine_rows], weights.at[2, :, mine_rows], 3, sibling)
    multiply(1, 0)
    cross.landed(weights.at[2, :, other_rows], 3, sibling)
    deliver(0)

    for d in (1, 2, 3):
        for n, (da, db) in enumerate(((-d, 0), (0, -d))):
            at = hg_ref.at[turn(y, db, NY), turn(x, da, NX), core, rows[n]]
            units.landed(at, 2 * d - 2 + n, {"ctx": plane.at(da, db)})
    for d in (1, 2, 3):
        block = hg_ref.at[y, :, core, rows[0]]
        units.start(block, block, 4 + 2 * d, {"ctx": plane.at(0, d)})
        block = hg_ref.at[:, x, core, rows[1]]
        units.start(block, block, 5 + 2 * d, {"ctx": plane.at(d, 0)})

    multiply(1, 1)
    multiply(1, 3)
    deliver(1)

    for d in (1, 2, 3):
        units.landed(hg_ref.at[turn(y, -d, NY), :, core, rows[0]], 4 + 2 * d, {"ctx": plane.at(0, -d)})
        units.landed(hg_ref.at[:, turn(x, -d, NX), core, rows[1]], 5 + 2 * d, {"ctx": plane.at(-d, 0)})
    units.start(hg_ref.at[:, :, core], hg_ref.at[:, :, core], 12, sibling)
    units.landed(hg_ref.at[:, :, 1 - core], 12, sibling)
    cross.landed(gqo_ref, 2, sibling)

    for m in range(PARTS):
        rows_out = pl.ds(m * rows_of_part, rows_of_part)
        for n in range(width // step):
            for d in (1, 3, 2):
                origin = turn(me_z, -d, NZ)
                out_cols = pl.ds(pl.multiple_of(origin * width + n * step, step), step)
                outs.landed(gx_ref.at[rows_out, out_cols], (m * 3 + d - 1) * 4 + n, {"head": origin})
    for m in range(PARTS):
        for way in ways[m]:
            way.copies.finish()
    for copies in (moves, cross, sends, outs, units):
        copies.finish()
    for copy in own_outs:
        copy.wait()


def reduce_project(pk, pv, near, gqx, hdq, w_key, w_value):
    vmem = pl.BlockSpec(memory_space=pltpu.VMEM)
    anyspace = pl.BlockSpec(memory_space=pl.ANY)
    blk = jnp.bfloat16
    depth = w_key.shape[0]
    width = depth // NZ
    rows = 2 * CH // PARTS
    block = (2, NZ, rows // NZ, HD)
    one = [
        pltpu.VMEM((PARTS, 4, 4) + block, blk),
        pltpu.VMEM((PARTS, 4) + block, blk),
        pltpu.VMEM((PARTS, 4, 2) + block, blk),
        pltpu.VMEM((PARTS,) + block, blk),
        pltpu.VMEM((PARTS, 2) + block, blk),
    ]

    def pair(*shape):
        return [pltpu.SemaphoreType.DMA(shape)] * 2

    return pl.pallas_call(
        reduce_project_kernel,
        out_shape=(
            jax.ShapeDtypeStruct((2 * CH, 2 * HD), blk),
            jax.ShapeDtypeStruct((2 * CH, 2 * HD), blk),
            jax.ShapeDtypeStruct(gqx.shape, blk),
            jax.ShapeDtypeStruct((2 * CH // NZ, depth), blk),
            jax.ShapeDtypeStruct((NY, NX, 2, CH, HD), blk),
        ),
        in_specs=[anyspace] * 4 + [vmem] + [anyspace] * 2,
        out_specs=(vmem, vmem, anyspace, vmem, vmem),
        scratch_shapes=one + one
        + [
            pltpu.VMEM((2, rows, HD), jnp.float32),
            pltpu.VMEM((PARTS, 2, rows, HD), blk),
            pltpu.VMEM((PARTS, 2, rows, HD), blk),
            pltpu.VMEM((PARTS, NZ, 2, rows, 2 * HD), blk),
            pltpu.VMEM((NZ, 2, width, 2 * HD), blk),
            pltpu.VMEM((PARTS, rows, width), jnp.float32),
            pltpu.VMEM((PARTS, rows, width), blk),
        ]
        + pair(PARTS, 20) + pair(PARTS, 20) + pair(2) + pair(8) + pair(6) + pair(24) + pair(13)
        + [
            pltpu.SemaphoreType.DMA((PARTS, 2, 16)),
            pltpu.SemaphoreType.DMA((4,)),
            pltpu.SemaphoreType.DMA((1,)),
            pltpu.SemaphoreType.DMA((8,)),
        ],
        compiler_params=pltpu.CompilerParams(
            collective_id=1, has_side_effects=True, vmem_limit_bytes=VMEM_MIB * MIB
        ),
        name="reduce_project",
    )(pk, pv, near, gqx, hdq, w_key, w_value)


def finish_kernel(span_slot, gq_hbm, gqo_hbm, hg_hbm, gk_hbm, gv_hbm, gx_hbm, oq, ok, ov, ox, vq, vk, vv, vx, sems, head_sems):
    me = lax.axis_index("ctx")
    core = lax.rem(me, 2)
    ways = ((gx_hbm, vx, ox), (gk_hbm, vk, ok), (gv_hbm, vv, ov))
    loads = [pltpu.make_async_copy(src, mid, sems.at[n]) for n, (src, mid, _) in enumerate(ways)]
    for copy in loads:
        copy.start()
    for i in range(2):
        rows = pl.ds(i * CH, CH)
        dense = [span_slot[SPANS - 2 + s] == 2 * me + i for s in range(2)]
        light = jnp.logical_not(jnp.logical_or(dense[0], dense[1]))

        @pl.when(light)
        def _():
            pair = []
            for n, (src, which) in enumerate(((gq_hbm, core), (gqo_hbm, 1 - core))):
                cols = pl.ds(pl.multiple_of(which * GROUP * HD, GROUP * HD), GROUP * HD)
                pair.append(pltpu.make_async_copy(src.at[rows], vq.at[rows, cols], head_sems.at[n]))
                pair[-1].start()
            for copy in pair:
                copy.wait()

        for s in range(2):
            @pl.when(dense[s])
            def _():
                heads = []
                for h in range(2 * GROUP):
                    chip = s * GROUP + h % GROUP
                    heads.append(pltpu.make_async_copy(
                        hg_hbm.at[chip // NX, chip % NX, h // GROUP], vq.at[rows, pl.ds(h * HD, HD)], head_sems.at[h]
                    ))
                    heads[-1].start()
                for copy in heads:
                    copy.wait()

    stores = [pltpu.make_async_copy(vq, oq, sems.at[3])]
    stores[0].start()
    for n, (_, mid, dst) in enumerate(ways):
        loads[n].wait()
        stores.append(pltpu.make_async_copy(mid, dst, sems.at[n]))
        stores[-1].start()
    for copy in stores:
        copy.wait()


def finish(span_slot, gq, gqo, units, grad_k, grad_v, grad_x):
    anyspace = pl.BlockSpec(memory_space=pl.ANY)
    return pl.pallas_call(
        finish_kernel,
        out_shape=(
            jax.ShapeDtypeStruct((2 * CH, 2 * GROUP * HD), gq.dtype),
            jax.ShapeDtypeStruct(grad_k.shape, grad_k.dtype),
            jax.ShapeDtypeStruct(grad_v.shape, grad_v.dtype),
            jax.ShapeDtypeStruct(grad_x.shape, grad_x.dtype),
        ),
        in_specs=[pl.BlockSpec(memory_space=pltpu.SMEM)] + [anyspace] * 6,
        out_specs=(anyspace,) * 4,
        scratch_shapes=[
            pltpu.VMEM((2 * CH, 2 * GROUP * HD), gq.dtype),
            pltpu.VMEM(grad_k.shape, grad_k.dtype),
            pltpu.VMEM(grad_v.shape, grad_v.dtype),
            pltpu.VMEM(grad_x.shape, grad_x.dtype),
            pltpu.SemaphoreType.DMA((4,)),
            pltpu.SemaphoreType.DMA((2 * GROUP,)),
        ],
        compiler_params=pltpu.CompilerParams(vmem_limit_bytes=VMEM_MIB * MIB),
        name="finish",
    )(span_slot, gq, gqo, units, grad_k, grad_v, grad_x)


def per_device(queries, keys, values, d_out, w_key, w_value, pair_list, span_slot):
    pair_rows = jnp.pad(pair_list.astype(jnp.bfloat16), ((0, 0), (0, HD - 2)))
    kg, vg, unit, qx, dox, near = gather_all(span_slot, pair_rows, keys, values, queries, d_out, w_key, w_value)
    kg = kg.reshape((NCTX,) + kg.shape[2:])
    vg = vg.reshape((NCTX,) + vg.shape[2:])
    gq, gqx, hdq, pk, pv = attend(span_slot, queries, d_out, qx, dox, kg, vg, unit)
    pk = pk.reshape((PARTS, CHIPS, 2) + pk.shape[2:])
    pv = pv.reshape((PARTS, CHIPS, 2) + pv.shape[2:])
    grad_k, grad_v, gqo, grad_x, units = reduce_project(pk, pv, near, gqx, hdq, w_key, w_value)
    return finish(span_slot, gq, gqo, units, grad_k, grad_v, grad_x)


def solution(mesh):
    return jax.shard_map(
        per_device,
        mesh=mesh,
        in_specs=(
            P("ctx", "head"),
            P("ctx", "head"),
            P("ctx", "head"),
            P("ctx", "head"),
            P(None, "head"),
            P(None, "head"),
            P("ctx", None),
            P(),
        ),
        out_specs=(P("ctx", "head"), P("ctx", "head"), P("ctx", "head"), P(("ctx", "head"), None)),
        check_vma=False,
    )
```

```python
import functools

import jax
import jax.numpy as jnp
from jax import lax
from jax.experimental import pallas as pl
from jax.experimental.pallas import tpu as pltpu
from jax.sharding import PartitionSpec as P

MESH = pl.DeviceIdType.MESH
HD = 128
CH = 128
SPANS = 64
NX = 4
NY = 4
NZ = 4
NCTX = NX * NY * 2
CHIPS = NX * NY
GROUP = 8
PARTS = 2
WIDE = 8
KEPT = 6
NPAD = 16
SCALE = HD ** -0.5
EXP_SCALE = SCALE * 1.4426950408889634
neg_fill = -1e30
QB = 1024
MIB = 1024 * 1024
VMEM_MIB = 62


def ctx_coords():
    me = lax.axis_index("ctx")
    return me // (2 * NX), lax.rem(me // 2, NX), lax.rem(me, 2)


def ctx_id(y, x, core):
    return (y * NX + x) * 2 + core


def turn(pos, step, size):
    return lax.rem(pos + step + size, size)


class Plane:
    def __init__(self, first):
        self.y, self.x, self.core = ctx_coords()
        self.first = first

    def at(self, da, db, flip=False):
        dy, dx = (da, db) if self.first == "y" else (db, da)
        core = 1 - self.core if flip else self.core
        return ctx_id(turn(self.y, dy, NY), turn(self.x, dx, NX), core)

    def chip(self, da, db):
        dy, dx = (da, db) if self.first == "y" else (db, da)
        return turn(self.y, dy, NY) * NX + turn(self.x, dx, NX)


def barrier_with(targets):
    barrier = pltpu.get_barrier_semaphore()
    for device in targets:
        pl.semaphore_signal(barrier, inc=1, device_id=device, device_id_type=MESH)
    pl.semaphore_wait(barrier, len(targets))


def ctx_targets():
    plane = Plane("x")
    steps = [(1, 0), (2, 0), (3, 0), (0, 1), (0, 2), (0, 3)]
    return [{"ctx": plane.at(da, db)} for da, db in steps] + [{"ctx": plane.at(0, 0, True)}]


def head_targets(steps):
    me_z = lax.axis_index("head")
    return [{"head": turn(me_z, d, NZ)} for d in steps]


class Copies:
    def __init__(self, send, recv):
        self.send, self.recv, self.started = send, recv, []

    def start(self, src, dst, index, device):
        copy = pltpu.make_async_remote_copy(
            src_ref=src, dst_ref=dst, send_sem=self.send.at[index], recv_sem=self.recv.at[index],
            device_id=device, device_id_type=MESH,
        )
        copy.start()
        self.started.append(copy)

    def landed(self, dst, index, device):
        pltpu.make_async_remote_copy(
            src_ref=dst, dst_ref=dst, send_sem=self.send.at[index], recv_sem=self.recv.at[index],
            device_id=device, device_id_type=MESH,
        ).wait_recv()

    def finish(self):
        for copy in self.started:
            copy.wait_send()


DA_OF = (0, -1, 1, 2)


class Gather:
    def __init__(self, first, out, send, recv):
        self.plane = Plane(first)
        self.out = out
        self.copies = Copies(send, recv)

    def dev(self, da, db):
        return {"ctx": self.plane.at(da, db)}

    def region(self, da, db):
        return self.out.at[self.plane.chip(da, db)]

    def send(self, region, index, da, db):
        self.copies.start(region, region, index, self.dev(da, db))

    def begin_a(self):
        self.send(self.region(0, 0), 0, 1, 0)
        self.send(self.region(0, 0), 1, -1, 0)

    def spread(self, m):
        region = self.region(DA_OF[m], 0)
        self.send(region, 4 + 4 * m, 0, 1)
        self.send(region, 5 + 4 * m, 0, -1)

    def got_a(self, step):
        index = 0 if step < 0 else 1
        region = self.region(step, 0)
        self.copies.landed(region, index, self.dev(step, 0))
        self.send(region.at[index], 2 + index, -step, 0)

    def got_a_far(self):
        region = self.region(2, 0)
        self.copies.landed(region.at[0], 2, self.dev(-1, 0))
        self.copies.landed(region.at[1], 3, self.dev(1, 0))

    def got_b(self, m, step):
        index = 0 if step < 0 else 1
        region = self.region(DA_OF[m], step)
        self.copies.landed(region, 4 + 4 * m + index, self.dev(0, step))
        self.send(region.at[index], 6 + 4 * m + index, 0, -step)

    def got_b_far(self, m):
        region = self.region(DA_OF[m], 2)
        self.copies.landed(region.at[0], 6 + 4 * m, self.dev(0, -1))
        self.copies.landed(region.at[1], 7 + 4 * m, self.dev(0, 1))


def gather_kernel(
    span_slot, pairs_ref, keys_ref, values_ref, q_ref, do_ref, wk_hbm, wv_hbm,
    kg_ref, vg_ref, unit_ref, qx_ref, dox_ref, near_ref,
    keys_pad, give, held, from_core, first_in, mid, last_in,
    k_send, k_recv, v_send, v_recv, u_send, u_recv, w_send, w_recv, c_send, c_recv, own_sem,
):
    keys_pad[0:2 * CH, :] = keys_ref[...]
    for g in range(2):
        keys_pad[2 * CH:2 * CH + NPAD, g * HD:(g + 1) * HD] = pairs_ref[...]
    barrier_with(ctx_targets() + head_targets((1, 3)))
    y, x, core = ctx_coords()
    plane = Plane("x")
    chip = plane.chip(0, 0)
    sibling = {"ctx": plane.at(0, 0, True)}
    gathers = [
        Gather("x", kg_ref, k_send, k_recv),
        Gather("y", vg_ref, v_send, v_recv),
    ]

    def group_cols(which, width):
        return pl.ds(pl.multiple_of(which * width, width), width)

    cross = Copies(c_send, c_recv)
    other = group_cols(1 - core, HD)
    cross.start(keys_pad.at[:, other], kg_ref.at[chip, core], 0, sibling)
    cross.start(values_ref.at[:, other], vg_ref.at[chip, core], 1, sibling)
    mine = group_cols(core, HD)
    own_copies = [
        pltpu.make_async_copy(keys_pad.at[:, mine], kg_ref.at[chip, core], own_sem.at[0]),
        pltpu.make_async_copy(values_ref.at[:, mine], vg_ref.at[chip, core], own_sem.at[1]),
    ]
    for copy in own_copies:
        copy.start()

    def pick(dst, group):
        def unit(j, carry):
            cols = pl.ds(pl.multiple_of((group * GROUP + lax.rem(j, GROUP)) * HD, HD), HD)
            dense = span_slot[SPANS - 2 + j // GROUP]
            first, second = [
                jnp.full((1, HD), (dense == 4 * chip + 2 * core + i).astype(jnp.float32)).astype(jnp.bfloat16)
                for i in range(2)
            ]
            for n, ref in enumerate((q_ref, do_ref)):
                dst[n, j // NX, lax.rem(j, NX)] = ref[0:CH, cols] * first + ref[CH:2 * CH, cols] * second
            return carry

        lax.fori_loop(0, CHIPS, unit, 0)

    for copy in own_copies:
        copy.wait()
    cross.landed(kg_ref.at[chip, 1 - core], 0, sibling)
    cross.landed(vg_ref.at[chip, 1 - core], 1, sibling)
    for gather in gathers:
        gather.begin_a()
    for gather in gathers:
        gather.spread(0)

    units = Copies(u_send, u_recv)
    pick(give, 1 - core)
    units.start(give, from_core, 0, sibling)

    me_z = lax.axis_index("head")
    piece = near_ref.shape[2]
    moves = Copies(w_send, w_recv)
    for n, ref in enumerate((wk_hbm, wv_hbm)):
        for side, step in enumerate((1, -1)):
            to = turn(me_z, step, NZ)
            start = pl.multiple_of((2 * to + core) * piece, piece)
            moves.start(ref.at[pl.ds(start, piece)], near_ref.at[side, n], 2 * side + n, {"head": to})
    qcols = group_cols(1 - core, GROUP * HD)
    cross.start(q_ref.at[:, qcols], qx_ref, 2, sibling)
    cross.start(do_ref.at[:, qcols], dox_ref, 3, sibling)

    pick(held, core)
    units.landed(from_core, 0, sibling)

    def add_core(j, carry):
        for n in range(2):
            held[n, j // NX, lax.rem(j, NX)] += from_core[n, j // NX, lax.rem(j, NX)]
        return carry

    lax.fori_loop(0, CHIPS, add_core, 0)
    for d in (1, 2, 3):
        far_x, far_y = turn(x, d, NX), turn(y, d, NY)
        units.start(held.at[0, :, far_x], first_in.at[0, d - 1], d, {"ctx": plane.at(d, 0)})
        units.start(held.at[1, far_y], first_in.at[1, d - 1], 3 + d, {"ctx": plane.at(0, d)})

    for gather in gathers:
        gather.got_a(-1)
        gather.got_a(1)
    for gather in gathers:
        gather.spread(1)
        gather.spread(2)
    for gather in gathers:
        gather.got_b(0, -1)
        gather.got_b(0, 1)
    for gather in gathers:
        gather.got_a_far()
        gather.spread(3)

    for d in (1, 2, 3):
        units.landed(first_in.at[0, d - 1], d, {"ctx": plane.at(-d, 0)})
        units.landed(first_in.at[1, d - 1], 3 + d, {"ctx": plane.at(0, -d)})
    for n in range(4):
        mid[0, n] = held[0, n, x] + first_in[0, 0, n] + first_in[0, 1, n] + first_in[0, 2, n]
        mid[1, n] = held[1, y, n] + first_in[1, 0, n] + first_in[1, 1, n] + first_in[1, 2, n]
    for d in (1, 2, 3):
        units.start(mid.at[0, turn(y, d, NY)], last_in.at[0, d - 1], 6 + d, {"ctx": plane.at(0, d)})
        units.start(mid.at[1, turn(x, d, NX)], last_in.at[1, d - 1], 9 + d, {"ctx": plane.at(d, 0)})

    for m in (1, 2, 3):
        for gather in gathers:
            gather.got_b(m, -1)
            gather.got_b(m, 1)

    for d in (1, 2, 3):
        units.landed(last_in.at[0, d - 1], 6 + d, {"ctx": plane.at(0, -d)})
        units.landed(last_in.at[1, d - 1], 9 + d, {"ctx": plane.at(-d, 0)})
    unit_ref[0] = mid[0, y] + last_in[0, 0] + last_in[0, 1] + last_in[0, 2]
    unit_ref[1] = mid[1, x] + last_in[1, 0] + last_in[1, 1] + last_in[1, 2]

    cross.landed(qx_ref, 2, sibling)
    cross.landed(dox_ref, 3, sibling)
    for n in range(2):
        for side, step in enumerate((1, -1)):
            origin = {"head": turn(me_z, -step, NZ)}
            moves.landed(near_ref.at[side, n], 2 * side + n, origin)
    for m in range(4):
        for gather in gathers:
            gather.got_b_far(m)
    for gather in gathers:
        gather.copies.finish()
    cross.finish()
    units.finish()
    moves.finish()


def gather_all(span_slot, pair_rows, keys, values, queries, d_out, w_key, w_value):
    vmem = pl.BlockSpec(memory_space=pltpu.VMEM)
    anyspace = pl.BlockSpec(memory_space=pl.ANY)
    blk = jnp.bfloat16
    piece = w_key.shape[0] // NZ // 2
    return pl.pallas_call(
        gather_kernel,
        out_shape=(
            jax.ShapeDtypeStruct((CHIPS, 2, keys.shape[0] + NPAD, HD), blk),
            jax.ShapeDtypeStruct((CHIPS, 2, values.shape[0], HD), blk),
            jax.ShapeDtypeStruct((2, CH, HD), blk),
            jax.ShapeDtypeStruct((2 * CH, GROUP * HD), blk),
            jax.ShapeDtypeStruct((2 * CH, GROUP * HD), blk),
            jax.ShapeDtypeStruct((2, 2, piece) + w_key.shape[1:], blk),
        ),
        in_specs=[pl.BlockSpec(memory_space=pltpu.SMEM)] + [vmem] * 5 + [anyspace] * 2,
        out_specs=(anyspace, anyspace, vmem) + (anyspace,) * 3,
        scratch_shapes=[
            pltpu.VMEM((keys.shape[0] + NPAD, keys.shape[1]), blk),
            pltpu.VMEM((2, NY, NX, CH, HD), blk),
            pltpu.VMEM((2, NY, NX, CH, HD), blk),
            pltpu.VMEM((2, NY, NX, CH, HD), blk),
            pltpu.VMEM((2, 3, 4, CH, HD), blk),
            pltpu.VMEM((2, 4, CH, HD), blk),
            pltpu.VMEM((2, 3, CH, HD), blk),
            pltpu.SemaphoreType.DMA((20,)),
            pltpu.SemaphoreType.DMA((20,)),
            pltpu.SemaphoreType.DMA((20,)),
            pltpu.SemaphoreType.DMA((20,)),
            pltpu.SemaphoreType.DMA((13,)),
            pltpu.SemaphoreType.DMA((13,)),
            pltpu.SemaphoreType.DMA((8,)),
            pltpu.SemaphoreType.DMA((8,)),
            pltpu.SemaphoreType.DMA((4,)),
            pltpu.SemaphoreType.DMA((4,)),
            pltpu.SemaphoreType.DMA((2,)),
        ],
        compiler_params=pltpu.CompilerParams(
            collective_id=0, has_side_effects=True, vmem_limit_bytes=VMEM_MIB * MIB
        ),
        name="gather_kv",
    )(span_slot, pair_rows, keys, values, queries, d_out, w_key, w_value)


def dot_nt(a, b):
    return lax.dot_general(a, b, (((1,), (1,)), ((), ())), preferred_element_type=jnp.float32)


def dot_nn(a, b):
    return lax.dot_general(a, b, (((1,), (0,)), ((), ())), preferred_element_type=jnp.float32)


def dot_tn(a, b):
    return lax.dot_general(a, b, (((0,), (0,)), ((), ())), preferred_element_type=jnp.float32)


def attend_kernel(
    span_slot, q_hbm, do_hbm, qx_hbm, dox_hbm, kg_hbm, vg_hbm, unit_ref,
    gq_ref, gqx_ref, hdq_ref, pk_hbm, pv_hbm,
    kg, vg, qs, ds, gq_all, stage, probs, dprob, tops, kept_probs, kept_dprob, kept_tops, stat, acck, accv, dqt, found, flags, slot_label, todo,
    flag_sem, qsems, load_sems, store_sems,
):
    me = lax.axis_index("ctx")
    core = lax.rem(me, 2)
    unit = me // 2
    quarter = NCTX // 4
    pair_copy = pltpu.make_async_copy(
        kg_hbm.at[:, pl.ds(2 * CH, NPAD)], kg.at[:, pl.ds(2 * CH, NPAD)], load_sems.at[4, 0]
    )
    pair_copy.start()
    loads = []
    for n in range(4):
        part = pl.ds(n * quarter, quarter)
        for side, (src, dst) in enumerate(((kg_hbm, kg), (vg_hbm, vg))):
            at = (part, pl.ds(0, 2 * CH))
            loads.append(pltpu.make_async_copy(src.at[at], dst.at[at], load_sems.at[n, side]))
            loads[-1].start()
    stacks = []
    for u in range(4):
        for r in range(GROUP):
            rows = pl.ds((u % 2) * CH, CH)
            own_cols = pl.ds(pl.multiple_of((core * GROUP + r) * HD, HD), HD)
            for n, (own, other, dst) in enumerate(((q_hbm, qx_hbm, qs), (do_hbm, dox_hbm, ds))):
                src = own.at[rows, own_cols] if u < 2 else other.at[rows, pl.ds(r * HD, HD)]
                stacks.append(pltpu.make_async_copy(src, dst.at[u, pl.ds(r * CH, CH)], qsems.at[n, u * GROUP + r]))
    for copy in stacks:
        copy.start()

    def name_slot(c, carry):
        slot_label[span_slot[c]] = c
        return carry

    lax.fori_loop(0, SPANS, name_slot, 0, unroll=8)

    def slot_of(u):
        return 2 * (2 * unit + lax.rem(core + u // 2, 2)) + lax.rem(u, 2)

    pair_copy.wait()
    pair_rows = kg[:, 2 * CH:2 * CH + NPAD, :].reshape(NCTX * NPAD, HD).astype(jnp.float32)
    lanes = lax.broadcasted_iota(jnp.int32, (1, HD), 1).astype(jnp.float32)
    for u in range(4):
        own = slot_label[slot_of(u)].astype(jnp.float32)
        hit = jnp.logical_and(pair_rows[:, 0:1] == own, pair_rows[:, 1:2] == lanes)
        found[u:u + 1, :] = jnp.max(jnp.where(hit, 1.0, 0.0), axis=0, keepdims=True).astype(jnp.int32)
    flag_copy = pltpu.make_async_copy(found, flags, flag_sem.at[0])
    flag_copy.start()

    label = SPANS - 2 + unit // GROUP
    q_unit = unit_ref[0]
    do_unit = unit_ref[1]

    steps = NCTX // WIDE

    def many(ref, t):
        return jnp.concatenate([ref[WIDE * t + u, 0:2 * CH, :] for u in range(WIDE)], axis=0)

    def unit_first(t, carry):
        top, total, mix = carry
        scores = dot_nt(many(kg, t), q_unit) * EXP_SCALE
        mixed = dot_nt(many(vg, t), do_unit)
        diff = lax.broadcasted_iota(jnp.int32, (CH, HD), 0) - lax.broadcasted_iota(jnp.int32, (CH, HD), 1)
        scores = jnp.concatenate([
            jnp.where(diff <= (label - slot_label[2 * WIDE * t + u]) * CH, scores[u * CH:(u + 1) * CH], neg_fill)
            for u in range(2 * WIDE)
        ], axis=0)
        new_top = jnp.maximum(top, jnp.max(scores, axis=0, keepdims=True))
        weights = jnp.exp2(scores - new_top)
        factor = jnp.exp2(top - new_top)
        probs[t] = weights
        dprob[t] = mixed
        tops[t] = new_top
        return (
            new_top,
            total * factor + jnp.sum(weights, axis=0, keepdims=True),
            mix * factor + jnp.sum(weights * mixed, axis=0, keepdims=True),
        )

    zero_row = jnp.zeros((1, HD), jnp.float32)
    state = (jnp.full((1, HD), neg_fill, jnp.float32), zero_row, zero_row)
    for n in range(4):
        for copy in loads[2 * n:2 * n + 2]:
            copy.wait()
        state = lax.fori_loop(n * steps // 4, (n + 1) * steps // 4, unit_first, state)
    top, total, mix = state
    over = 1.0 / total
    delta = mix * over

    def unit_second(t, acc):
        factor = jnp.exp2(tops[t] - top) * over
        weights = probs[t] * factor
        dscore = (weights * (dprob[t] - delta)).astype(jnp.bfloat16)
        value_part = dot_nn(weights.astype(jnp.bfloat16), do_unit)
        key_part = dot_nn(dscore, q_unit)
        for u in range(WIDE):
            accv[WIDE * t + u] = value_part[2 * u * CH:2 * (u + 1) * CH]
            acck[WIDE * t + u] = key_part[2 * u * CH:2 * (u + 1) * CH]
        return acc + dot_tn(many(kg, t), dscore)

    acc = lax.fori_loop(0, steps, unit_second, jnp.zeros((HD, CH), jnp.float32))
    hdq_ref[...] = (acc * SCALE).T.astype(jnp.bfloat16)

    flag_copy.wait()
    for copy in stacks:
        copy.wait()

    def span_work(u, carry):
        own_slot = slot_of(u)
        own_label = slot_label[own_slot]

        @pl.when(own_label < SPANS - 2)
        def _():
            todo[0] = own_slot

            def note(c, n):
                todo[n] = span_slot[c]
                wanted = jnp.logical_and(flags[u, c] > 0, c != own_label)
                return n + wanted.astype(jnp.int32)

            count = lax.fori_loop(0, SPANS, note, jnp.int32(1), unroll=8)
            todo[count] = own_slot

            def rows_at(slot):
                return pl.ds(pl.multiple_of(lax.rem(slot, 2) * CH, CH), CH)

            todo[count + 1] = own_slot

            def some(ref, base, size):
                slots = [todo[base + v] for v in range(size)]
                return jnp.concatenate([ref[slot // 2, rows_at(slot), :] for slot in slots], axis=0)

            def dots(base, size, masked):
                scores = dot_nt(some(kg, base, size), qs[u]) * EXP_SCALE
                if masked:
                    diff = lax.broadcasted_iota(jnp.int32, (CH, QB), 0) - lax.rem(
                        lax.broadcasted_iota(jnp.int32, (CH, QB), 1), CH
                    )
                    limits = [
                        jnp.where(base + v == 0, 0, jnp.where(base + v < count, CH, -CH)) for v in range(size)
                    ]
                    scores = jnp.concatenate([
                        jnp.where(diff <= limits[v], scores[v * CH:(v + 1) * CH], neg_fill) for v in range(size)
                    ], axis=0)
                return scores, dot_nt(some(vg, base, size), ds[u])

            def first(keep, base, size, masked):
                scores, mixed = dots(base, size, masked)
                old_top = stat[0:1, :]
                new_top = jnp.maximum(old_top, jnp.max(scores, axis=0, keepdims=True))
                weights = jnp.exp2(scores - new_top)
                factor = jnp.exp2(old_top - new_top)
                if keep:
                    kept_probs[base // 4, 0:size * CH, :] = weights
                    kept_dprob[base // 4, 0:size * CH, :] = mixed
                    kept_tops[base // 4] = new_top
                stat[0:1, :] = new_top
                stat[1:2, :] = stat[1:2, :] * factor + jnp.sum(weights, axis=0, keepdims=True)
                stat[2:3, :] = stat[2:3, :] * factor + jnp.sum(weights * mixed, axis=0, keepdims=True)

            def second(keep, base, size, masked):
                if keep:
                    weights = kept_probs[base // 4, 0:size * CH, :] * jnp.exp2(kept_tops[base // 4] - stat[3:4, :])
                    mixed = kept_dprob[base // 4, 0:size * CH, :]
                else:
                    scores, mixed = dots(base, size, masked)
                    weights = jnp.exp2(scores - stat[3:4, :])
                dscore = (weights * (mixed - stat[4:5, :])).astype(jnp.bfloat16)
                value_part = dot_nn(weights.astype(jnp.bfloat16), ds[u])
                key_part = dot_nn(dscore, qs[u])
                for v in range(size):
                    slot = todo[base + v]
                    accv[slot // 2, rows_at(slot), :] += value_part[v * CH:(v + 1) * CH]
                    acck[slot // 2, rows_at(slot), :] += key_part[v * CH:(v + 1) * CH]
                dqt[...] += dot_tn(some(kg, base, size), dscore)

            fours = (count + 1) // 4
            fits = (count + 3) // 4 <= KEPT

            def sweep(work, keep):
                def step(t, c):
                    masked = jnp.logical_or(t == 0, 4 * t + 4 > count)

                    @pl.when(masked)
                    def _():
                        work(keep, 4 * t, 4, True)

                    @pl.when(jnp.logical_not(masked))
                    def _():
                        work(keep, 4 * t, 4, False)

                    return c

                def plain(t, c):
                    work(keep, 4 * t, 4, False)
                    return c

                lax.fori_loop(0, fours, plain if keep and work is second else step, 0)

                @pl.when(4 * fours < count)
                def _():
                    work(keep, 4 * fours, 2, True)

            stat[0:1, :] = jnp.full((1, QB), neg_fill, jnp.float32)
            stat[1:3, :] = jnp.zeros((2, QB), jnp.float32)
            dqt[...] = jnp.zeros_like(dqt)

            def both_sweeps(keep):
                sweep(first, keep)
                total_row = stat[1:2, :]
                stat[3:4, :] = stat[0:1, :] + jnp.log2(total_row)
                stat[4:5, :] = stat[2:3, :] / total_row
                sweep(second, keep)

            @pl.when(fits)
            def _():
                both_sweeps(True)

            @pl.when(jnp.logical_not(fits))
            def _():
                both_sweeps(False)

            for r in range(GROUP):
                gq_all[pl.ds(pl.multiple_of(u * CH, CH), CH), r * HD:(r + 1) * HD] = (
                    (dqt[:, r * CH:(r + 1) * CH] * SCALE).T.astype(jnp.bfloat16)
                )

        return carry

    lax.fori_loop(0, 4, span_work, 0)

    stores = [
        pltpu.make_async_copy(gq_all.at[pl.ds(0, 2 * CH)], gq_ref, store_sems.at[4, 0]),
        pltpu.make_async_copy(gq_all.at[pl.ds(2 * CH, 2 * CH)], gqx_ref, store_sems.at[4, 1]),
    ]
    for copy in stores:
        copy.start()
    for n in range(4):
        part = pl.ds(n * quarter, quarter)

        def narrow(t, carry):
            for side, ref in enumerate((acck, accv)):
                rows = ref[t].astype(jnp.bfloat16).reshape(NZ, PARTS, 2 * CH // NZ // PARTS, HD)
                for m in range(PARTS):
                    stage[side, m, t] = rows[:, m]
            return carry

        lax.fori_loop(n * quarter, (n + 1) * quarter, narrow, 0)
        for side, dst in enumerate((pk_hbm, pv_hbm)):
            stores.append(
                pltpu.make_async_copy(stage.at[side, :, part], dst.at[:, part], store_sems.at[n, side])
            )
            stores[-1].start()
    for copy in stores:
        copy.wait()


def attend(span_slot, queries, d_out, qx, dox, kg, vg, unit):
    vmem = pl.BlockSpec(memory_space=pltpu.VMEM)
    smem = pl.BlockSpec(memory_space=pltpu.SMEM)
    anyspace = pl.BlockSpec(memory_space=pl.ANY)
    blk = jnp.bfloat16
    return pl.pallas_call(
        attend_kernel,
        out_shape=(
            jax.ShapeDtypeStruct((2 * CH, GROUP * HD), blk),
            jax.ShapeDtypeStruct((2 * CH, GROUP * HD), blk),
            jax.ShapeDtypeStruct((CH, HD), blk),
            jax.ShapeDtypeStruct((PARTS, NCTX, NZ, 2 * CH // NZ // PARTS, HD), blk),
            jax.ShapeDtypeStruct((PARTS, NCTX, NZ, 2 * CH // NZ // PARTS, HD), blk),
        ),
        in_specs=[smem] + [anyspace] * 6 + [vmem],
        out_specs=(anyspace, anyspace, vmem, anyspace, anyspace),
        scratch_shapes=[
            pltpu.VMEM(kg.shape, blk),
            pltpu.VMEM(vg.shape, blk),
            pltpu.VMEM((4, GROUP * CH, HD), blk),
            pltpu.VMEM((4, GROUP * CH, HD), blk),
            pltpu.VMEM((4 * CH, GROUP * HD), blk),
            pltpu.VMEM((2, PARTS, NCTX, NZ, 2 * CH // NZ // PARTS, HD), blk),
            pltpu.VMEM((NCTX // WIDE, 2 * WIDE * CH, HD), jnp.float32),
            pltpu.VMEM((NCTX // WIDE, 2 * WIDE * CH, HD), jnp.float32),
            pltpu.VMEM((NCTX // WIDE, 1, HD), jnp.float32),
            pltpu.VMEM((KEPT, 4 * CH, QB), jnp.float32),
            pltpu.VMEM((KEPT, 4 * CH, QB), jnp.float32),
            pltpu.VMEM((KEPT, 1, QB), jnp.float32),
            pltpu.VMEM((8, QB), jnp.float32),
            pltpu.VMEM((NCTX, 2 * CH, HD), jnp.float32),
            pltpu.VMEM((NCTX, 2 * CH, HD), jnp.float32),
            pltpu.VMEM((HD, QB), jnp.float32),
            pltpu.VMEM((8, HD), jnp.int32),
            pltpu.SMEM((8, HD), jnp.int32),
            pltpu.SMEM((SPANS,), jnp.int32),
            pltpu.SMEM((SPANS + 8,), jnp.int32),
            pltpu.SemaphoreType.DMA((1,)),
            pltpu.SemaphoreType.DMA((2, 32)),
            pltpu.SemaphoreType.DMA((5, 2)),
            pltpu.SemaphoreType.DMA((5, 2)),
        ],
        compiler_params=pltpu.CompilerParams(vmem_limit_bytes=VMEM_MIB * MIB),
        cost_estimate=pl.CostEstimate(flops=8 * 10**9, bytes_accessed=32 * 10**6, transcendentals=4 * 10**6),
        name="attend",
    )(span_slot, queries, d_out, qx, dox, kg, vg, unit)


def plus(a, b):
    return (a.astype(jnp.float32) + b.astype(jnp.float32)).astype(jnp.bfloat16)


class Scatter:
    def __init__(self, first, parts, own, near, full, near_b, full_b, send, recv, own_sem):
        self.plane = Plane(first)
        self.parts, self.own, self.own_sem = parts, own, own_sem
        self.near, self.full, self.near_b, self.full_b = near, full, near_b, full_b
        self.copies = Copies(send, recv)

    def dev(self, da, db):
        return {"ctx": self.plane.at(da, db)}

    def load(self, q, e):
        return pltpu.make_async_copy(self.parts.at[self.plane.chip(e, q)], self.own.at[q, e], self.own_sem.at[4 * q + e])

    def far(self, q):
        block = self.parts.at[self.plane.chip(2, q)]
        self.copies.start(block.at[0], self.near.at[q, 0], 4 * q, self.dev(1, 0))
        self.copies.start(block.at[1], self.near.at[q, 1], 4 * q + 1, self.dev(-1, 0))

    def next(self, q):
        for side, step in enumerate((1, -1)):
            e = step % 4
            self.load(q, e).wait()
            self.copies.landed(self.near.at[q, side], 4 * q + side, self.dev(-step, 0))
            self.own[q, e, side] = plus(self.own[q, e, side], self.near[q, side])
            self.copies.start(self.own.at[q, e], self.full.at[q, side], 4 * q + 2 + side, self.dev(step, 0))

    def last(self, q):
        self.load(q, 0).wait()
        self.copies.landed(self.full.at[q, 0], 4 * q + 2, self.dev(-1, 0))
        self.copies.landed(self.full.at[q, 1], 4 * q + 3, self.dev(1, 0))
        return (
            self.own[q, 0].astype(jnp.float32)
            + self.full[q, 0].astype(jnp.float32)
            + self.full[q, 1].astype(jnp.float32)
        )

    def last_far(self):
        self.own[2, 0] = self.last(2).astype(jnp.bfloat16)
        for side, step in enumerate((1, -1)):
            self.copies.start(self.own.at[2, 0, side], self.near_b.at[side], 16 + side, self.dev(0, step))

    def last_near(self, side):
        step = (1, -1)[side]
        q = step % 4
        total = self.last(q)
        self.copies.landed(self.near_b.at[side], 16 + side, self.dev(0, -step))
        self.own[q, 0, 1 - side] = total[1 - side].astype(jnp.bfloat16)
        self.own[q, 0, side] = (total[side] + self.near_b[side].astype(jnp.float32)).astype(jnp.bfloat16)
        self.copies.start(self.own.at[q, 0], self.full_b.at[side], 18 + side, self.dev(0, step))

    def finish(self):
        total = self.last(0)
        self.copies.landed(self.full_b.at[0], 18, self.dev(0, -1))
        self.copies.landed(self.full_b.at[1], 19, self.dev(0, 1))
        return total + self.full_b[0].astype(jnp.float32) + self.full_b[1].astype(jnp.float32)


def reduce_project_kernel(
    pk_ref, pv_ref, near_ref, gqx_ref, hdq_ref, wk_hbm, wv_hbm,
    gk_ref, gv_ref, gqo_ref, gx_ref, hg_ref,
    k_own, k_near, k_full, k_near_b, k_full_b,
    v_own, v_near, v_full, v_near_b, v_full_b,
    sums, swap, swap_in, grads, weights, total, half,
    k_send, k_recv, v_send, v_recv, w_send, w_recv, c_send, c_recv, g_send, g_recv, o_send, o_recv, h_send, h_recv,
    own_sems, w_sem, hg_sem, o_sem,
):
    barrier_with(ctx_targets() + head_targets((1, 2, 3)))
    me_z = lax.axis_index("head")
    y, x, core = ctx_coords()
    plane = Plane("x")
    sibling = {"ctx": plane.at(0, 0, True)}
    ways = [
        [
            Scatter("y", pk_ref.at[m], *(ref.at[m] for ref in (
                k_own, k_near, k_full, k_near_b, k_full_b, k_send, k_recv)), own_sems.at[m, 0]),
            Scatter("x", pv_ref.at[m], *(ref.at[m] for ref in (
                v_own, v_near, v_full, v_near_b, v_full_b, v_send, v_recv)), own_sems.at[m, 1]),
        ]
        for m in range(PARTS)
    ]
    order = (2, 1, 3, 0)

    def far(m):
        for q in order:
            for way in ways[m]:
                way.far(q)
        for e in (1, 3, 0):
            for q in order:
                for way in ways[m]:
                    way.load(q, e).start()

    def next_hop(m):
        for q in order:
            for way in ways[m]:
                way.next(q)

    def last_hop(m):
        for way in ways[m]:
            way.last_far()
        for side in range(2):
            for way in ways[m]:
                way.last_near(side)

    far(0)

    width = weights.shape[2]
    piece = width // 2
    moves = Copies(w_send, w_recv)
    two = turn(me_z, 2, NZ)
    start = pl.multiple_of((2 * two + core) * piece, piece)
    for n, ref in enumerate((wk_hbm, wv_hbm)):
        moves.start(
            ref.at[pl.ds(start, piece)], weights.at[2, n, pl.ds(pl.multiple_of(core * piece, piece), piece)], n,
            {"head": two},
        )
    mine_rows = pl.ds(pl.multiple_of(core * piece, piece), piece)
    other_rows = pl.ds(pl.multiple_of((1 - core) * piece, piece), piece)
    cross = Copies(c_send, c_recv)
    for side, d in enumerate((1, 3)):
        cross.start(near_ref.at[side], weights.at[d, :, mine_rows], side, sibling)
    cross.start(gqx_ref, gqo_ref, 2, sibling)
    wrows = pl.ds(pl.multiple_of(me_z * width, width), width)
    fetches = [
        pltpu.make_async_copy(wk_hbm.at[wrows], weights.at[0, 0], w_sem.at[0]),
        pltpu.make_async_copy(wv_hbm.at[wrows], weights.at[0, 1], w_sem.at[1]),
        pltpu.make_async_copy(near_ref.at[0], weights.at[1, :, mine_rows], w_sem.at[2]),
        pltpu.make_async_copy(near_ref.at[1], weights.at[3, :, mine_rows], w_sem.at[3]),
    ]
    for copy in fetches:
        copy.start()
    hg_copy = pltpu.make_async_copy(hdq_ref, hg_ref.at[y, x, core], hg_sem.at[0])
    hg_copy.start()

    rows_of_part = 2 * CH // NZ // PARTS
    sends = Copies(g_send, g_recv)
    outs = Copies(o_send, o_recv)
    own_outs = []

    def collect(m):
        for n, (way, factor) in enumerate(zip(ways[m], (SCALE, 1.0))):
            sums[...] = (way.finish() * factor).reshape(sums.shape)
            swap[m, n] = sums[1 - core].astype(jnp.bfloat16)
            cross.start(swap.at[m, n], swap_in.at[m, n], 4 + 2 * m + n, sibling)
            grads[m, 0, n, :, pl.ds(pl.multiple_of(core * HD, HD), HD)] = sums[core].astype(jnp.bfloat16)

    def share(m):
        for n, out in enumerate((gk_ref, gv_ref)):
            cross.landed(swap_in.at[m, n], 4 + 2 * m + n, sibling)
            grads[m, 0, n, :, pl.ds(pl.multiple_of((1 - core) * HD, HD), HD)] = swap_in[m, n]
        for d in (1, 3, 2):
            sends.start(grads.at[m, 0], grads.at[m, d], 3 * m + d - 1, {"head": turn(me_z, d, NZ)})
        for n, out in enumerate((gk_ref, gv_ref)):
            for h in range(NZ):
                at = (h * PARTS + m) * rows_of_part
                out[at:at + rows_of_part, :] = grads[m, 0, n, h * rows_of_part:(h + 1) * rows_of_part, :]

    step = 512

    def partial(m, d, cols):
        return dot_nt(grads[m, d, 0], weights[d, 0, cols, :]) + dot_nt(grads[m, d, 1], weights[d, 1, cols, :])

    def columns(n):
        return pl.ds(pl.multiple_of(n * step, step), step)

    def multiply(m, d):
        if d != 0:
            sends.landed(grads.at[m, d], 3 * m + d - 1, {"head": turn(me_z, -d, NZ)})

        def part(n, carry):
            if d == 0:
                total[m, :, columns(n)] = partial(m, d, columns(n))
            else:
                total[m, :, columns(n)] += partial(m, d, columns(n))
            return carry

        lax.fori_loop(0, width // step, part, 0)

    def deliver(m):
        sends.landed(grads.at[m, 2], 3 * m + 1, {"head": turn(me_z, -2, NZ)})
        rows_out = pl.ds(m * rows_of_part, rows_of_part)
        for n in range(width // step):
            cols = pl.ds(n * step, step)
            half[m, :, n * step:(n + 1) * step] = (
                total[m, :, n * step:(n + 1) * step] + partial(m, 2, cols)
            ).astype(jnp.bfloat16)
            out_cols = pl.ds(pl.multiple_of(me_z * width + n * step, step), step)

            def block(to):
                return half.at[m, pl.ds(pl.multiple_of(to * rows_of_part, rows_of_part), rows_of_part), cols]

            for d in (1, 3, 2):
                to = turn(me_z, d, NZ)
                outs.start(block(to), gx_ref.at[rows_out, out_cols], (m * 3 + d - 1) * 4 + n, {"head": to})
            own_outs.append(pltpu.make_async_copy(block(me_z), gx_ref.at[rows_out, out_cols], o_sem.at[m * 4 + n]))
            own_outs[-1].start()

    next_hop(0)
    far(1)
    last_hop(0)
    next_hop(1)
    collect(0)
    last_hop(1)
    share(0)

    for side, d in enumerate((1, 3)):
        cross.landed(weights.at[d, :, other_rows], side, sibling)
    for copy in fetches:
        copy.wait()
    multiply(0, 0)
    collect(1)
    share(1)

    units = Copies(h_send, h_recv)
    rows = [pl.ds(0, CH // 2), pl.ds(CH // 2, CH // 2)]
    hg_copy.wait()
    for d in (1, 2, 3):
        for n, (da, db) in enumerate(((d, 0), (0, d))):
            block = hg_ref.at[y, x, core, rows[n]]
            units.start(block, block, 2 * d - 2 + n, {"ctx": plane.at(da, db)})

    multiply(0, 1)
    multiply(0, 3)
    for n in range(2):
        moves.landed(weights.at[2, n, mine_rows], n, {"head": two})
    cross.start(weights.at[2, :, mine_rows], weights.at[2, :, mine_rows], 3, sibling)
    multiply(1, 0)
    cross.landed(weights.at[2, :, other_rows], 3, sibling)
    deliver(0)

    for d in (1, 2, 3):
        for n, (da, db) in enumerate(((-d, 0), (0, -d))):
            at = hg_ref.at[turn(y, db, NY), turn(x, da, NX), core, rows[n]]
            units.landed(at, 2 * d - 2 + n, {"ctx": plane.at(da, db)})
    for d in (1, 2, 3):
        block = hg_ref.at[y, :, core, rows[0]]
        units.start(block, block, 4 + 2 * d, {"ctx": plane.at(0, d)})
        block = hg_ref.at[:, x, core, rows[1]]
        units.start(block, block, 5 + 2 * d, {"ctx": plane.at(d, 0)})

    multiply(1, 1)
    multiply(1, 3)
    deliver(1)

    for d in (1, 2, 3):
        units.landed(hg_ref.at[turn(y, -d, NY), :, core, rows[0]], 4 + 2 * d, {"ctx": plane.at(0, -d)})
        units.landed(hg_ref.at[:, turn(x, -d, NX), core, rows[1]], 5 + 2 * d, {"ctx": plane.at(-d, 0)})
    units.start(hg_ref.at[:, :, core], hg_ref.at[:, :, core], 12, sibling)
    units.landed(hg_ref.at[:, :, 1 - core], 12, sibling)
    cross.landed(gqo_ref, 2, sibling)

    for m in range(PARTS):
        rows_out = pl.ds(m * rows_of_part, rows_of_part)
        for n in range(width // step):
            for d in (1, 3, 2):
                origin = turn(me_z, -d, NZ)
                out_cols = pl.ds(pl.multiple_of(origin * width + n * step, step), step)
                outs.landed(gx_ref.at[rows_out, out_cols], (m * 3 + d - 1) * 4 + n, {"head": origin})
    for m in range(PARTS):
        for way in ways[m]:
            way.copies.finish()
    for copies in (moves, cross, sends, outs, units):
        copies.finish()
    for copy in own_outs:
        copy.wait()


def reduce_project(pk, pv, near, gqx, hdq, w_key, w_value):
    vmem = pl.BlockSpec(memory_space=pltpu.VMEM)
    anyspace = pl.BlockSpec(memory_space=pl.ANY)
    blk = jnp.bfloat16
    depth = w_key.shape[0]
    width = depth // NZ
    rows = 2 * CH // PARTS
    block = (2, NZ, rows // NZ, HD)
    one = [
        pltpu.VMEM((PARTS, 4, 4) + block, blk),
        pltpu.VMEM((PARTS, 4) + block, blk),
        pltpu.VMEM((PARTS, 4, 2) + block, blk),
        pltpu.VMEM((PARTS,) + block, blk),
        pltpu.VMEM((PARTS, 2) + block, blk),
    ]

    def pair(*shape):
        return [pltpu.SemaphoreType.DMA(shape)] * 2

    return pl.pallas_call(
        reduce_project_kernel,
        out_shape=(
            jax.ShapeDtypeStruct((2 * CH, 2 * HD), blk),
            jax.ShapeDtypeStruct((2 * CH, 2 * HD), blk),
            jax.ShapeDtypeStruct(gqx.shape, blk),
            jax.ShapeDtypeStruct((2 * CH // NZ, depth), blk),
            jax.ShapeDtypeStruct((NY, NX, 2, CH, HD), blk),
        ),
        in_specs=[anyspace] * 4 + [vmem] + [anyspace] * 2,
        out_specs=(vmem, vmem, anyspace, vmem, vmem),
        scratch_shapes=one + one
        + [
            pltpu.VMEM((2, rows, HD), jnp.float32),
            pltpu.VMEM((PARTS, 2, rows, HD), blk),
            pltpu.VMEM((PARTS, 2, rows, HD), blk),
            pltpu.VMEM((PARTS, NZ, 2, rows, 2 * HD), blk),
            pltpu.VMEM((NZ, 2, width, 2 * HD), blk),
            pltpu.VMEM((PARTS, rows, width), jnp.float32),
            pltpu.VMEM((PARTS, rows, width), blk),
        ]
        + pair(PARTS, 20) + pair(PARTS, 20) + pair(2) + pair(8) + pair(6) + pair(24) + pair(13)
        + [
            pltpu.SemaphoreType.DMA((PARTS, 2, 16)),
            pltpu.SemaphoreType.DMA((4,)),
            pltpu.SemaphoreType.DMA((1,)),
            pltpu.SemaphoreType.DMA((8,)),
        ],
        compiler_params=pltpu.CompilerParams(
            collective_id=1, has_side_effects=True, vmem_limit_bytes=VMEM_MIB * MIB
        ),
        name="reduce_project",
    )(pk, pv, near, gqx, hdq, w_key, w_value)


def finish_kernel(span_slot, gq_hbm, gqo_hbm, hg_hbm, gk_hbm, gv_hbm, gx_hbm, oq, ok, ov, ox, vq, vk, vv, vx, sems, head_sems):
    me = lax.axis_index("ctx")
    core = lax.rem(me, 2)
    ways = ((gx_hbm, vx, ox), (gk_hbm, vk, ok), (gv_hbm, vv, ov))
    loads = [pltpu.make_async_copy(src, mid, sems.at[n]) for n, (src, mid, _) in enumerate(ways)]
    for copy in loads:
        copy.start()
    def span_copies(i):
        rows = pl.ds(i * CH, CH)
        pair = []
        for n, (src, which) in enumerate(((gq_hbm, core), (gqo_hbm, 1 - core))):
            cols = pl.ds(pl.multiple_of(which * GROUP * HD, GROUP * HD), GROUP * HD)
            pair.append(pltpu.make_async_copy(src.at[rows], vq.at[rows, cols], head_sems.at[i, n]))
        heads = []
        for s in range(2):
            heads.append([])
            for h in range(2 * GROUP):
                chip = s * GROUP + h % GROUP
                heads[s].append(pltpu.make_async_copy(
                    hg_hbm.at[chip // NX, chip % NX, h // GROUP], vq.at[rows, pl.ds(h * HD, HD)], head_sems.at[i, h]
                ))
        dense = [span_slot[SPANS - 2 + s] == 2 * me + i for s in range(2)]
        light = jnp.logical_not(jnp.logical_or(dense[0], dense[1]))
        return [(light, pair), (dense[0], heads[0]), (dense[1], heads[1])]

    choices = span_copies(0) + span_copies(1)
    for chosen, group in choices:
        @pl.when(chosen)
        def _():
            for copy in group:
                copy.start()

    for chosen, group in choices:
        @pl.when(chosen)
        def _():
            for copy in group:
                copy.wait()

    stores = [pltpu.make_async_copy(vq, oq, sems.at[3])]
    stores[0].start()
    for n, (_, mid, dst) in enumerate(ways):
        loads[n].wait()
        stores.append(pltpu.make_async_copy(mid, dst, sems.at[n]))
        stores[-1].start()
    for copy in stores:
        copy.wait()


def finish(span_slot, gq, gqo, units, grad_k, grad_v, grad_x):
    anyspace = pl.BlockSpec(memory_space=pl.ANY)
    return pl.pallas_call(
        finish_kernel,
        out_shape=(
            jax.ShapeDtypeStruct((2 * CH, 2 * GROUP * HD), gq.dtype),
            jax.ShapeDtypeStruct(grad_k.shape, grad_k.dtype),
            jax.ShapeDtypeStruct(grad_v.shape, grad_v.dtype),
            jax.ShapeDtypeStruct(grad_x.shape, grad_x.dtype),
        ),
        in_specs=[pl.BlockSpec(memory_space=pltpu.SMEM)] + [anyspace] * 6,
        out_specs=(anyspace,) * 4,
        scratch_shapes=[
            pltpu.VMEM((2 * CH, 2 * GROUP * HD), gq.dtype),
            pltpu.VMEM(grad_k.shape, grad_k.dtype),
            pltpu.VMEM(grad_v.shape, grad_v.dtype),
            pltpu.VMEM(grad_x.shape, grad_x.dtype),
            pltpu.SemaphoreType.DMA((4,)),
            pltpu.SemaphoreType.DMA((2, 2 * GROUP)),
        ],
        compiler_params=pltpu.CompilerParams(vmem_limit_bytes=VMEM_MIB * MIB),
        name="finish",
    )(span_slot, gq, gqo, units, grad_k, grad_v, grad_x)


def per_device(queries, keys, values, d_out, w_key, w_value, pair_list, span_slot):
    pair_rows = jnp.pad(pair_list.astype(jnp.bfloat16), ((0, 0), (0, HD - 2)))
    kg, vg, unit, qx, dox, near = gather_all(span_slot, pair_rows, keys, values, queries, d_out, w_key, w_value)
    kg = kg.reshape((NCTX,) + kg.shape[2:])
    vg = vg.reshape((NCTX,) + vg.shape[2:])
    gq, gqx, hdq, pk, pv = attend(span_slot, queries, d_out, qx, dox, kg, vg, unit)
    pk = pk.reshape((PARTS, CHIPS, 2) + pk.shape[2:])
    pv = pv.reshape((PARTS, CHIPS, 2) + pv.shape[2:])
    grad_k, grad_v, gqo, grad_x, units = reduce_project(pk, pv, near, gqx, hdq, w_key, w_value)
    return finish(span_slot, gq, gqo, units, grad_k, grad_v, grad_x)


def solution(mesh):
    return jax.shard_map(
        per_device,
        mesh=mesh,
        in_specs=(
            P("ctx", "head"),
            P("ctx", "head"),
            P("ctx", "head"),
            P("ctx", "head"),
            P(None, "head"),
            P(None, "head"),
            P("ctx", None),
            P(),
        ),
        out_specs=(P("ctx", "head"), P("ctx", "head"), P("ctx", "head"), P(("ctx", "head"), None)),
        check_vma=False,
    )
```

```python
import functools

import jax
import jax.numpy as jnp
from jax import lax
from jax.experimental import pallas as pl
from jax.experimental.pallas import tpu as pltpu
from jax.sharding import PartitionSpec as P

MESH = pl.DeviceIdType.MESH
HD = 128
CH = 128
SPANS = 64
NX = 4
NY = 4
NZ = 4
NCTX = NX * NY * 2
CHIPS = NX * NY
GROUP = 8
PARTS = 2
WIDE = 8
KEPT = 6
NPAD = 16
SCALE = HD ** -0.5
EXP_SCALE = SCALE * 1.4426950408889634
neg_fill = -1e30
QB = 1024
MIB = 1024 * 1024
VMEM_MIB = 62


def ctx_coords():
    me = lax.axis_index("ctx")
    return me // (2 * NX), lax.rem(me // 2, NX), lax.rem(me, 2)


def ctx_id(y, x, core):
    return (y * NX + x) * 2 + core


def turn(pos, step, size):
    return lax.rem(pos + step + size, size)


class Plane:
    def __init__(self, first):
        self.y, self.x, self.core = ctx_coords()
        self.first = first

    def at(self, da, db, flip=False):
        dy, dx = (da, db) if self.first == "y" else (db, da)
        core = 1 - self.core if flip else self.core
        return ctx_id(turn(self.y, dy, NY), turn(self.x, dx, NX), core)

    def chip(self, da, db):
        dy, dx = (da, db) if self.first == "y" else (db, da)
        return turn(self.y, dy, NY) * NX + turn(self.x, dx, NX)


def barrier_with(targets):
    barrier = pltpu.get_barrier_semaphore()
    for device in targets:
        pl.semaphore_signal(barrier, inc=1, device_id=device, device_id_type=MESH)
    pl.semaphore_wait(barrier, len(targets))


def ctx_targets():
    plane = Plane("x")
    steps = [(1, 0), (2, 0), (3, 0), (0, 1), (0, 2), (0, 3)]
    return [{"ctx": plane.at(da, db)} for da, db in steps] + [{"ctx": plane.at(0, 0, True)}]


def head_targets(steps):
    me_z = lax.axis_index("head")
    return [{"head": turn(me_z, d, NZ)} for d in steps]


class Copies:
    def __init__(self, send, recv):
        self.send, self.recv, self.started = send, recv, []

    def start(self, src, dst, index, device):
        copy = pltpu.make_async_remote_copy(
            src_ref=src, dst_ref=dst, send_sem=self.send.at[index], recv_sem=self.recv.at[index],
            device_id=device, device_id_type=MESH,
        )
        copy.start()
        self.started.append(copy)

    def landed(self, dst, index, device):
        pltpu.make_async_remote_copy(
            src_ref=dst, dst_ref=dst, send_sem=self.send.at[index], recv_sem=self.recv.at[index],
            device_id=device, device_id_type=MESH,
        ).wait_recv()

    def finish(self):
        for copy in self.started:
            copy.wait_send()


DA_OF = (0, -1, 1, 2)


class Gather:
    def __init__(self, first, out, send, recv):
        self.plane = Plane(first)
        self.out = out
        self.copies = Copies(send, recv)

    def dev(self, da, db):
        return {"ctx": self.plane.at(da, db)}

    def region(self, da, db):
        return self.out.at[self.plane.chip(da, db)]

    def send(self, region, index, da, db):
        self.copies.start(region, region, index, self.dev(da, db))

    def begin_a(self):
        self.send(self.region(0, 0), 0, 1, 0)
        self.send(self.region(0, 0), 1, -1, 0)

    def spread(self, m):
        region = self.region(DA_OF[m], 0)
        self.send(region, 4 + 4 * m, 0, 1)
        self.send(region, 5 + 4 * m, 0, -1)

    def got_a(self, step):
        index = 0 if step < 0 else 1
        region = self.region(step, 0)
        self.copies.landed(region, index, self.dev(step, 0))
        self.send(region.at[index], 2 + index, -step, 0)

    def got_a_far(self):
        region = self.region(2, 0)
        self.copies.landed(region.at[0], 2, self.dev(-1, 0))
        self.copies.landed(region.at[1], 3, self.dev(1, 0))

    def got_b(self, m, step):
        index = 0 if step < 0 else 1
        region = self.region(DA_OF[m], step)
        self.copies.landed(region, 4 + 4 * m + index, self.dev(0, step))
        self.send(region.at[index], 6 + 4 * m + index, 0, -step)

    def got_b_far(self, m):
        region = self.region(DA_OF[m], 2)
        self.copies.landed(region.at[0], 6 + 4 * m, self.dev(0, -1))
        self.copies.landed(region.at[1], 7 + 4 * m, self.dev(0, 1))


def gather_kernel(
    span_slot, pairs_ref, keys_ref, values_ref, q_ref, do_ref, wk_hbm, wv_hbm,
    kg_ref, vg_ref, unit_ref, qx_ref, dox_ref, near_ref,
    keys_pad, give, held, from_core, first_in, mid, last_in,
    k_send, k_recv, v_send, v_recv, u_send, u_recv, w_send, w_recv, c_send, c_recv, own_sem,
):
    keys_pad[0:2 * CH, :] = keys_ref[...]
    lanes = lax.broadcasted_iota(jnp.int32, (NPAD, HD), 1)
    pairs = pairs_ref[...].astype(jnp.float32)
    pair_rows = jnp.where(lanes == 0, pairs[:, 0:1], jnp.where(lanes == 1, pairs[:, 1:2], 0.0)).astype(jnp.bfloat16)
    for g in range(2):
        keys_pad[2 * CH:2 * CH + NPAD, g * HD:(g + 1) * HD] = pair_rows
    barrier_with(ctx_targets() + head_targets((1, 3)))
    y, x, core = ctx_coords()
    plane = Plane("x")
    chip = plane.chip(0, 0)
    sibling = {"ctx": plane.at(0, 0, True)}
    gathers = [
        Gather("x", kg_ref, k_send, k_recv),
        Gather("y", vg_ref, v_send, v_recv),
    ]

    def group_cols(which, width):
        return pl.ds(pl.multiple_of(which * width, width), width)

    cross = Copies(c_send, c_recv)
    other = group_cols(1 - core, HD)
    cross.start(keys_pad.at[:, other], kg_ref.at[chip, core], 0, sibling)
    cross.start(values_ref.at[:, other], vg_ref.at[chip, core], 1, sibling)
    mine = group_cols(core, HD)
    own_copies = [
        pltpu.make_async_copy(keys_pad.at[:, mine], kg_ref.at[chip, core], own_sem.at[0]),
        pltpu.make_async_copy(values_ref.at[:, mine], vg_ref.at[chip, core], own_sem.at[1]),
    ]
    for copy in own_copies:
        copy.start()

    def pick(dst, group):
        def unit(j, carry):
            cols = pl.ds(pl.multiple_of((group * GROUP + lax.rem(j, GROUP)) * HD, HD), HD)
            dense = span_slot[SPANS - 2 + j // GROUP]
            first, second = [
                jnp.full((1, HD), (dense == 4 * chip + 2 * core + i).astype(jnp.float32)).astype(jnp.bfloat16)
                for i in range(2)
            ]
            for n, ref in enumerate((q_ref, do_ref)):
                dst[n, j // NX, lax.rem(j, NX)] = ref[0:CH, cols] * first + ref[CH:2 * CH, cols] * second
            return carry

        lax.fori_loop(0, CHIPS, unit, 0)

    for copy in own_copies:
        copy.wait()
    cross.landed(kg_ref.at[chip, 1 - core], 0, sibling)
    cross.landed(vg_ref.at[chip, 1 - core], 1, sibling)
    for gather in gathers:
        gather.begin_a()
    for gather in gathers:
        gather.spread(0)

    units = Copies(u_send, u_recv)
    pick(give, 1 - core)
    units.start(give, from_core, 0, sibling)

    me_z = lax.axis_index("head")
    piece = near_ref.shape[2]
    moves = Copies(w_send, w_recv)
    for n, ref in enumerate((wk_hbm, wv_hbm)):
        for side, step in enumerate((1, -1)):
            to = turn(me_z, step, NZ)
            start = pl.multiple_of((2 * to + core) * piece, piece)
            moves.start(ref.at[pl.ds(start, piece)], near_ref.at[side, n], 2 * side + n, {"head": to})
    qcols = group_cols(1 - core, GROUP * HD)
    cross.start(q_ref.at[:, qcols], qx_ref, 2, sibling)
    cross.start(do_ref.at[:, qcols], dox_ref, 3, sibling)

    pick(held, core)
    units.landed(from_core, 0, sibling)

    def add_core(j, carry):
        for n in range(2):
            held[n, j // NX, lax.rem(j, NX)] += from_core[n, j // NX, lax.rem(j, NX)]
        return carry

    lax.fori_loop(0, CHIPS, add_core, 0)
    for d in (1, 2, 3):
        far_x, far_y = turn(x, d, NX), turn(y, d, NY)
        units.start(held.at[0, :, far_x], first_in.at[0, d - 1], d, {"ctx": plane.at(d, 0)})
        units.start(held.at[1, far_y], first_in.at[1, d - 1], 3 + d, {"ctx": plane.at(0, d)})

    for gather in gathers:
        gather.got_a(-1)
        gather.got_a(1)
    for gather in gathers:
        gather.spread(1)
        gather.spread(2)
    for gather in gathers:
        gather.got_b(0, -1)
        gather.got_b(0, 1)
    for gather in gathers:
        gather.got_a_far()
        gather.spread(3)

    for d in (1, 2, 3):
        units.landed(first_in.at[0, d - 1], d, {"ctx": plane.at(-d, 0)})
        units.landed(first_in.at[1, d - 1], 3 + d, {"ctx": plane.at(0, -d)})
    for n in range(4):
        mid[0, n] = held[0, n, x] + first_in[0, 0, n] + first_in[0, 1, n] + first_in[0, 2, n]
        mid[1, n] = held[1, y, n] + first_in[1, 0, n] + first_in[1, 1, n] + first_in[1, 2, n]
    for d in (1, 2, 3):
        units.start(mid.at[0, turn(y, d, NY)], last_in.at[0, d - 1], 6 + d, {"ctx": plane.at(0, d)})
        units.start(mid.at[1, turn(x, d, NX)], last_in.at[1, d - 1], 9 + d, {"ctx": plane.at(d, 0)})

    for m in (1, 2, 3):
        for gather in gathers:
            gather.got_b(m, -1)
            gather.got_b(m, 1)

    for d in (1, 2, 3):
        units.landed(last_in.at[0, d - 1], 6 + d, {"ctx": plane.at(0, -d)})
        units.landed(last_in.at[1, d - 1], 9 + d, {"ctx": plane.at(-d, 0)})
    unit_ref[0] = mid[0, y] + last_in[0, 0] + last_in[0, 1] + last_in[0, 2]
    unit_ref[1] = mid[1, x] + last_in[1, 0] + last_in[1, 1] + last_in[1, 2]

    cross.landed(qx_ref, 2, sibling)
    cross.landed(dox_ref, 3, sibling)
    for n in range(2):
        for side, step in enumerate((1, -1)):
            origin = {"head": turn(me_z, -step, NZ)}
            moves.landed(near_ref.at[side, n], 2 * side + n, origin)
    for m in range(4):
        for gather in gathers:
            gather.got_b_far(m)
    for gather in gathers:
        gather.copies.finish()
    cross.finish()
    units.finish()
    moves.finish()


def gather_all(span_slot, pair_list, keys, values, queries, d_out, w_key, w_value):
    vmem = pl.BlockSpec(memory_space=pltpu.VMEM)
    anyspace = pl.BlockSpec(memory_space=pl.ANY)
    blk = jnp.bfloat16
    piece = w_key.shape[0] // NZ // 2
    return pl.pallas_call(
        gather_kernel,
        out_shape=(
            jax.ShapeDtypeStruct((CHIPS, 2, keys.shape[0] + NPAD, HD), blk),
            jax.ShapeDtypeStruct((CHIPS, 2, values.shape[0], HD), blk),
            jax.ShapeDtypeStruct((2, CH, HD), blk),
            jax.ShapeDtypeStruct((2 * CH, GROUP * HD), blk),
            jax.ShapeDtypeStruct((2 * CH, GROUP * HD), blk),
            jax.ShapeDtypeStruct((2, 2, piece) + w_key.shape[1:], blk),
        ),
        in_specs=[pl.BlockSpec(memory_space=pltpu.SMEM)] + [vmem] * 5 + [anyspace] * 2,
        out_specs=(anyspace, anyspace, vmem) + (anyspace,) * 3,
        scratch_shapes=[
            pltpu.VMEM((keys.shape[0] + NPAD, keys.shape[1]), blk),
            pltpu.VMEM((2, NY, NX, CH, HD), blk),
            pltpu.VMEM((2, NY, NX, CH, HD), blk),
            pltpu.VMEM((2, NY, NX, CH, HD), blk),
            pltpu.VMEM((2, 3, 4, CH, HD), blk),
            pltpu.VMEM((2, 4, CH, HD), blk),
            pltpu.VMEM((2, 3, CH, HD), blk),
            pltpu.SemaphoreType.DMA((20,)),
            pltpu.SemaphoreType.DMA((20,)),
            pltpu.SemaphoreType.DMA((20,)),
            pltpu.SemaphoreType.DMA((20,)),
            pltpu.SemaphoreType.DMA((13,)),
            pltpu.SemaphoreType.DMA((13,)),
            pltpu.SemaphoreType.DMA((8,)),
            pltpu.SemaphoreType.DMA((8,)),
            pltpu.SemaphoreType.DMA((4,)),
            pltpu.SemaphoreType.DMA((4,)),
            pltpu.SemaphoreType.DMA((2,)),
        ],
        compiler_params=pltpu.CompilerParams(
            collective_id=0, has_side_effects=True, vmem_limit_bytes=VMEM_MIB * MIB
        ),
        name="gather_kv",
    )(span_slot, pair_list, keys, values, queries, d_out, w_key, w_value)


def dot_nt(a, b):
    return lax.dot_general(a, b, (((1,), (1,)), ((), ())), preferred_element_type=jnp.float32)


def dot_nn(a, b):
    return lax.dot_general(a, b, (((1,), (0,)), ((), ())), preferred_element_type=jnp.float32)


def dot_tn(a, b):
    return lax.dot_general(a, b, (((0,), (0,)), ((), ())), preferred_element_type=jnp.float32)


def attend_kernel(
    span_slot, q_hbm, do_hbm, qx_hbm, dox_hbm, kg_hbm, vg_hbm, unit_ref,
    gq_ref, gqx_ref, hdq_ref, pk_hbm, pv_hbm,
    kg, vg, qs, ds, gq_all, stage, probs, dprob, tops, kept_probs, kept_dprob, kept_tops, stat, acck, accv, dqt, found, flags, slot_label, todo,
    flag_sem, qsems, load_sems, store_sems,
):
    me = lax.axis_index("ctx")
    core = lax.rem(me, 2)
    unit = me // 2
    quarter = NCTX // 4
    pair_copy = pltpu.make_async_copy(
        kg_hbm.at[:, pl.ds(2 * CH, NPAD)], kg.at[:, pl.ds(2 * CH, NPAD)], load_sems.at[4, 0]
    )
    pair_copy.start()
    loads = []
    for n in range(4):
        part = pl.ds(n * quarter, quarter)
        for side, (src, dst) in enumerate(((kg_hbm, kg), (vg_hbm, vg))):
            at = (part, pl.ds(0, 2 * CH))
            loads.append(pltpu.make_async_copy(src.at[at], dst.at[at], load_sems.at[n, side]))
            loads[-1].start()
    stacks = []
    for u in range(4):
        for r in range(GROUP):
            rows = pl.ds((u % 2) * CH, CH)
            own_cols = pl.ds(pl.multiple_of((core * GROUP + r) * HD, HD), HD)
            for n, (own, other, dst) in enumerate(((q_hbm, qx_hbm, qs), (do_hbm, dox_hbm, ds))):
                src = own.at[rows, own_cols] if u < 2 else other.at[rows, pl.ds(r * HD, HD)]
                stacks.append(pltpu.make_async_copy(src, dst.at[u, pl.ds(r * CH, CH)], qsems.at[n, u * GROUP + r]))
    for copy in stacks:
        copy.start()

    def name_slot(c, carry):
        slot_label[span_slot[c]] = c
        return carry

    lax.fori_loop(0, SPANS, name_slot, 0, unroll=8)

    def slot_of(u):
        return 2 * (2 * unit + lax.rem(core + u // 2, 2)) + lax.rem(u, 2)

    pair_copy.wait()
    pair_rows = kg[:, 2 * CH:2 * CH + NPAD, :].reshape(NCTX * NPAD, HD).astype(jnp.float32)
    lanes = lax.broadcasted_iota(jnp.int32, (1, HD), 1).astype(jnp.float32)
    for u in range(4):
        own = slot_label[slot_of(u)].astype(jnp.float32)
        hit = jnp.logical_and(pair_rows[:, 0:1] == own, pair_rows[:, 1:2] == lanes)
        found[u:u + 1, :] = jnp.max(jnp.where(hit, 1.0, 0.0), axis=0, keepdims=True).astype(jnp.int32)
    flag_copy = pltpu.make_async_copy(found, flags, flag_sem.at[0])
    flag_copy.start()

    label = SPANS - 2 + unit // GROUP
    q_unit = unit_ref[0]
    do_unit = unit_ref[1]

    steps = NCTX // WIDE

    def many(ref, t):
        return jnp.concatenate([ref[WIDE * t + u, 0:2 * CH, :] for u in range(WIDE)], axis=0)

    def unit_first(t, carry):
        top, total, mix = carry
        scores = dot_nt(many(kg, t), q_unit) * EXP_SCALE
        mixed = dot_nt(many(vg, t), do_unit)
        diff = lax.broadcasted_iota(jnp.int32, (CH, HD), 0) - lax.broadcasted_iota(jnp.int32, (CH, HD), 1)
        scores = jnp.concatenate([
            jnp.where(diff <= (label - slot_label[2 * WIDE * t + u]) * CH, scores[u * CH:(u + 1) * CH], neg_fill)
            for u in range(2 * WIDE)
        ], axis=0)
        new_top = jnp.maximum(top, jnp.max(scores, axis=0, keepdims=True))
        weights = jnp.exp2(scores - new_top)
        factor = jnp.exp2(top - new_top)
        probs[t] = weights
        dprob[t] = mixed
        tops[t] = new_top
        return (
            new_top,
            total * factor + jnp.sum(weights, axis=0, keepdims=True),
            mix * factor + jnp.sum(weights * mixed, axis=0, keepdims=True),
        )

    zero_row = jnp.zeros((1, HD), jnp.float32)
    state = (jnp.full((1, HD), neg_fill, jnp.float32), zero_row, zero_row)
    for n in range(4):
        for copy in loads[2 * n:2 * n + 2]:
            copy.wait()
        state = lax.fori_loop(n * steps // 4, (n + 1) * steps // 4, unit_first, state)
    top, total, mix = state
    over = 1.0 / total
    delta = mix * over

    def unit_second(t, acc):
        factor = jnp.exp2(tops[t] - top) * over
        weights = probs[t] * factor
        dscore = (weights * (dprob[t] - delta)).astype(jnp.bfloat16)
        value_part = dot_nn(weights.astype(jnp.bfloat16), do_unit)
        key_part = dot_nn(dscore, q_unit)
        for u in range(WIDE):
            accv[WIDE * t + u] = value_part[2 * u * CH:2 * (u + 1) * CH]
            acck[WIDE * t + u] = key_part[2 * u * CH:2 * (u + 1) * CH]
        return acc + dot_tn(many(kg, t), dscore)

    acc = lax.fori_loop(0, steps, unit_second, jnp.zeros((HD, CH), jnp.float32))
    hdq_ref[...] = (acc * SCALE).T.astype(jnp.bfloat16)

    flag_copy.wait()
    for copy in stacks:
        copy.wait()

    def span_work(u, carry):
        own_slot = slot_of(u)
        own_label = slot_label[own_slot]

        @pl.when(own_label < SPANS - 2)
        def _():
            todo[0] = own_slot

            def note(c, n):
                todo[n] = span_slot[c]
                wanted = jnp.logical_and(flags[u, c] > 0, c != own_label)
                return n + wanted.astype(jnp.int32)

            count = lax.fori_loop(0, SPANS, note, jnp.int32(1), unroll=8)
            todo[count] = own_slot

            def rows_at(slot):
                return pl.ds(pl.multiple_of(lax.rem(slot, 2) * CH, CH), CH)

            todo[count + 1] = own_slot

            def some(ref, base, size):
                slots = [todo[base + v] for v in range(size)]
                return jnp.concatenate([ref[slot // 2, rows_at(slot), :] for slot in slots], axis=0)

            def dots(base, size, masked):
                scores = dot_nt(some(kg, base, size), qs[u]) * EXP_SCALE
                if masked:
                    diff = lax.broadcasted_iota(jnp.int32, (CH, QB), 0) - lax.rem(
                        lax.broadcasted_iota(jnp.int32, (CH, QB), 1), CH
                    )
                    limits = [
                        jnp.where(base + v == 0, 0, jnp.where(base + v < count, CH, -CH)) for v in range(size)
                    ]
                    scores = jnp.concatenate([
                        jnp.where(diff <= limits[v], scores[v * CH:(v + 1) * CH], neg_fill) for v in range(size)
                    ], axis=0)
                return scores, dot_nt(some(vg, base, size), ds[u])

            def first(keep, base, size, masked):
                scores, mixed = dots(base, size, masked)
                old_top = stat[0:1, :]
                new_top = jnp.maximum(old_top, jnp.max(scores, axis=0, keepdims=True))
                weights = jnp.exp2(scores - new_top)
                factor = jnp.exp2(old_top - new_top)
                if keep:
                    kept_probs[base // 4, 0:size * CH, :] = weights
                    kept_dprob[base // 4, 0:size * CH, :] = mixed
                    kept_tops[base // 4] = new_top
                stat[0:1, :] = new_top
                stat[1:2, :] = stat[1:2, :] * factor + jnp.sum(weights, axis=0, keepdims=True)
                stat[2:3, :] = stat[2:3, :] * factor + jnp.sum(weights * mixed, axis=0, keepdims=True)

            def second(keep, base, size, masked):
                if keep:
                    weights = kept_probs[base // 4, 0:size * CH, :] * jnp.exp2(kept_tops[base // 4] - stat[3:4, :])
                    mixed = kept_dprob[base // 4, 0:size * CH, :]
                else:
                    scores, mixed = dots(base, size, masked)
                    weights = jnp.exp2(scores - stat[3:4, :])
                dscore = (weights * (mixed - stat[4:5, :])).astype(jnp.bfloat16)
                value_part = dot_nn(weights.astype(jnp.bfloat16), ds[u])
                key_part = dot_nn(dscore, qs[u])
                for v in range(size):
                    slot = todo[base + v]
                    accv[slot // 2, rows_at(slot), :] += value_part[v * CH:(v + 1) * CH]
                    acck[slot // 2, rows_at(slot), :] += key_part[v * CH:(v + 1) * CH]
                dqt[...] += dot_tn(some(kg, base, size), dscore)

            fours = (count + 1) // 4
            fits = (count + 3) // 4 <= KEPT

            def sweep(work, keep):
                def step(t, c):
                    masked = jnp.logical_or(t == 0, 4 * t + 4 > count)

                    @pl.when(masked)
                    def _():
                        work(keep, 4 * t, 4, True)

                    @pl.when(jnp.logical_not(masked))
                    def _():
                        work(keep, 4 * t, 4, False)

                    return c

                def plain(t, c):
                    work(keep, 4 * t, 4, False)
                    return c

                lax.fori_loop(0, fours, plain if keep and work is second else step, 0)

                @pl.when(4 * fours < count)
                def _():
                    work(keep, 4 * fours, 2, True)

            stat[0:1, :] = jnp.full((1, QB), neg_fill, jnp.float32)
            stat[1:3, :] = jnp.zeros((2, QB), jnp.float32)
            dqt[...] = jnp.zeros_like(dqt)

            def both_sweeps(keep):
                sweep(first, keep)
                total_row = stat[1:2, :]
                stat[3:4, :] = stat[0:1, :] + jnp.log2(total_row)
                stat[4:5, :] = stat[2:3, :] / total_row
                sweep(second, keep)

            @pl.when(fits)
            def _():
                both_sweeps(True)

            @pl.when(jnp.logical_not(fits))
            def _():
                both_sweeps(False)

            for r in range(GROUP):
                gq_all[pl.ds(pl.multiple_of(u * CH, CH), CH), r * HD:(r + 1) * HD] = (
                    (dqt[:, r * CH:(r + 1) * CH] * SCALE).T.astype(jnp.bfloat16)
                )

        return carry

    lax.fori_loop(0, 4, span_work, 0)

    stores = [
        pltpu.make_async_copy(gq_all.at[pl.ds(0, 2 * CH)], gq_ref, store_sems.at[4, 0]),
        pltpu.make_async_copy(gq_all.at[pl.ds(2 * CH, 2 * CH)], gqx_ref, store_sems.at[4, 1]),
    ]
    for copy in stores:
        copy.start()
    for n in range(4):
        part = pl.ds(n * quarter, quarter)

        def narrow(t, carry):
            for side, ref in enumerate((acck, accv)):
                rows = ref[t].astype(jnp.bfloat16).reshape(NZ, PARTS, 2 * CH // NZ // PARTS, HD)
                for m in range(PARTS):
                    stage[side, m, t] = rows[:, m]
            return carry

        lax.fori_loop(n * quarter, (n + 1) * quarter, narrow, 0)
        for side, dst in enumerate((pk_hbm, pv_hbm)):
            stores.append(
                pltpu.make_async_copy(stage.at[side, :, part], dst.at[:, part], store_sems.at[n, side])
            )
            stores[-1].start()
    for copy in stores:
        copy.wait()


def attend(span_slot, queries, d_out, qx, dox, kg, vg, unit):
    vmem = pl.BlockSpec(memory_space=pltpu.VMEM)
    smem = pl.BlockSpec(memory_space=pltpu.SMEM)
    anyspace = pl.BlockSpec(memory_space=pl.ANY)
    blk = jnp.bfloat16
    return pl.pallas_call(
        attend_kernel,
        out_shape=(
            jax.ShapeDtypeStruct((2 * CH, GROUP * HD), blk),
            jax.ShapeDtypeStruct((2 * CH, GROUP * HD), blk),
            jax.ShapeDtypeStruct((CH, HD), blk),
            jax.ShapeDtypeStruct((PARTS, NCTX, NZ, 2 * CH // NZ // PARTS, HD), blk),
            jax.ShapeDtypeStruct((PARTS, NCTX, NZ, 2 * CH // NZ // PARTS, HD), blk),
        ),
        in_specs=[smem] + [anyspace] * 6 + [vmem],
        out_specs=(anyspace, anyspace, vmem, anyspace, anyspace),
        scratch_shapes=[
            pltpu.VMEM(kg.shape, blk),
            pltpu.VMEM(vg.shape, blk),
            pltpu.VMEM((4, GROUP * CH, HD), blk),
            pltpu.VMEM((4, GROUP * CH, HD), blk),
            pltpu.VMEM((4 * CH, GROUP * HD), blk),
            pltpu.VMEM((2, PARTS, NCTX, NZ, 2 * CH // NZ // PARTS, HD), blk),
            pltpu.VMEM((NCTX // WIDE, 2 * WIDE * CH, HD), jnp.float32),
            pltpu.VMEM((NCTX // WIDE, 2 * WIDE * CH, HD), jnp.float32),
            pltpu.VMEM((NCTX // WIDE, 1, HD), jnp.float32),
            pltpu.VMEM((KEPT, 4 * CH, QB), jnp.float32),
            pltpu.VMEM((KEPT, 4 * CH, QB), jnp.float32),
            pltpu.VMEM((KEPT, 1, QB), jnp.float32),
            pltpu.VMEM((8, QB), jnp.float32),
            pltpu.VMEM((NCTX, 2 * CH, HD), jnp.float32),
            pltpu.VMEM((NCTX, 2 * CH, HD), jnp.float32),
            pltpu.VMEM((HD, QB), jnp.float32),
            pltpu.VMEM((8, HD), jnp.int32),
            pltpu.SMEM((8, HD), jnp.int32),
            pltpu.SMEM((SPANS,), jnp.int32),
            pltpu.SMEM((SPANS + 8,), jnp.int32),
            pltpu.SemaphoreType.DMA((1,)),
            pltpu.SemaphoreType.DMA((2, 32)),
            pltpu.SemaphoreType.DMA((5, 2)),
            pltpu.SemaphoreType.DMA((5, 2)),
        ],
        compiler_params=pltpu.CompilerParams(vmem_limit_bytes=VMEM_MIB * MIB),
        cost_estimate=pl.CostEstimate(flops=8 * 10**9, bytes_accessed=32 * 10**6, transcendentals=4 * 10**6),
        name="attend",
    )(span_slot, queries, d_out, qx, dox, kg, vg, unit)


def plus(a, b):
    return (a.astype(jnp.float32) + b.astype(jnp.float32)).astype(jnp.bfloat16)


class Scatter:
    def __init__(self, first, parts, own, near, full, near_b, full_b, send, recv, own_sem):
        self.plane = Plane(first)
        self.parts, self.own, self.own_sem = parts, own, own_sem
        self.near, self.full, self.near_b, self.full_b = near, full, near_b, full_b
        self.copies = Copies(send, recv)

    def dev(self, da, db):
        return {"ctx": self.plane.at(da, db)}

    def load(self, q, e):
        return pltpu.make_async_copy(self.parts.at[self.plane.chip(e, q)], self.own.at[q, e], self.own_sem.at[4 * q + e])

    def far(self, q):
        block = self.parts.at[self.plane.chip(2, q)]
        self.copies.start(block.at[0], self.near.at[q, 0], 4 * q, self.dev(1, 0))
        self.copies.start(block.at[1], self.near.at[q, 1], 4 * q + 1, self.dev(-1, 0))

    def next(self, q):
        for side, step in enumerate((1, -1)):
            e = step % 4
            self.load(q, e).wait()
            self.copies.landed(self.near.at[q, side], 4 * q + side, self.dev(-step, 0))
            self.own[q, e, side] = plus(self.own[q, e, side], self.near[q, side])
            self.copies.start(self.own.at[q, e], self.full.at[q, side], 4 * q + 2 + side, self.dev(step, 0))

    def last(self, q):
        self.load(q, 0).wait()
        self.copies.landed(self.full.at[q, 0], 4 * q + 2, self.dev(-1, 0))
        self.copies.landed(self.full.at[q, 1], 4 * q + 3, self.dev(1, 0))
        return (
            self.own[q, 0].astype(jnp.float32)
            + self.full[q, 0].astype(jnp.float32)
            + self.full[q, 1].astype(jnp.float32)
        )

    def last_far(self):
        self.own[2, 0] = self.last(2).astype(jnp.bfloat16)
        for side, step in enumerate((1, -1)):
            self.copies.start(self.own.at[2, 0, side], self.near_b.at[side], 16 + side, self.dev(0, step))

    def last_near(self, side):
        step = (1, -1)[side]
        q = step % 4
        total = self.last(q)
        self.copies.landed(self.near_b.at[side], 16 + side, self.dev(0, -step))
        self.own[q, 0, 1 - side] = total[1 - side].astype(jnp.bfloat16)
        self.own[q, 0, side] = (total[side] + self.near_b[side].astype(jnp.float32)).astype(jnp.bfloat16)
        self.copies.start(self.own.at[q, 0], self.full_b.at[side], 18 + side, self.dev(0, step))

    def finish(self):
        total = self.last(0)
        self.copies.landed(self.full_b.at[0], 18, self.dev(0, -1))
        self.copies.landed(self.full_b.at[1], 19, self.dev(0, 1))
        return total + self.full_b[0].astype(jnp.float32) + self.full_b[1].astype(jnp.float32)


def reduce_project_kernel(
    pk_ref, pv_ref, near_ref, gqx_ref, hdq_ref, wk_hbm, wv_hbm,
    gk_ref, gv_ref, gqo_ref, gx_ref, hg_ref,
    k_own, k_near, k_full, k_near_b, k_full_b,
    v_own, v_near, v_full, v_near_b, v_full_b,
    sums, swap, swap_in, grads, weights, total, half,
    k_send, k_recv, v_send, v_recv, w_send, w_recv, c_send, c_recv, g_send, g_recv, o_send, o_recv, h_send, h_recv,
    own_sems, w_sem, hg_sem, o_sem,
):
    barrier_with(ctx_targets() + head_targets((1, 2, 3)))
    me_z = lax.axis_index("head")
    y, x, core = ctx_coords()
    plane = Plane("x")
    sibling = {"ctx": plane.at(0, 0, True)}
    ways = [
        [
            Scatter("y", pk_ref.at[m], *(ref.at[m] for ref in (
                k_own, k_near, k_full, k_near_b, k_full_b, k_send, k_recv)), own_sems.at[m, 0]),
            Scatter("x", pv_ref.at[m], *(ref.at[m] for ref in (
                v_own, v_near, v_full, v_near_b, v_full_b, v_send, v_recv)), own_sems.at[m, 1]),
        ]
        for m in range(PARTS)
    ]
    order = (2, 1, 3, 0)

    def far(m):
        for q in order:
            for way in ways[m]:
                way.far(q)
        for e in (1, 3, 0):
            for q in order:
                for way in ways[m]:
                    way.load(q, e).start()

    def next_hop(m):
        for q in order:
            for way in ways[m]:
                way.next(q)

    def last_hop(m):
        for way in ways[m]:
            way.last_far()
        for side in range(2):
            for way in ways[m]:
                way.last_near(side)

    far(0)

    width = weights.shape[2]
    piece = width // 2
    moves = Copies(w_send, w_recv)
    two = turn(me_z, 2, NZ)
    start = pl.multiple_of((2 * two + core) * piece, piece)
    for n, ref in enumerate((wk_hbm, wv_hbm)):
        moves.start(
            ref.at[pl.ds(start, piece)], weights.at[2, n, pl.ds(pl.multiple_of(core * piece, piece), piece)], n,
            {"head": two},
        )
    mine_rows = pl.ds(pl.multiple_of(core * piece, piece), piece)
    other_rows = pl.ds(pl.multiple_of((1 - core) * piece, piece), piece)
    cross = Copies(c_send, c_recv)
    for side, d in enumerate((1, 3)):
        cross.start(near_ref.at[side], weights.at[d, :, mine_rows], side, sibling)
    cross.start(gqx_ref, gqo_ref, 2, sibling)
    wrows = pl.ds(pl.multiple_of(me_z * width, width), width)
    fetches = [
        pltpu.make_async_copy(wk_hbm.at[wrows], weights.at[0, 0], w_sem.at[0]),
        pltpu.make_async_copy(wv_hbm.at[wrows], weights.at[0, 1], w_sem.at[1]),
        pltpu.make_async_copy(near_ref.at[0], weights.at[1, :, mine_rows], w_sem.at[2]),
        pltpu.make_async_copy(near_ref.at[1], weights.at[3, :, mine_rows], w_sem.at[3]),
    ]
    for copy in fetches:
        copy.start()
    hg_copy = pltpu.make_async_copy(hdq_ref, hg_ref.at[y, x, core], hg_sem.at[0])
    hg_copy.start()

    rows_of_part = 2 * CH // NZ // PARTS
    sends = Copies(g_send, g_recv)
    outs = Copies(o_send, o_recv)
    own_outs = []

    def collect(m):
        for n, (way, factor) in enumerate(zip(ways[m], (SCALE, 1.0))):
            sums[...] = (way.finish() * factor).reshape(sums.shape)
            swap[m, n] = sums[1 - core].astype(jnp.bfloat16)
            cross.start(swap.at[m, n], swap_in.at[m, n], 4 + 2 * m + n, sibling)
            grads[m, 0, n, :, pl.ds(pl.multiple_of(core * HD, HD), HD)] = sums[core].astype(jnp.bfloat16)

    def share(m):
        for n, out in enumerate((gk_ref, gv_ref)):
            cross.landed(swap_in.at[m, n], 4 + 2 * m + n, sibling)
            grads[m, 0, n, :, pl.ds(pl.multiple_of((1 - core) * HD, HD), HD)] = swap_in[m, n]
        for d in (1, 3, 2):
            sends.start(grads.at[m, 0], grads.at[m, d], 3 * m + d - 1, {"head": turn(me_z, d, NZ)})
        for n, out in enumerate((gk_ref, gv_ref)):
            for h in range(NZ):
                at = (h * PARTS + m) * rows_of_part
                out[at:at + rows_of_part, :] = grads[m, 0, n, h * rows_of_part:(h + 1) * rows_of_part, :]

    step = 512

    def partial(m, d, cols):
        return dot_nt(grads[m, d, 0], weights[d, 0, cols, :]) + dot_nt(grads[m, d, 1], weights[d, 1, cols, :])

    def columns(n):
        return pl.ds(pl.multiple_of(n * step, step), step)

    def multiply(m, d):
        if d != 0:
            sends.landed(grads.at[m, d], 3 * m + d - 1, {"head": turn(me_z, -d, NZ)})

        def part(n, carry):
            if d == 0:
                total[m, :, columns(n)] = partial(m, d, columns(n))
            else:
                total[m, :, columns(n)] += partial(m, d, columns(n))
            return carry

        lax.fori_loop(0, width // step, part, 0)

    def deliver(m):
        sends.landed(grads.at[m, 2], 3 * m + 1, {"head": turn(me_z, -2, NZ)})
        rows_out = pl.ds(m * rows_of_part, rows_of_part)
        for n in range(width // step):
            cols = pl.ds(n * step, step)
            half[m, :, n * step:(n + 1) * step] = (
                total[m, :, n * step:(n + 1) * step] + partial(m, 2, cols)
            ).astype(jnp.bfloat16)
            out_cols = pl.ds(pl.multiple_of(me_z * width + n * step, step), step)

            def block(to):
                return half.at[m, pl.ds(pl.multiple_of(to * rows_of_part, rows_of_part), rows_of_part), cols]

            for d in (1, 3, 2):
                to = turn(me_z, d, NZ)
                outs.start(block(to), gx_ref.at[rows_out, out_cols], (m * 3 + d - 1) * 4 + n, {"head": to})
            own_outs.append(pltpu.make_async_copy(block(me_z), gx_ref.at[rows_out, out_cols], o_sem.at[m * 4 + n]))
            own_outs[-1].start()

    next_hop(0)
    far(1)
    last_hop(0)
    next_hop(1)
    collect(0)
    last_hop(1)
    share(0)

    for side, d in enumerate((1, 3)):
        cross.landed(weights.at[d, :, other_rows], side, sibling)
    for copy in fetches:
        copy.wait()
    multiply(0, 0)
    collect(1)
    share(1)

    units = Copies(h_send, h_recv)
    rows = [pl.ds(0, CH // 2), pl.ds(CH // 2, CH // 2)]
    hg_copy.wait()
    for d in (1, 2, 3):
        for n, (da, db) in enumerate(((d, 0), (0, d))):
            block = hg_ref.at[y, x, core, rows[n]]
            units.start(block, block, 2 * d - 2 + n, {"ctx": plane.at(da, db)})

    multiply(0, 1)
    multiply(0, 3)
    for n in range(2):
        moves.landed(weights.at[2, n, mine_rows], n, {"head": two})
    cross.start(weights.at[2, :, mine_rows], weights.at[2, :, mine_rows], 3, sibling)
    multiply(1, 0)
    cross.landed(weights.at[2, :, other_rows], 3, sibling)
    deliver(0)

    for d in (1, 2, 3):
        for n, (da, db) in enumerate(((-d, 0), (0, -d))):
            at = hg_ref.at[turn(y, db, NY), turn(x, da, NX), core, rows[n]]
            units.landed(at, 2 * d - 2 + n, {"ctx": plane.at(da, db)})
    for d in (1, 2, 3):
        block = hg_ref.at[y, :, core, rows[0]]
        units.start(block, block, 4 + 2 * d, {"ctx": plane.at(0, d)})
        block = hg_ref.at[:, x, core, rows[1]]
        units.start(block, block, 5 + 2 * d, {"ctx": plane.at(d, 0)})

    multiply(1, 1)
    multiply(1, 3)
    deliver(1)

    for d in (1, 2, 3):
        units.landed(hg_ref.at[turn(y, -d, NY), :, core, rows[0]], 4 + 2 * d, {"ctx": plane.at(0, -d)})
        units.landed(hg_ref.at[:, turn(x, -d, NX), core, rows[1]], 5 + 2 * d, {"ctx": plane.at(-d, 0)})
    units.start(hg_ref.at[:, :, core], hg_ref.at[:, :, core], 12, sibling)
    units.landed(hg_ref.at[:, :, 1 - core], 12, sibling)
    cross.landed(gqo_ref, 2, sibling)

    for m in range(PARTS):
        rows_out = pl.ds(m * rows_of_part, rows_of_part)
        for n in range(width // step):
            for d in (1, 3, 2):
                origin = turn(me_z, -d, NZ)
                out_cols = pl.ds(pl.multiple_of(origin * width + n * step, step), step)
                outs.landed(gx_ref.at[rows_out, out_cols], (m * 3 + d - 1) * 4 + n, {"head": origin})
    for m in range(PARTS):
        for way in ways[m]:
            way.copies.finish()
    for copies in (moves, cross, sends, outs, units):
        copies.finish()
    for copy in own_outs:
        copy.wait()


def reduce_project(pk, pv, near, gqx, hdq, w_key, w_value):
    vmem = pl.BlockSpec(memory_space=pltpu.VMEM)
    anyspace = pl.BlockSpec(memory_space=pl.ANY)
    blk = jnp.bfloat16
    depth = w_key.shape[0]
    width = depth // NZ
    rows = 2 * CH // PARTS
    block = (2, NZ, rows // NZ, HD)
    one = [
        pltpu.VMEM((PARTS, 4, 4) + block, blk),
        pltpu.VMEM((PARTS, 4) + block, blk),
        pltpu.VMEM((PARTS, 4, 2) + block, blk),
        pltpu.VMEM((PARTS,) + block, blk),
        pltpu.VMEM((PARTS, 2) + block, blk),
    ]

    def pair(*shape):
        return [pltpu.SemaphoreType.DMA(shape)] * 2

    return pl.pallas_call(
        reduce_project_kernel,
        out_shape=(
            jax.ShapeDtypeStruct((2 * CH, 2 * HD), blk),
            jax.ShapeDtypeStruct((2 * CH, 2 * HD), blk),
            jax.ShapeDtypeStruct(gqx.shape, blk),
            jax.ShapeDtypeStruct((2 * CH // NZ, depth), blk),
            jax.ShapeDtypeStruct((NY, NX, 2, CH, HD), blk),
        ),
        in_specs=[anyspace] * 4 + [vmem] + [anyspace] * 2,
        out_specs=(vmem, vmem, anyspace, vmem, vmem),
        scratch_shapes=one + one
        + [
            pltpu.VMEM((2, rows, HD), jnp.float32),
            pltpu.VMEM((PARTS, 2, rows, HD), blk),
            pltpu.VMEM((PARTS, 2, rows, HD), blk),
            pltpu.VMEM((PARTS, NZ, 2, rows, 2 * HD), blk),
            pltpu.VMEM((NZ, 2, width, 2 * HD), blk),
            pltpu.VMEM((PARTS, rows, width), jnp.float32),
            pltpu.VMEM((PARTS, rows, width), blk),
        ]
        + pair(PARTS, 20) + pair(PARTS, 20) + pair(2) + pair(8) + pair(6) + pair(24) + pair(13)
        + [
            pltpu.SemaphoreType.DMA((PARTS, 2, 16)),
            pltpu.SemaphoreType.DMA((4,)),
            pltpu.SemaphoreType.DMA((1,)),
            pltpu.SemaphoreType.DMA((8,)),
        ],
        compiler_params=pltpu.CompilerParams(
            collective_id=1, has_side_effects=True, vmem_limit_bytes=VMEM_MIB * MIB
        ),
        name="reduce_project",
    )(pk, pv, near, gqx, hdq, w_key, w_value)


def finish_kernel(span_slot, gq_hbm, gqo_hbm, hg_hbm, gk_hbm, gv_hbm, gx_hbm, oq, ok, ov, ox, vq, vk, vv, vx, sems, head_sems):
    me = lax.axis_index("ctx")
    core = lax.rem(me, 2)
    ways = ((gx_hbm, vx, ox), (gk_hbm, vk, ok), (gv_hbm, vv, ov))
    loads = [pltpu.make_async_copy(src, mid, sems.at[n]) for n, (src, mid, _) in enumerate(ways)]
    for copy in loads:
        copy.start()
    def span_copies(i):
        rows = pl.ds(i * CH, CH)
        pair = []
        for n, (src, which) in enumerate(((gq_hbm, core), (gqo_hbm, 1 - core))):
            cols = pl.ds(pl.multiple_of(which * GROUP * HD, GROUP * HD), GROUP * HD)
            pair.append(pltpu.make_async_copy(src.at[rows], vq.at[rows, cols], head_sems.at[i, n]))
        heads = []
        for s in range(2):
            heads.append([])
            for h in range(2 * GROUP):
                chip = s * GROUP + h % GROUP
                heads[s].append(pltpu.make_async_copy(
                    hg_hbm.at[chip // NX, chip % NX, h // GROUP], vq.at[rows, pl.ds(h * HD, HD)], head_sems.at[i, h]
                ))
        dense = [span_slot[SPANS - 2 + s] == 2 * me + i for s in range(2)]
        light = jnp.logical_not(jnp.logical_or(dense[0], dense[1]))
        return [(light, pair), (dense[0], heads[0]), (dense[1], heads[1])]

    choices = span_copies(0) + span_copies(1)
    for chosen, group in choices:
        @pl.when(chosen)
        def _():
            for copy in group:
                copy.start()

    for chosen, group in choices:
        @pl.when(chosen)
        def _():
            for copy in group:
                copy.wait()

    stores = [pltpu.make_async_copy(vq, oq, sems.at[3])]
    stores[0].start()
    for n, (_, mid, dst) in enumerate(ways):
        loads[n].wait()
        stores.append(pltpu.make_async_copy(mid, dst, sems.at[n]))
        stores[-1].start()
    for copy in stores:
        copy.wait()


def finish(span_slot, gq, gqo, units, grad_k, grad_v, grad_x):
    anyspace = pl.BlockSpec(memory_space=pl.ANY)
    return pl.pallas_call(
        finish_kernel,
        out_shape=(
            jax.ShapeDtypeStruct((2 * CH, 2 * GROUP * HD), gq.dtype),
            jax.ShapeDtypeStruct(grad_k.shape, grad_k.dtype),
            jax.ShapeDtypeStruct(grad_v.shape, grad_v.dtype),
            jax.ShapeDtypeStruct(grad_x.shape, grad_x.dtype),
        ),
        in_specs=[pl.BlockSpec(memory_space=pltpu.SMEM)] + [anyspace] * 6,
        out_specs=(anyspace,) * 4,
        scratch_shapes=[
            pltpu.VMEM((2 * CH, 2 * GROUP * HD), gq.dtype),
            pltpu.VMEM(grad_k.shape, grad_k.dtype),
            pltpu.VMEM(grad_v.shape, grad_v.dtype),
            pltpu.VMEM(grad_x.shape, grad_x.dtype),
            pltpu.SemaphoreType.DMA((4,)),
            pltpu.SemaphoreType.DMA((2, 2 * GROUP)),
        ],
        compiler_params=pltpu.CompilerParams(vmem_limit_bytes=VMEM_MIB * MIB),
        name="finish",
    )(span_slot, gq, gqo, units, grad_k, grad_v, grad_x)


def per_device(queries, keys, values, d_out, w_key, w_value, pair_list, span_slot):
    kg, vg, unit, qx, dox, near = gather_all(span_slot, pair_list, keys, values, queries, d_out, w_key, w_value)
    kg = kg.reshape((NCTX,) + kg.shape[2:])
    vg = vg.reshape((NCTX,) + vg.shape[2:])
    gq, gqx, hdq, pk, pv = attend(span_slot, queries, d_out, qx, dox, kg, vg, unit)
    pk = pk.reshape((PARTS, CHIPS, 2) + pk.shape[2:])
    pv = pv.reshape((PARTS, CHIPS, 2) + pv.shape[2:])
    grad_k, grad_v, gqo, grad_x, units = reduce_project(pk, pv, near, gqx, hdq, w_key, w_value)
    return finish(span_slot, gq, gqo, units, grad_k, grad_v, grad_x)


def solution(mesh):
    return jax.shard_map(
        per_device,
        mesh=mesh,
        in_specs=(
            P("ctx", "head"),
            P("ctx", "head"),
            P("ctx", "head"),
            P("ctx", "head"),
            P(None, "head"),
            P(None, "head"),
            P("ctx", None),
            P(),
        ),
        out_specs=(P("ctx", "head"), P("ctx", "head"), P("ctx", "head"), P(("ctx", "head"), None)),
        check_vma=False,
    )
```
